32 devices in a mesh: sec: 4 (over z), band: 4 (over y, x), ch: 2 (over core).
Axes of the slice: x: 2, y: 2, z: 4, core: 2. Of those that a mesh axis runs over, the one named last changes fastest.
Arguments:
- air_field_lattice: bfloat16 [64, 1024, 768], P(('sec', 'band', 'ch')), may hold values from -6 to 6
- associated_polynomial_matrix: bfloat16 [512, 64, 64], P(('sec', 'band', 'ch')), may hold values from -0.75 to 0.75
- harmonic_damping_factor: float32 [64, 768], replicated, may hold values from 0.5 to 2
- boundary_exchange_projector: bfloat16 [768, 8], replicated, may hold values from -0.21875 to 0.21875
- warmth_response_factor: float32 [768], replicated, may hold values from -4 to 4
- water_patch_fields: bfloat16 [192, 128, 4, 258], P(('sec', 'band', 'ch')), may hold values from -6 to 6
- kernel_coefficients: bfloat16 [3, 3, 128, 128], replicated, may hold values from -0.1875 to 0.1875
- local_exchange_matrix: bfloat16 [8, 128], replicated, may hold values from -2 to 2
- patch_average_matrix: float32 [8, 128], replicated, may hold values from -15 to 15
- water_kernel_offset: float32 [128], replicated, may hold values from -3 to 3
- water_readout_matrix: bfloat16 [128, 128], replicated, may hold values from -0.5 to 0.5
- patch_holder_index: int32 [32, 4], replicated, may hold values from 0 to 3, as said below
- water_point_indicator: int32 [192, 2, 256], P(('sec', 'band', 'ch')), may hold values from 0 to 1, as said below
- water_point_totals: int32 [192], P(('sec', 'band', 'ch')), may hold values from 0 to 512, as said below
Outputs:
- advanced_air_field: bfloat16 [64, 1024, 768], P(('sec', 'band', 'ch'))
- ocean_next: bfloat16 [192, 128, 2, 256], P(('sec', 'band', 'ch'))
The draws below stay inside these ranges and needn't reach their ends.
Inputs may be any that keep to these rules, and one draw needn't show every extreme that they name: `patch_holder_index`: within each group of equal s and c, every band index owns either 6 or 2 of the group's tiles, half of them each way, so no device owns more than 6. `water_point_indicator`: empty slots are all zeros. `water_point_totals`: the number of ones of the slot in water_point_indicator.
All inputs are finite; a program needn't handle non-finite values.
Results may differ from the reference program's by a relative error of at most 0.0058.
Values may be sent and summed in bfloat16 or wider, within the bound.
No kernel may reach another device: no remote copies, remote signals or barrier semaphores. Data moves between devices by JAX's collectives and lax.ppermute only.
A program may use at most 128 MiB of HBM per device.

```python
import math
import jax
import jax.numpy as jnp
from jax import lax

LATD = 2
MERIDIANS = 1024
AIR_FEATURES = 768
K = 512
NF = 8
OCH = 128
TPR = 4
TSLOT = 6
TW = 256
PARALLELS = 64
OSLOTS = 192
N_SEC = 4
N_BAND = 4
N_CH = 2
DEVICES = 32


def owner_layout(key):
    group_total = N_SEC * N_CH
    group_keys = jax.random.split(jax.random.fold_in(key, 11), group_total)

    def one_group(group_key):
        first_key, second_key = jax.random.split(group_key)
        heavy = jax.random.permutation(first_key, N_BAND) < N_BAND // 2
        counts = jnp.where(heavy, TPR + TPR // 2, TPR - TPR // 2).astype(jnp.int32)
        bounds = jnp.cumsum(counts)
        tile_index = jnp.arange(N_BAND * TPR, dtype=jnp.int32)
        sequence = jnp.sum((bounds[None, :] <= tile_index[:, None]).astype(jnp.int32), axis=1)
        shuffle = jax.random.permutation(second_key, N_BAND * TPR)
        return (sequence[shuffle].astype(jnp.int32), counts)
    owners, counts = jax.vmap(one_group)(group_keys)
    owners = owners.reshape(N_SEC, N_CH, N_BAND, TPR).transpose(0, 2, 1, 3).reshape(N_SEC * N_BAND * N_CH, TPR)
    counts = counts.reshape(N_SEC, N_CH, N_BAND).transpose(0, 2, 1).reshape(-1)
    return (owners, counts)


def wet_layout(key):
    owners, counts = owner_layout(key)
    mask_key = jax.random.fold_in(key, 23)
    kind_key, level_key, cell_key = jax.random.split(mask_key, 3)
    slot_total = N_SEC * N_BAND * N_CH * TSLOT
    live = (jnp.arange(TSLOT, dtype=jnp.int32)[None, :] < counts[:, None]).reshape(-1)
    kind = jax.random.randint(kind_key, (slot_total,), 0, 8)
    level = jax.random.randint(level_key, (slot_total,), 300, 1001)
    level = jnp.where(kind == 0, 0, jnp.where(kind == 1, 1000, level))
    cell_draw = jax.random.randint(cell_key, (slot_total, LATD, TW), 0, 1000)
    wet = ((cell_draw < level[:, None, None]) & live[:, None, None]).astype(jnp.int32)
    return (wet, jnp.sum(wet, axis=(1, 2)).astype(jnp.int32))


def draw_patch_holder_index(key, part):
    return owner_layout(key)[0]


def draw_water_point_indicator(key, part):
    return wet_layout(key)[0]


def draw_water_point_totals(key, part):
    return wet_layout(key)[1]


def block_levels(rng, extent, shards, smallest, top_value):
    gain, own = 1.0, jax.random.fold_in(rng, 6)
    for axis_at, blocks in shards:
        heights = jnp.exp(jax.random.uniform(jax.random.fold_in(own, axis_at), (blocks,), jnp.float32, smallest / len(shards), top_value / len(shards)))
        gain = gain * jnp.repeat(heights, extent[axis_at] // blocks).reshape([-1 if axis == axis_at else 1 for axis in range(len(extent))])
    return gain


def scatter_about(key, dims, spread, reach, cuts=(), kind=jnp.bfloat16):
    result = jax.random.normal(key, dims, jnp.float32) * spread
    if len(cuts) > 0:
        result = block_levels(key, dims, cuts, -0.22, 0.18) * result
    return jnp.clip(result, min=-reach, max=reach).astype(kind)


def setup_inputs(seed: int = 0) -> dict:
    splits = jax.random.split(jax.random.key(seed), 15)
    air_field_lattice = scatter_about(splits[0], (PARALLELS, MERIDIANS, AIR_FEATURES), 1.0, 6.0, ((0, 32),))
    associated_polynomial_matrix = scatter_about(splits[1], (K, PARALLELS, PARALLELS), PARALLELS ** -0.5, 0.75, ((0, 32),))
    harmonic_damping_factor = jnp.clip(jnp.exp(jax.random.uniform(splits[2], (PARALLELS, AIR_FEATURES), jnp.float32, math.log(0.5), math.log(2.0))), 0.5, 2.0)
    boundary_exchange_projector = scatter_about(splits[3], (AIR_FEATURES, NF), AIR_FEATURES ** -0.5, 0.21875)
    warmth_response_factor = scatter_about(splits[4], (AIR_FEATURES,), 1.0, 4.0, (), jnp.float32)
    water_patch_fields = scatter_about(splits[5], (OSLOTS, OCH, LATD + 2, TW + 2), 1.0, 6.0, ((0, 32),))
    kernel_coefficients = scatter_about(splits[6], (3, 3, OCH, OCH), (9 * OCH) ** -0.5, 0.1875)
    local_exchange_matrix = scatter_about(splits[7], (NF, OCH), NF ** -0.5, 2.0)
    patch_average_matrix = scatter_about(splits[8], (NF, OCH), 3.0, 15.0, (), jnp.float32)
    water_kernel_offset = scatter_about(splits[9], (OCH,), 0.5, 3.0, (), jnp.float32)
    water_readout_matrix = scatter_about(splits[10], (OCH, OCH), OCH ** -0.5, 0.5)
    patch_holder_index = draw_patch_holder_index(jax.random.fold_in(splits[14], 71), 0)
    water_point_indicator = draw_water_point_indicator(jax.random.fold_in(splits[14], 71), 0)
    water_point_totals = draw_water_point_totals(jax.random.fold_in(splits[14], 71), 0)
    return {"air_field_lattice": air_field_lattice, "associated_polynomial_matrix": associated_polynomial_matrix, "harmonic_damping_factor": harmonic_damping_factor, "boundary_exchange_projector": boundary_exchange_projector, "warmth_response_factor": warmth_response_factor, "water_patch_fields": water_patch_fields, "kernel_coefficients": kernel_coefficients, "local_exchange_matrix": local_exchange_matrix, "patch_average_matrix": patch_average_matrix, "water_kernel_offset": water_kernel_offset, "water_readout_matrix": water_readout_matrix, "patch_holder_index": patch_holder_index, "water_point_indicator": water_point_indicator, "water_point_totals": water_point_totals}


def dft_tables(meridian_number, column_order):
    cell_index = jnp.arange(meridian_number, dtype=jnp.int32)[:, None]
    wavenumber = (column_order // 2)[None, :]
    component = (column_order % 2)[None, :]
    phase_angle = ((cell_index * wavenumber) % meridian_number).astype(jnp.float32) * (2.0 * math.pi / meridian_number)
    basis_table = jnp.where(component == 0, jnp.cos(phase_angle), -jnp.sin(phase_angle))
    forward = basis_table.astype(jnp.bfloat16)
    inverse = (basis_table.T * (2.0 / meridian_number)).astype(jnp.bfloat16)
    return forward, inverse


def ocean_update(state, tile_flux, mask_tile, count_tile, kernel_coefficients, local_exchange_matrix, patch_average_matrix, water_kernel_offset, water_readout_matrix):
    mask_f = mask_tile.astype(jnp.float32)
    masked = tile_flux.astype(jnp.float32) * mask_f[:, None]
    fmean = jnp.sum(masked, axis=(2, 3)) / jnp.maximum(count_tile.astype(jnp.float32), 1.0)[:, None]
    state_f = state.astype(jnp.float32)
    total = jnp.einsum('fo,sfrw->sorw', local_exchange_matrix.astype(jnp.float32), masked)
    for shift_row in range(3):
        for shift_col in range(3):
            window = state_f[:, :, shift_row:shift_row + LATD, shift_col:shift_col + TW]
            total = total + jnp.einsum('io,sirw->sorw', kernel_coefficients[shift_row, shift_col].astype(jnp.float32), window)
    mean_term = jnp.sum(fmean[:, :, None] * patch_average_matrix[None], axis=1)
    total = total + mean_term[:, :, None, None] + water_kernel_offset[None, :, None, None]
    hidden = jax.nn.gelu(total, approximate=True).astype(jnp.bfloat16)
    update = jnp.einsum('io,sirw->sorw', water_readout_matrix.astype(jnp.float32), hidden.astype(jnp.float32))
    fresh = (state_f[:, :, 1:1 + LATD, 1:1 + TW] + update) * mask_f[:, None]
    return fresh.astype(jnp.bfloat16)


def reference(air_field_lattice, associated_polynomial_matrix, harmonic_damping_factor, boundary_exchange_projector, warmth_response_factor, water_patch_fields, kernel_coefficients, local_exchange_matrix, patch_average_matrix, water_kernel_offset, water_readout_matrix, patch_holder_index, water_point_indicator, water_point_totals):
    column_order = jnp.arange(2 * K, dtype=jnp.int32)
    forward, inverse = dft_tables(MERIDIANS, column_order)
    forward_f = forward.astype(jnp.float32)
    inverse_f = inverse.astype(jnp.float32)

    def analyse(parallel_line):
        return jnp.dot(forward_f.T, parallel_line.astype(jnp.float32)).astype(jnp.bfloat16)

    fourier = lax.map(analyse, air_field_lattice)
    paired = jnp.moveaxis(fourier.reshape(PARALLELS, K, 2, AIR_FEATURES), 0, 1)

    def latitudinal(operands):
        matrix, coeffs = operands
        matrix_f = matrix.astype(jnp.float32)
        spectrum = jnp.einsum('lt,tpc->lpc', matrix_f, coeffs.astype(jnp.float32))
        scaled = (spectrum * harmonic_damping_factor[:, None, :]).astype(jnp.bfloat16)
        return jnp.einsum('lt,lpc->tpc', matrix_f, scaled.astype(jnp.float32)).astype(jnp.bfloat16)

    damped_modes = lax.map(latitudinal, (associated_polynomial_matrix, paired))
    damped_modes = jnp.moveaxis(damped_modes, 0, 1).reshape(PARALLELS, 2 * K, AIR_FEATURES)

    flux_f = boundary_exchange_projector.astype(jnp.float32)

    def surface(parallel_line):
        return jnp.dot(parallel_line.astype(jnp.float32), flux_f).T.astype(jnp.bfloat16)

    flux_rows = lax.map(surface, air_field_lattice)
    grouped = flux_rows.reshape(N_SEC, N_BAND, N_CH, LATD, NF, TPR, TW).transpose(0, 2, 1, 5, 4, 3, 6)
    grouped = grouped.reshape(N_SEC, N_CH, N_BAND * TPR, NF, LATD, TW).astype(jnp.float32)

    owner_grid = patch_holder_index.reshape(N_SEC, N_BAND, N_CH, TPR)
    group_tiles = owner_grid.transpose(0, 2, 1, 3).reshape(N_SEC, N_CH, N_BAND * TPR)
    holders = jnp.arange(N_BAND, dtype=jnp.int32)
    mine = group_tiles[:, :, None, :] == holders[None, None, :, None]
    ranks = jnp.cumsum(mine.astype(jnp.int32), axis=-1) - 1
    slot_index = jnp.arange(TSLOT, dtype=jnp.int32)
    chooser = (mine[:, :, :, None, :] & (ranks[:, :, :, None, :] == slot_index[None, None, None, :, None])).astype(jnp.float32)
    tile_flux = jnp.einsum('scbit,sctfrw->sbcifrw', chooser, grouped)
    tile_flux = tile_flux.reshape(DEVICES, TSLOT, NF, LATD, TW).astype(jnp.bfloat16)

    def ocean_device(operands):
        state, flux_tile, mask_tile, count_tile = operands
        return ocean_update(state, flux_tile, mask_tile, count_tile, kernel_coefficients, local_exchange_matrix, patch_average_matrix, water_kernel_offset, water_readout_matrix)

    ocean_next = lax.map(ocean_device, (water_patch_fields.reshape(DEVICES, TSLOT, OCH, LATD + 2, TW + 2), tile_flux, water_point_indicator.reshape(DEVICES, TSLOT, LATD, TW), water_point_totals.reshape(DEVICES, TSLOT)))

    sea_slots = ocean_next[:, :, 0].reshape(N_SEC, N_BAND, N_CH, TSLOT, LATD, TW)
    rank_tile = jnp.sum(jnp.where(mine, ranks, 0), axis=2)
    rank_grid = rank_tile.reshape(N_SEC, N_CH, N_BAND, TPR).transpose(0, 2, 1, 3)
    sec_idx = jnp.arange(N_SEC, dtype=jnp.int32)[:, None, None, None]
    core_idx = jnp.arange(N_CH, dtype=jnp.int32)[None, None, :, None]
    chosen_entries = sea_slots[sec_idx, owner_grid, core_idx, rank_grid]
    water_skin_warmth = chosen_entries.transpose(0, 1, 2, 4, 3, 5).reshape(PARALLELS, MERIDIANS)

    def merge_parts(operands):
        coeffs, parallel_line, water_line = operands
        reconstruct_physical = jnp.dot(inverse_f.T, coeffs.astype(jnp.float32))
        advanced_pair = parallel_line.astype(jnp.float32) + reconstruct_physical + water_line.astype(jnp.float32)[:, None] * warmth_response_factor[None, :]
        return advanced_pair.astype(jnp.bfloat16)

    advanced_air_field = lax.map(merge_parts, (damped_modes, air_field_lattice, water_skin_warmth))
    return advanced_air_field, ocean_next.reshape(OSLOTS, OCH, LATD, TW)
```

```python
import functools
import math

import jax
import jax.numpy as jnp
import numpy as np
from jax import lax
from jax.sharding import PartitionSpec as P

K = 512
AXES = ("sec", "band", "ch")
PARTS = (256, 512)


@functools.lru_cache(maxsize=None)
def dft_table(meridian_number):
    cell_index = np.arange(meridian_number, dtype=np.int64)[:, None]
    column = np.arange(2 * K, dtype=np.int64)[None, :]
    phase_angle = (cell_index * (column // 2) % meridian_number) * (2.0 * math.pi / meridian_number)
    table = np.where(column % 2 == 0, np.cos(phase_angle), -np.sin(phase_angle))
    return table.astype(np.float32).astype(jnp.bfloat16)


def ocean_update(
    state,
    tile_flux,
    mask_tile,
    count_tile,
    kernel_coefficients,
    local_exchange_matrix,
    patch_average_matrix,
    water_kernel_offset,
    water_readout_matrix,
):
    parallel_lines = mask_tile.shape[1]
    tile_width = mask_tile.shape[2]
    mask_f = mask_tile.astype(jnp.float32)
    masked = tile_flux * mask_tile[:, None].astype(jnp.bfloat16)
    fmean = (
        jnp.sum(masked.astype(jnp.float32), axis=(2, 3))
        / jnp.maximum(count_tile.astype(jnp.float32), 1.0)[:, None]
    )
    total = jnp.einsum(
        "fo,sfrw->sorw", local_exchange_matrix, masked, preferred_element_type=jnp.float32
    )
    for shift_row in range(3):
        for shift_col in range(3):
            window = state[
                :, :, shift_row : shift_row + parallel_lines, shift_col : shift_col + tile_width
            ]
            total = total + jnp.einsum(
                "io,sirw->sorw",
                kernel_coefficients[shift_row, shift_col],
                window,
                preferred_element_type=jnp.float32,
            )
    mean_term = jnp.sum(fmean[:, :, None] * patch_average_matrix[None], axis=1)
    total = total + mean_term[:, :, None, None] + water_kernel_offset[None, :, None, None]
    hidden = jax.nn.gelu(total, approximate=True).astype(jnp.bfloat16)
    update = jnp.einsum(
        "io,sirw->sorw", water_readout_matrix, hidden, preferred_element_type=jnp.float32
    )
    fresh = (
        state[:, :, 1 : 1 + parallel_lines, 1 : 1 + tile_width].astype(jnp.float32) + update
    ) * mask_f[:, None]
    return fresh.astype(jnp.bfloat16)


def shards(
    air_field_lattice,
    associated_polynomial_matrix,
    harmonic_damping_factor,
    boundary_exchange_projector,
    warmth_response_factor,
    water_patch_fields,
    kernel_coefficients,
    local_exchange_matrix,
    patch_average_matrix,
    water_kernel_offset,
    water_readout_matrix,
    patch_holder_index,
    water_point_indicator,
    water_point_totals,
):
    parallel_lines, meridian_number, channel_count = air_field_lattice.shape
    sec_count = lax.axis_size("sec")
    band_count = lax.axis_size("band")
    core_count = lax.axis_size("ch")
    device_count = sec_count * band_count * core_count
    total_cols = 2 * K
    per_device = total_cols // device_count
    slot_count = water_patch_fields.shape[0]
    mode_count = associated_polynomial_matrix.shape[0]
    lat_count = associated_polynomial_matrix.shape[1]
    table = dft_table(meridian_number)
    forward = jnp.asarray(np.ascontiguousarray(table.T))
    backward = jnp.asarray((table.astype(np.float32) * (2.0 / meridian_number)).astype(jnp.bfloat16))

    ends = np.cumsum((0,) + PARTS)
    spans = [slice(int(a), int(b)) for a, b in zip(ends[:-1], ends[1:])]
    collected = []
    for span in spans:
        fourier = jnp.einsum(
            "qn,anc->aqc", forward, air_field_lattice[:, :, span], preferred_element_type=jnp.float32
        ).astype(jnp.bfloat16)
        collected.append(lax.all_to_all(fourier, AXES, split_axis=1, concat_axis=0, tiled=True))
    returned = []
    for span, coeffs in zip(spans, collected):
        width = coeffs.shape[-1]
        pairs = coeffs.reshape(lat_count, mode_count, 2, width)
        spectrum = jnp.einsum(
            "mlt,tmpc->mlpc", associated_polynomial_matrix, pairs, preferred_element_type=jnp.float32
        )
        scaled = (spectrum * harmonic_damping_factor[None, :, None, span]).astype(jnp.bfloat16)
        damped = jnp.einsum(
            "mlt,mlpc->tmpc", associated_polynomial_matrix, scaled, preferred_element_type=jnp.float32
        ).astype(jnp.bfloat16).reshape(lat_count, per_device, width)
        returned.append(lax.all_to_all(damped, AXES, split_axis=0, concat_axis=1, tiled=True))

    flux_local = jnp.einsum(
        "anc,cf->fan",
        air_field_lattice,
        boundary_exchange_projector,
        preferred_element_type=jnp.float32,
    ).astype(jnp.bfloat16)
    gathered = lax.all_gather(flux_local, "band", axis=1, tiled=True)
    sec_id = lax.axis_index("sec")
    band_id = lax.axis_index("band")
    core_id = lax.axis_index("ch")
    owner_grid = patch_holder_index.reshape(sec_count, band_count, core_count, -1)
    tiles_per_row = owner_grid.shape[3]
    owner_group = lax.dynamic_index_in_dim(owner_grid, sec_id, 0, keepdims=False)
    owner_group = lax.dynamic_index_in_dim(owner_group, core_id, 1, keepdims=False)
    owner_flat = owner_group.reshape(-1)
    holders = jnp.arange(band_count, dtype=jnp.int32)
    mine_all = owner_flat[None, :] == holders[:, None]
    rank_all = jnp.cumsum(mine_all.astype(jnp.int32), axis=1) - 1
    slot_index = jnp.arange(slot_count, dtype=jnp.int32)
    pick_all = mine_all[:, None, :] & (rank_all[:, None, :] == slot_index[None, :, None])
    my_pick = lax.dynamic_index_in_dim(pick_all, band_id, 0, keepdims=False)
    flux_count = gathered.shape[0]
    tile_width = meridian_number // tiles_per_row
    pieces = gathered.reshape(flux_count, band_count, parallel_lines, tiles_per_row, tile_width)
    chooser = my_pick.reshape(slot_count, band_count, tiles_per_row).astype(jnp.bfloat16)
    tile_flux = jnp.einsum(
        "sbj,fbrjw->sfrw", chooser, pieces, preferred_element_type=jnp.float32
    ).astype(jnp.bfloat16)
    ocean_next = ocean_update(
        water_patch_fields,
        tile_flux,
        water_point_indicator,
        water_point_totals,
        kernel_coefficients,
        local_exchange_matrix,
        patch_average_matrix,
        water_kernel_offset,
        water_readout_matrix,
    )
    sea_slots = ocean_next[:, 0]
    sea_all = lax.all_gather(sea_slots, "band", axis=0, tiled=True)
    rank_tile = jnp.sum(jnp.where(mine_all, rank_all, 0), axis=0)
    my_owners = lax.dynamic_index_in_dim(owner_group, band_id, 0, keepdims=False)
    my_ranks = lax.dynamic_slice_in_dim(rank_tile, band_id * tiles_per_row, tiles_per_row)
    target = my_owners * slot_count + my_ranks
    selector = (
        target[:, None] == jnp.arange(band_count * slot_count, dtype=jnp.int32)[None, :]
    ).astype(jnp.bfloat16)
    water_patches = jnp.einsum(
        "jk,krw->rjw", selector, sea_all, preferred_element_type=jnp.float32
    ).astype(jnp.bfloat16)
    water_skin_warmth = water_patches.reshape(parallel_lines, meridian_number)
    pieces_out = []
    for span, coeffs in zip(spans, returned):
        rebuilt = jnp.einsum("nq,aqc->anc", backward, coeffs, preferred_element_type=jnp.float32)
        pieces_out.append(
            (
                air_field_lattice[:, :, span].astype(jnp.float32)
                + rebuilt
                + water_skin_warmth.astype(jnp.float32)[:, :, None]
                * warmth_response_factor[None, None, span]
            ).astype(jnp.bfloat16)
        )
    return (jnp.concatenate(pieces_out, axis=-1), ocean_next)


def solution(mesh):
    placed = (
        P(("sec", "band", "ch"), None, None),
        P(("sec", "band", "ch"), None, None),
        P(),
        P(),
        P(),
        P(("sec", "band", "ch"), None, None, None),
        P(),
        P(),
        P(),
        P(),
        P(),
        P(),
        P(("sec", "band", "ch"), None, None),
        P(("sec", "band", "ch")),
    )
    return jax.shard_map(
        shards,
        mesh=mesh,
        in_specs=placed,
        out_specs=(
            P(("sec", "band", "ch"), None, None),
            P(("sec", "band", "ch"), None, None, None),
        ),
        check_vma=False,
    )
```

```python
import functools
import math

import jax
import jax.numpy as jnp
import numpy as np
from jax import lax
from jax.experimental import pallas as pl
from jax.experimental.pallas import tpu as pltpu
from jax.sharding import PartitionSpec as P

K = 512
AXES = ("sec", "band", "ch")
GROUP = 16
SLIM = 128
MIB = 1024 * 1024


@functools.lru_cache(maxsize=None)
def dft_table(meridian_number):
    cell_index = np.arange(meridian_number, dtype=np.int64)[:, None]
    column = np.arange(2 * K, dtype=np.int64)[None, :]
    phase_angle = (cell_index * (column // 2) % meridian_number) * (2.0 * math.pi / meridian_number)
    table = np.where(column % 2 == 0, np.cos(phase_angle), -np.sin(phase_angle))
    return table.astype(np.float32).astype(jnp.bfloat16)


@functools.lru_cache(maxsize=None)
def folded_tables(meridian_number, groups):
    half = meridian_number // 2
    table = dft_table(meridian_number)[:half].astype(np.float32)
    per_parity = table.reshape(half, groups, -1, 2, 2).transpose(3, 1, 2, 4, 0)
    forward = per_parity.reshape(2, -1, half)
    backward = forward.transpose(0, 2, 1) * (2.0 / meridian_number)
    return tuple(np.ascontiguousarray(x).astype(jnp.bfloat16) for x in (forward, backward))


def ocean_update(
    state,
    tile_flux,
    mask_tile,
    count_tile,
    kernel_coefficients,
    local_exchange_matrix,
    patch_average_matrix,
    water_kernel_offset,
    water_readout_matrix,
):
    parallel_lines = mask_tile.shape[1]
    tile_width = mask_tile.shape[2]
    mask_f = mask_tile.astype(jnp.float32)
    masked = tile_flux * mask_tile[:, None].astype(jnp.bfloat16)
    fmean = (
        jnp.sum(masked.astype(jnp.float32), axis=(2, 3))
        / jnp.maximum(count_tile.astype(jnp.float32), 1.0)[:, None]
    )
    total = jnp.einsum(
        "fo,sfrw->sorw", local_exchange_matrix, masked, preferred_element_type=jnp.float32
    )
    for shift_row in range(3):
        for shift_col in range(3):
            window = state[
                :, :, shift_row : shift_row + parallel_lines, shift_col : shift_col + tile_width
            ]
            total = total + jnp.einsum(
                "io,sirw->sorw",
                kernel_coefficients[shift_row, shift_col],
                window,
                preferred_element_type=jnp.float32,
            )
    mean_term = jnp.sum(fmean[:, :, None] * patch_average_matrix[None], axis=1)
    total = total + mean_term[:, :, None, None] + water_kernel_offset[None, :, None, None]
    hidden = jax.nn.gelu(total, approximate=True).astype(jnp.bfloat16)
    update = jnp.einsum(
        "io,sirw->sorw", water_readout_matrix, hidden, preferred_element_type=jnp.float32
    )
    fresh = (
        state[:, :, 1 : 1 + parallel_lines, 1 : 1 + tile_width].astype(jnp.float32) + update
    ) * mask_f[:, None]
    return fresh.astype(jnp.bfloat16)


def compiler_params():
    return pltpu.CompilerParams(vmem_limit_bytes=60 * MIB)


def cost(flops, *arrays):
    return pl.CostEstimate(
        flops=flops, bytes_accessed=sum(x.size * x.dtype.itemsize for x in arrays), transcendentals=0
    )


def fold(low, high, odd):
    low, high = low.astype(jnp.float32), high.astype(jnp.float32)
    return jnp.where(odd == 1, low - high, low + high).astype(jnp.bfloat16)


def lane_spans(width, size=256):
    return [slice(at, min(at + size, width)) for at in range(0, width, size)]


def analyse_wide(air, table, width, groups):
    lines, cells, _ = air.shape
    half = cells // 2
    out = jax.ShapeDtypeStruct((groups, lines, 2 * GROUP, width), jnp.bfloat16)

    def body(table_ref, air_ref, out_ref):
        for span in lane_spans(width):
            low = air_ref[0, :half, span].astype(jnp.float32)
            high = air_ref[0, half:, span].astype(jnp.float32)
            for odd, folded in enumerate((low + high, low - high)):
                coeffs = jnp.dot(table_ref[odd], folded.astype(jnp.bfloat16), preferred_element_type=jnp.float32)
                out_ref[:, :, odd * GROUP : (odd + 1) * GROUP, span] = coeffs.astype(jnp.bfloat16).reshape(
                    groups, 1, GROUP, -1
                )

    return pl.pallas_call(
        body,
        grid=(lines,),
        in_specs=[
            pl.BlockSpec(table.shape, lambda a: (0, 0, 0)),
            pl.BlockSpec((1, cells, width), lambda a: (a, 0, 0)),
        ],
        out_specs=pl.BlockSpec((groups, 1, 2 * GROUP, width), lambda a: (0, a, 0, 0)),
        out_shape=out,
        compiler_params=compiler_params(),
        cost_estimate=cost(lines * cells * cells * width, table, air, out),
        name="analyse_wide",
    )(table, air)


def analyse_slim(air, table, start, sec, sections, groups):
    lines, cells, channels = air.shape
    half = cells // 2
    width = channels - start
    plane = groups // sections
    out = jax.ShapeDtypeStruct((lines, plane, 2 * GROUP, width), jnp.bfloat16)

    def body(sec_ref, table_ref, air_ref, *refs):
        outs, blocks = refs[:-1], refs[-1]
        both = jnp.concatenate([air_ref[a] for a in range(lines)], axis=1)
        folded = fold(both[:half], both[half:], pl.program_id(0))
        coeffs = jnp.dot(table_ref[0], folded, preferred_element_type=jnp.float32)
        blocks[...] = coeffs.astype(jnp.bfloat16).reshape(sections, plane, GROUP, lines * width)
        for o, out_ref in enumerate(outs):
            for a in range(lines):
                out_ref[a] = blocks[sec_ref[0] ^ o, :, :, a * width : (a + 1) * width]

    return pl.pallas_call(
        body,
        grid=(2,),
        in_specs=[
            pl.BlockSpec(memory_space=pltpu.SMEM),
            pl.BlockSpec((1,) + table.shape[1:], lambda p: (p, 0, 0)),
            pl.BlockSpec((lines, cells, width), lambda p: (0, 0, start // width)),
        ],
        out_specs=[pl.BlockSpec((lines, plane, GROUP, width), lambda p: (0, 0, p, 0))] * sections,
        out_shape=[out] * sections,
        scratch_shapes=[pltpu.VMEM((sections, plane, GROUP, lines * width), jnp.bfloat16)],
        compiler_params=compiler_params(),
        cost_estimate=cost(lines * cells * cells * width, table, *[out] * 2 * sections),
        name="analyse_slim",
    )(sec, table, air)


def wavenumber_at(row):
    return row % GROUP // 2 * 2 + row // GROUP


def damp(transform, coeffs, damping):
    spectrum = jnp.dot(transform, coeffs, preferred_element_type=jnp.float32)
    scaled = (spectrum * damping).astype(jnp.bfloat16)
    back = lax.dot_general(transform, scaled, (((0,), (0,)), ((), ())), preferred_element_type=jnp.float32)
    return back.astype(jnp.bfloat16)


def latitudinal_wide(coeffs, matrix, damping):
    devices, lines, rows, width = coeffs.shape
    modes, degrees, lats = matrix.shape

    def body(x_ref, matrix_ref, damping_ref, out_ref):
        for span in lane_spans(width):
            by_coeff = jnp.swapaxes(x_ref[:, :, :, span].reshape(lats, rows, -1), 0, 1)
            results = [
                damp(matrix_ref[wavenumber_at(row)], by_coeff[row], damping_ref[:, span]) for row in range(rows)
            ]
            out_ref[:, :, :, span] = jnp.swapaxes(jnp.stack(results), 0, 1).reshape(devices, lines, rows, -1)

    return pl.pallas_call(
        body,
        grid=(1,),
        in_specs=[whole(coeffs), whole(matrix), pl.BlockSpec((degrees, width), lambda i: (0, 0))],
        out_specs=whole(coeffs),
        out_shape=jax.ShapeDtypeStruct(coeffs.shape, jnp.bfloat16),
        compiler_params=compiler_params(),
        cost_estimate=cost(4 * rows * degrees * lats * width, coeffs, coeffs, matrix),
        name="latitudinal_wide",
    )(coeffs, matrix, damping)


def whole(x):
    return pl.BlockSpec(x.shape, lambda *_: (0,) * len(x.shape))


def to_plane(parts, place):
    lines, plane, rows, width = parts[0].shape
    sections = len(parts)
    out = jax.ShapeDtypeStruct((sections, lines, rows, width), jnp.bfloat16)

    def body(place_ref, *refs):
        for p, out_ref in enumerate(refs[sections:]):
            for o in range(sections):
                for a in range(lines):
                    out_ref[o, a] = refs[o][a, place_ref[0] ^ p]

    return pl.pallas_call(
        body,
        grid=(1,),
        in_specs=[pl.BlockSpec(memory_space=pltpu.SMEM)] + [whole(parts[0])] * sections,
        out_specs=[whole(out)] * plane,
        out_shape=[out] * plane,
        compiler_params=compiler_params(),
        cost_estimate=cost(0, *parts, *parts),
        name="to_plane",
    )(place, *parts)


def from_plane(parts, place):
    sections, lines, rows, width = parts[0].shape
    plane = len(parts)
    out = jax.ShapeDtypeStruct((lines, plane, rows, width), jnp.bfloat16)

    def body(place_ref, *refs):
        for o, out_ref in enumerate(refs[plane:]):
            for p in range(plane):
                for a in range(lines):
                    out_ref[a, place_ref[0] ^ p] = refs[p][o, a]

    return pl.pallas_call(
        body,
        grid=(1,),
        in_specs=[pl.BlockSpec(memory_space=pltpu.SMEM)] + [whole(parts[0])] * plane,
        out_specs=[whole(out)] * sections,
        out_shape=[out] * sections,
        compiler_params=compiler_params(),
        cost_estimate=cost(0, *parts, *parts),
        name="from_plane",
    )(place, *parts)


def latitudinal_slim(parts, matrix, damping, start):
    sections, lines, rows, width = parts[0].shape
    plane = len(parts)
    degrees = damping.shape[0]
    own = sections * lines
    out = jax.ShapeDtypeStruct(parts[0].shape, jnp.bfloat16)

    def body(matrix_ref, damping_ref, *refs):
        latitudes = jnp.concatenate([ref[...].reshape(own, rows, width) for ref in refs[:plane]], axis=0)
        by_coeff = jnp.swapaxes(latitudes, 0, 1)
        results = [
            damp(matrix_ref[wavenumber_at(row)], by_coeff[row], damping_ref[...]) for row in range(rows)
        ]
        by_lat = jnp.swapaxes(jnp.stack(results), 0, 1)
        for p, out_ref in enumerate(refs[plane:]):
            out_ref[...] = by_lat[p * own : (p + 1) * own].reshape(out_ref.shape)

    return pl.pallas_call(
        body,
        grid=(1,),
        in_specs=[
            whole(matrix),
            pl.BlockSpec((degrees, width), lambda i: (0, start // width)),
        ]
        + [whole(out)] * plane,
        out_specs=[whole(out)] * plane,
        out_shape=[out] * plane,
        compiler_params=compiler_params(),
        cost_estimate=cost(4 * rows * degrees * plane * own * width, matrix, *parts, *parts),
        name="latitudinal_slim",
    )(matrix, damping, *parts)


def advance(air, rebuilt, sea, warmth):
    warmed = lax.dot_general(sea, warmth, (((0,), (0,)), ((), ())), preferred_element_type=jnp.float32)
    return (air.astype(jnp.float32) + rebuilt + warmed).astype(jnp.bfloat16)


def three_parts(values):
    parts, rest = [], values
    for _ in range(3):
        parts.append(lax.reduce_precision(rest, 8, 7))
        rest = rest - parts[-1]
    parts += [jnp.zeros_like(values)] * (GROUP - 3)
    return jnp.stack(parts).astype(jnp.bfloat16)


def synthesise_slim(parts, table, air, sea, warmth, start, sec):
    lines, plane, rows, width = parts[0].shape
    sections = len(parts)
    half = air.shape[2]

    def body(sec_ref, table_ref, air_ref, sea_ref, warmth_ref, *refs):
        part_refs, out_ref, gathered = refs[:sections], refs[-2], refs[-1]
        for o, part_ref in enumerate(part_refs):
            for a in range(lines):
                for odd in range(2):
                    gathered[odd, sec_ref[0] ^ o, :, :, a * width : (a + 1) * width] = part_ref[
                        a, :, odd * GROUP : (odd + 1) * GROUP, :
                    ]
        even, odd = (
            jnp.dot(
                table_ref[odd],
                gathered[odd].reshape(sections * plane * GROUP, lines * width),
                preferred_element_type=jnp.float32,
            )
            for odd in range(2)
        )
        for at, rebuilt in enumerate((even + odd, even - odd)):
            for a in range(lines):
                out_ref[a, at] = advance(
                    air_ref[a, at], rebuilt[:, a * width : (a + 1) * width], sea_ref[a, at], warmth_ref[...]
                )

    return pl.pallas_call(
        body,
        grid=(1,),
        in_specs=[
            pl.BlockSpec(memory_space=pltpu.SMEM),
            pl.BlockSpec(table.shape, lambda i: (0, 0, 0)),
            pl.BlockSpec((lines, 2, half, width), lambda i: (0, 0, 0, start // width)),
            whole(sea),
            pl.BlockSpec((GROUP, width), lambda i: (0, start // width)),
        ]
        + [pl.BlockSpec(parts[0].shape, lambda i: (0, 0, 0, 0))] * sections,
        out_specs=pl.BlockSpec((lines, 2, half, width), lambda i: (0, 0, 0, start // width)),
        out_shape=jax.ShapeDtypeStruct(air.shape, jnp.bfloat16),
        scratch_shapes=[pltpu.VMEM((2, sections, plane, GROUP, lines * width), jnp.bfloat16)],
        compiler_params=compiler_params(),
        cost_estimate=pl.CostEstimate(flops=10**11, bytes_accessed=3 * 10**8, transcendentals=0),
        name="synthesise_slim",
    )(sec, table, air, sea, warmth, *parts)


def synthesise_wide(coeffs, table, air, sea, warmth, begun):
    groups, lines, rows, width = coeffs.shape
    half = air.shape[2]

    def body(table_ref, coeff_ref, air_ref, sea_ref, warmth_ref, begun_ref, out_ref):
        for span in lane_spans(width):
            even, odd = (
                jnp.dot(
                    table_ref[odd],
                    coeff_ref[:, 0, odd * GROUP : (odd + 1) * GROUP, span].reshape(groups * GROUP, -1),
                    preferred_element_type=jnp.float32,
                )
                for odd in range(2)
            )
            for at, rebuilt in enumerate((even + odd, even - odd)):
                out_ref[0, at, :, span] = advance(
                    air_ref[0, at, :, span], rebuilt, sea_ref[0, at], warmth_ref[:, span]
                )

    return pl.pallas_call(
        body,
        grid=(lines,),
        in_specs=[
            pl.BlockSpec(table.shape, lambda a: (0, 0, 0)),
            pl.BlockSpec((groups, 1, rows, width), lambda a: (0, a, 0, 0)),
            pl.BlockSpec((1, 2, half, width), lambda a: (a, 0, 0, 0)),
            pl.BlockSpec((1, 2, GROUP, half), lambda a: (a, 0, 0, 0)),
            pl.BlockSpec((GROUP, width), lambda a: (0, 0)),
            pl.BlockSpec(memory_space=pl.ANY),
        ],
        out_specs=pl.BlockSpec((1, 2, half, width), lambda a: (a, 0, 0, 0)),
        out_shape=jax.ShapeDtypeStruct(air.shape, jnp.bfloat16),
        input_output_aliases={5: 0},
        compiler_params=compiler_params(),
        cost_estimate=cost(4 * lines * half * half * width, table, coeffs, coeffs, coeffs),
        name="synthesise_wide",
    )(table, coeffs, air, sea, warmth, begun)


def gather_flux(air, projector):
    flux_local = jnp.einsum(
        "anc,cf->fan",
        air,
        projector,
        preferred_element_type=jnp.float32,
    ).astype(jnp.bfloat16)
    return lax.all_gather(flux_local, "band", axis=1, tiled=True)


def shards(
    air_field_lattice,
    associated_polynomial_matrix,
    harmonic_damping_factor,
    boundary_exchange_projector,
    warmth_response_factor,
    water_patch_fields,
    kernel_coefficients,
    local_exchange_matrix,
    patch_average_matrix,
    water_kernel_offset,
    water_readout_matrix,
    patch_holder_index,
    water_point_indicator,
    water_point_totals,
):
    parallel_lines, meridian_number, channel_count = air_field_lattice.shape
    sec_count = lax.axis_size("sec")
    band_count = lax.axis_size("band")
    core_count = lax.axis_size("ch")
    device_count = sec_count * band_count * core_count
    total_cols = 2 * K
    per_device = total_cols // device_count
    slot_count = water_patch_fields.shape[0]
    mode_count = associated_polynomial_matrix.shape[0]
    lat_count = associated_polynomial_matrix.shape[1]
    wide = channel_count - SLIM
    in_kernels = (
        per_device == 2 * GROUP
        and wide > 0
        and wide % SLIM == 0
        and sec_count & (sec_count - 1) == 0
        and lat_count == device_count * parallel_lines
    )
    if in_kernels:
        plane = band_count * core_count
        sec_id = lax.axis_index("sec")
        sec = sec_id.reshape(1).astype(jnp.int32)
        forward, backward = map(jnp.asarray, folded_tables(meridian_number, device_count))
        hops = [[(i, i ^ o) for i in range(sec_count)] for o in range(sec_count)]

        twists = [[(i, i ^ p) for i in range(plane)] for p in range(plane)]
        place = (lax.axis_index("band") * core_count + lax.axis_index("ch")).astype(jnp.int32)

        def over_sections(blocks):
            return [lax.ppermute(x, "sec", hops[o]) if o else x for o, x in enumerate(blocks)]

        def over_plane(blocks):
            return [lax.ppermute(x, ("band", "ch"), twists[p]) if p else x for p, x in enumerate(blocks)]

        at_lat = jnp.arange(lat_count, dtype=jnp.int32)
        sections_at = at_lat // parallel_lines % sec_count ^ sec_id
        places_at = at_lat // (parallel_lines * sec_count) ^ place
        order = (sections_at * plane + places_at) * parallel_lines + at_lat % parallel_lines
        shuffle = (at_lat[:, None] == order[None, :]).astype(jnp.bfloat16)
        shuffled = jnp.einsum(
            "mlt,tu->mlu", associated_polynomial_matrix, shuffle, preferred_element_type=jnp.float32
        ).astype(jnp.bfloat16)

        slim = analyse_slim(air_field_lattice, forward, wide, sec, sec_count, device_count)
        air_after, *slim = lax.optimization_barrier((air_field_lattice, *slim))
        slim = over_sections(slim)
        wide_coeffs = analyse_wide(air_after, forward, wide, device_count)
        wide_coeffs, *slim = lax.optimization_barrier((wide_coeffs, *slim))
        wide_coeffs = lax.all_to_all(wide_coeffs, AXES, split_axis=0, concat_axis=0, tiled=True)
        slim = to_plane(slim, place.reshape(1))
        air_after, *slim = lax.optimization_barrier((air_field_lattice, *slim))
        slim = over_plane(slim)
        gathered = gather_flux(air_after, boundary_exchange_projector)
        gathered, *slim = lax.optimization_barrier((gathered, *slim))
        slim = latitudinal_slim(slim, shuffled, harmonic_damping_factor, wide)
        slim = from_plane(over_plane(slim), place.reshape(1))
        wide_coeffs, *slim = lax.optimization_barrier((wide_coeffs, *slim))
        slim = over_sections(slim)
        wide_coeffs = latitudinal_wide(wide_coeffs, associated_polynomial_matrix, harmonic_damping_factor)
        wide_coeffs = lax.all_to_all(wide_coeffs, AXES, split_axis=0, concat_axis=0, tiled=True)
        water_patch_fields, gathered, *slim = lax.optimization_barrier((water_patch_fields, gathered, *slim))
    else:
        gathered = gather_flux(air_field_lattice, boundary_exchange_projector)
        table = dft_table(meridian_number)
        forward = jnp.asarray(np.ascontiguousarray(table.T))
        backward = jnp.asarray((table.astype(np.float32) * (2.0 / meridian_number)).astype(jnp.bfloat16))
        fourier = jnp.einsum(
            "qn,anc->aqc", forward, air_field_lattice, preferred_element_type=jnp.float32
        ).astype(jnp.bfloat16)
        collected = lax.all_to_all(fourier, AXES, split_axis=1, concat_axis=0, tiled=True)
        pairs = collected.reshape(lat_count, mode_count, 2, channel_count)
        spectrum = jnp.einsum(
            "mlt,tmpc->mlpc", associated_polynomial_matrix, pairs, preferred_element_type=jnp.float32
        )
        scaled = (spectrum * harmonic_damping_factor[None, :, None]).astype(jnp.bfloat16)
        damped = jnp.einsum(
            "mlt,mlpc->tmpc", associated_polynomial_matrix, scaled, preferred_element_type=jnp.float32
        ).astype(jnp.bfloat16).reshape(lat_count, per_device, channel_count)
        returned = lax.all_to_all(damped, AXES, split_axis=0, concat_axis=1, tiled=True)

    sec_id = lax.axis_index("sec")
    band_id = lax.axis_index("band")
    core_id = lax.axis_index("ch")
    owner_grid = patch_holder_index.reshape(sec_count, band_count, core_count, -1)
    tiles_per_row = owner_grid.shape[3]
    owner_group = lax.dynamic_index_in_dim(owner_grid, sec_id, 0, keepdims=False)
    owner_group = lax.dynamic_index_in_dim(owner_group, core_id, 1, keepdims=False)
    owner_flat = owner_group.reshape(-1)
    holders = jnp.arange(band_count, dtype=jnp.int32)
    mine_all = owner_flat[None, :] == holders[:, None]
    rank_all = jnp.cumsum(mine_all.astype(jnp.int32), axis=1) - 1
    slot_index = jnp.arange(slot_count, dtype=jnp.int32)
    pick_all = mine_all[:, None, :] & (rank_all[:, None, :] == slot_index[None, :, None])
    my_pick = lax.dynamic_index_in_dim(pick_all, band_id, 0, keepdims=False)
    flux_count = gathered.shape[0]
    tile_width = meridian_number // tiles_per_row
    pieces = gathered.reshape(flux_count, band_count, parallel_lines, tiles_per_row, tile_width)
    chooser = my_pick.reshape(slot_count, band_count, tiles_per_row).astype(jnp.bfloat16)
    tile_flux = jnp.einsum(
        "sbj,fbrjw->sfrw", chooser, pieces, preferred_element_type=jnp.float32
    ).astype(jnp.bfloat16)
    ocean_next = ocean_update(
        water_patch_fields,
        tile_flux,
        water_point_indicator,
        water_point_totals,
        kernel_coefficients,
        local_exchange_matrix,
        patch_average_matrix,
        water_kernel_offset,
        water_readout_matrix,
    )
    sea_slots = ocean_next[:, 0]
    sea_all = lax.all_gather(sea_slots, "band", axis=0, tiled=True)
    rank_tile = jnp.sum(jnp.where(mine_all, rank_all, 0), axis=0)
    my_owners = lax.dynamic_index_in_dim(owner_group, band_id, 0, keepdims=False)
    my_ranks = lax.dynamic_slice_in_dim(rank_tile, band_id * tiles_per_row, tiles_per_row)
    target = my_owners * slot_count + my_ranks
    selector = (
        target[:, None] == jnp.arange(band_count * slot_count, dtype=jnp.int32)[None, :]
    ).astype(jnp.bfloat16)
    water_patches = jnp.einsum(
        "jk,krw->rjw", selector, sea_all, preferred_element_type=jnp.float32
    ).astype(jnp.bfloat16)
    water_skin_warmth = water_patches.reshape(parallel_lines, meridian_number)
    if in_kernels:
        halves = (parallel_lines, 2, meridian_number // 2, -1)
        air = air_field_lattice.reshape(halves)
        sea = water_skin_warmth.reshape(parallel_lines, 2, 1, meridian_number // 2)
        sea = jnp.broadcast_to(sea, (parallel_lines, 2, GROUP, meridian_number // 2))
        warmth = three_parts(warmth_response_factor)
        begun = synthesise_slim(slim, backward, air, sea, warmth, wide, sec)
        advanced = synthesise_wide(wide_coeffs, backward, air, sea, warmth, begun)
        advanced = advanced.reshape(air_field_lattice.shape)
    else:
        rebuilt = jnp.einsum("nq,aqc->anc", backward, returned, preferred_element_type=jnp.float32)
        advanced = (
            air_field_lattice.astype(jnp.float32)
            + rebuilt
            + water_skin_warmth.astype(jnp.float32)[:, :, None] * warmth_response_factor[None, None]
        ).astype(jnp.bfloat16)
    return (advanced, ocean_next)


def solution(mesh):
    placed = (
        P(("sec", "band", "ch"), None, None),
        P(("sec", "band", "ch"), None, None),
        P(),
        P(),
        P(),
        P(("sec", "band", "ch"), None, None, None),
        P(),
        P(),
        P(),
        P(),
        P(),
        P(),
        P(("sec", "band", "ch"), None, None),
        P(("sec", "band", "ch")),
    )
    return jax.shard_map(
        shards,
        mesh=mesh,
        in_specs=placed,
        out_specs=(
            P(("sec", "band", "ch"), None, None),
            P(("sec", "band", "ch"), None, None, None),
        ),
        check_vma=False,
    )
```

```python
import functools
import math

import jax
import jax.numpy as jnp
import numpy as np
from jax import lax
from jax.experimental import pallas as pl
from jax.experimental.pallas import tpu as pltpu
from jax.sharding import PartitionSpec as P

K = 512
AXES = ("sec", "band", "ch")
GROUP = 16
SLIM = 128
MIB = 1024 * 1024


@functools.lru_cache(maxsize=None)
def dft_table(meridian_number):
    cell_index = np.arange(meridian_number, dtype=np.int64)[:, None]
    column = np.arange(2 * K, dtype=np.int64)[None, :]
    phase_angle = (cell_index * (column // 2) % meridian_number) * (2.0 * math.pi / meridian_number)
    table = np.where(column % 2 == 0, np.cos(phase_angle), -np.sin(phase_angle))
    return table.astype(np.float32).astype(jnp.bfloat16)


@functools.lru_cache(maxsize=None)
def transform_tables(meridian_number, groups):
    half = meridian_number // 2
    table = dft_table(meridian_number).astype(np.float32)
    by_parity = table.reshape(meridian_number, groups, -1, 2, 2).transpose(1, 3, 2, 4, 0)
    forward = by_parity.reshape(-1, meridian_number)
    backward = by_parity.transpose(1, 4, 0, 2, 3)[:, :half].reshape(2, half, -1) * (2.0 / meridian_number)
    return tuple(np.ascontiguousarray(x).astype(jnp.bfloat16) for x in (forward, backward))


def ocean_update(
    state,
    tile_flux,
    mask_tile,
    count_tile,
    kernel_coefficients,
    local_exchange_matrix,
    patch_average_matrix,
    water_kernel_offset,
    water_readout_matrix,
):
    parallel_lines = mask_tile.shape[1]
    tile_width = mask_tile.shape[2]
    mask_f = mask_tile.astype(jnp.float32)
    masked = tile_flux * mask_tile[:, None].astype(jnp.bfloat16)
    fmean = (
        jnp.sum(masked.astype(jnp.float32), axis=(2, 3))
        / jnp.maximum(count_tile.astype(jnp.float32), 1.0)[:, None]
    )
    total = jnp.einsum(
        "fo,sfrw->sorw", local_exchange_matrix, masked, preferred_element_type=jnp.float32
    )
    for shift_row in range(3):
        for shift_col in range(3):
            window = state[
                :, :, shift_row : shift_row + parallel_lines, shift_col : shift_col + tile_width
            ]
            total = total + jnp.einsum(
                "io,sirw->sorw",
                kernel_coefficients[shift_row, shift_col],
                window,
                preferred_element_type=jnp.float32,
            )
    mean_term = jnp.sum(fmean[:, :, None] * patch_average_matrix[None], axis=1)
    total = total + mean_term[:, :, None, None] + water_kernel_offset[None, :, None, None]
    hidden = jax.nn.gelu(total, approximate=True).astype(jnp.bfloat16)
    update = jnp.einsum(
        "io,sirw->sorw", water_readout_matrix, hidden, preferred_element_type=jnp.float32
    )
    fresh = (
        state[:, :, 1 : 1 + parallel_lines, 1 : 1 + tile_width].astype(jnp.float32) + update
    ) * mask_f[:, None]
    return fresh.astype(jnp.bfloat16)


def compiler_params():
    return pltpu.CompilerParams(vmem_limit_bytes=60 * MIB)


def cost(flops, *arrays):
    return pl.CostEstimate(
        flops=flops, bytes_accessed=sum(x.size * x.dtype.itemsize for x in arrays), transcendentals=0
    )


def lane_spans(width, size=256):
    return [slice(at, min(at + size, width)) for at in range(0, width, size)]


def analyse_wide(air, table, width, groups):
    lines, cells, _ = air.shape
    rows = table.shape[0] // groups
    out = jax.ShapeDtypeStruct((groups, lines, rows, width), jnp.bfloat16)

    def body(table_ref, air_ref, out_ref):
        for span in lane_spans(width):
            coeffs = jnp.dot(table_ref[...], air_ref[0, :, span], preferred_element_type=jnp.float32)
            out_ref[:, :, :, span] = coeffs.astype(jnp.bfloat16).reshape(groups, 1, rows, -1)

    return pl.pallas_call(
        body,
        grid=(lines,),
        in_specs=[
            pl.BlockSpec(table.shape, lambda a: (0, 0)),
            pl.BlockSpec((1, cells, width), lambda a: (a, 0, 0)),
        ],
        out_specs=pl.BlockSpec((groups, 1, rows, width), lambda a: (0, a, 0, 0)),
        out_shape=out,
        compiler_params=compiler_params(),
        cost_estimate=cost(2 * lines * table.size * width, table, air, out),
        name="analyse_wide",
    )(table, air)


def analyse_slim(air, table, start, sec, sections, groups):
    lines, cells, channels = air.shape
    width = channels - start
    plane = groups // sections
    rows = table.shape[0] // groups
    size = plane * rows
    out = jax.ShapeDtypeStruct((lines, plane, rows, width), jnp.bfloat16)

    def body(sec_ref, table_ref, air_ref, *outs):
        both = jnp.concatenate([air_ref[a] for a in range(lines)], axis=1)
        for o, out_ref in enumerate(outs):
            part = pl.ds(pl.multiple_of((sec_ref[0] ^ o) * size, size), size)
            coeffs = jnp.dot(table_ref[part, :], both, preferred_element_type=jnp.float32).astype(jnp.bfloat16)
            for a in range(lines):
                out_ref[a] = coeffs[:, a * width : (a + 1) * width].reshape(plane, rows, width)

    return pl.pallas_call(
        body,
        grid=(1,),
        in_specs=[
            pl.BlockSpec(memory_space=pltpu.SMEM),
            pl.BlockSpec(table.shape, lambda i: (0, 0)),
            pl.BlockSpec((lines, cells, width), lambda i: (0, 0, start // width)),
        ],
        out_specs=[pl.BlockSpec(out.shape, lambda i: (0, 0, 0, 0))] * sections,
        out_shape=[out] * sections,
        compiler_params=compiler_params(),
        cost_estimate=cost(2 * lines * table.size * width, table, *[out] * 2 * sections),
        name="analyse_slim",
    )(sec, table, air)


def wavenumber_at(row):
    return row % GROUP // 2 * 2 + row // GROUP


def damp(transform, coeffs, damping):
    spectrum = jnp.dot(transform, coeffs, preferred_element_type=jnp.float32)
    scaled = (spectrum * damping).astype(jnp.bfloat16)
    back = lax.dot_general(transform, scaled, (((0,), (0,)), ((), ())), preferred_element_type=jnp.float32)
    return back.astype(jnp.bfloat16)


def latitudinal_wide(coeffs, matrix, damping):
    devices, lines, rows, width = coeffs.shape
    modes, degrees, lats = matrix.shape

    def body(x_ref, matrix_ref, damping_ref, out_ref):
        for span in lane_spans(width):
            by_coeff = jnp.swapaxes(x_ref[:, :, :, span].reshape(lats, rows, -1), 0, 1)
            results = [
                damp(matrix_ref[wavenumber_at(row)], by_coeff[row], damping_ref[:, span]) for row in range(rows)
            ]
            out_ref[:, :, :, span] = jnp.swapaxes(jnp.stack(results), 0, 1).reshape(devices, lines, rows, -1)

    return pl.pallas_call(
        body,
        grid=(1,),
        in_specs=[whole(coeffs), whole(matrix), pl.BlockSpec((degrees, width), lambda i: (0, 0))],
        out_specs=whole(coeffs),
        out_shape=jax.ShapeDtypeStruct(coeffs.shape, jnp.bfloat16),
        compiler_params=compiler_params(),
        cost_estimate=cost(4 * rows * degrees * lats * width, coeffs, coeffs, matrix),
        name="latitudinal_wide",
    )(coeffs, matrix, damping)


def whole(x):
    return pl.BlockSpec(x.shape, lambda *_: (0,) * len(x.shape))


def to_plane(parts, place):
    lines, plane, rows, width = parts[0].shape
    sections = len(parts)
    out = jax.ShapeDtypeStruct((sections, lines, rows, width), jnp.bfloat16)

    def body(place_ref, *refs):
        for p, out_ref in enumerate(refs[sections:]):
            for o in range(sections):
                for a in range(lines):
                    out_ref[o, a] = refs[o][a, place_ref[0] ^ p]

    return pl.pallas_call(
        body,
        grid=(1,),
        in_specs=[pl.BlockSpec(memory_space=pltpu.SMEM)] + [whole(parts[0])] * sections,
        out_specs=[whole(out)] * plane,
        out_shape=[out] * plane,
        compiler_params=compiler_params(),
        cost_estimate=cost(0, *parts, *parts),
        name="to_plane",
    )(place, *parts)


def from_plane(parts, place):
    sections, lines, rows, width = parts[0].shape
    plane = len(parts)
    out = jax.ShapeDtypeStruct((lines, plane, rows, width), jnp.bfloat16)

    def body(place_ref, *refs):
        for o, out_ref in enumerate(refs[plane:]):
            for p in range(plane):
                for a in range(lines):
                    out_ref[a, place_ref[0] ^ p] = refs[p][o, a]

    return pl.pallas_call(
        body,
        grid=(1,),
        in_specs=[pl.BlockSpec(memory_space=pltpu.SMEM)] + [whole(parts[0])] * plane,
        out_specs=[whole(out)] * sections,
        out_shape=[out] * sections,
        compiler_params=compiler_params(),
        cost_estimate=cost(0, *parts, *parts),
        name="from_plane",
    )(place, *parts)


def latitudinal_slim(parts, matrix, damping, start):
    sections, lines, rows, width = parts[0].shape
    plane = len(parts)
    degrees = damping.shape[0]
    own = sections * lines
    out = jax.ShapeDtypeStruct(parts[0].shape, jnp.bfloat16)

    def body(matrix_ref, damping_ref, *refs):
        latitudes = jnp.concatenate([ref[...].reshape(own, rows, width) for ref in refs[:plane]], axis=0)
        by_coeff = jnp.swapaxes(latitudes, 0, 1)
        results = [
            damp(matrix_ref[wavenumber_at(row)], by_coeff[row], damping_ref[...]) for row in range(rows)
        ]
        by_lat = jnp.swapaxes(jnp.stack(results), 0, 1)
        for p, out_ref in enumerate(refs[plane:]):
            out_ref[...] = by_lat[p * own : (p + 1) * own].reshape(out_ref.shape)

    return pl.pallas_call(
        body,
        grid=(1,),
        in_specs=[
            whole(matrix),
            pl.BlockSpec((degrees, width), lambda i: (0, start // width)),
        ]
        + [whole(out)] * plane,
        out_specs=[whole(out)] * plane,
        out_shape=[out] * plane,
        compiler_params=compiler_params(),
        cost_estimate=pl.CostEstimate(flops=10**11, bytes_accessed=3 * 10**8, transcendentals=0),
        name="latitudinal_slim",
    )(matrix, damping, *parts)


def advance(air, rebuilt, sea, warmth):
    warmed = lax.dot_general(sea, warmth, (((0,), (0,)), ((), ())), preferred_element_type=jnp.float32)
    return (air.astype(jnp.float32) + rebuilt + warmed).astype(jnp.bfloat16)


def three_parts(values):
    parts, rest = [], values
    for _ in range(3):
        parts.append(lax.reduce_precision(rest, 8, 7))
        rest = rest - parts[-1]
    parts += [jnp.zeros_like(values)] * (GROUP - 3)
    return jnp.stack(parts).astype(jnp.bfloat16)


def synthesise_slim(parts, table, air, sea, warmth, start, sec):
    lines, plane, rows, width = parts[0].shape
    sections = len(parts)
    half = air.shape[2]

    def body(sec_ref, table_ref, air_ref, sea_ref, warmth_ref, *refs):
        part_refs, out_ref, gathered = refs[:sections], refs[-2], refs[-1]
        for o, part_ref in enumerate(part_refs):
            for a in range(lines):
                for odd in range(2):
                    gathered[odd, sec_ref[0] ^ o, :, :, a * width : (a + 1) * width] = part_ref[
                        a, :, odd * GROUP : (odd + 1) * GROUP, :
                    ]
        even, odd = (
            jnp.dot(
                table_ref[odd],
                gathered[odd].reshape(sections * plane * GROUP, lines * width),
                preferred_element_type=jnp.float32,
            )
            for odd in range(2)
        )
        for at, rebuilt in enumerate((even + odd, even - odd)):
            for a in range(lines):
                out_ref[a, at] = advance(
                    air_ref[a, at], rebuilt[:, a * width : (a + 1) * width], sea_ref[a, at], warmth_ref[...]
                )

    return pl.pallas_call(
        body,
        grid=(1,),
        in_specs=[
            pl.BlockSpec(memory_space=pltpu.SMEM),
            pl.BlockSpec(table.shape, lambda i: (0, 0, 0)),
            pl.BlockSpec((lines, 2, half, width), lambda i: (0, 0, 0, start // width)),
            whole(sea),
            pl.BlockSpec((GROUP, width), lambda i: (0, start // width)),
        ]
        + [pl.BlockSpec(parts[0].shape, lambda i: (0, 0, 0, 0))] * sections,
        out_specs=pl.BlockSpec((lines, 2, half, width), lambda i: (0, 0, 0, start // width)),
        out_shape=jax.ShapeDtypeStruct(air.shape, jnp.bfloat16),
        scratch_shapes=[pltpu.VMEM((2, sections, plane, GROUP, lines * width), jnp.bfloat16)],
        compiler_params=compiler_params(),
        cost_estimate=pl.CostEstimate(flops=10**11, bytes_accessed=3 * 10**8, transcendentals=0),
        name="synthesise_slim",
    )(sec, table, air, sea, warmth, *parts)


def synthesise_wide(coeffs, table, air, sea, warmth, begun):
    groups, lines, rows, width = coeffs.shape
    half = air.shape[2]

    def body(table_ref, coeff_ref, air_ref, sea_ref, warmth_ref, begun_ref, out_ref):
        for span in lane_spans(width):
            even, odd = (
                jnp.dot(
                    table_ref[odd],
                    coeff_ref[:, 0, odd * GROUP : (odd + 1) * GROUP, span].reshape(groups * GROUP, -1),
                    preferred_element_type=jnp.float32,
                )
                for odd in range(2)
            )
            for at, rebuilt in enumerate((even + odd, even - odd)):
                out_ref[0, at, :, span] = advance(
                    air_ref[0, at, :, span], rebuilt, sea_ref[0, at], warmth_ref[:, span]
                )

    return pl.pallas_call(
        body,
        grid=(lines,),
        in_specs=[
            pl.BlockSpec(table.shape, lambda a: (0, 0, 0)),
            pl.BlockSpec((groups, 1, rows, width), lambda a: (0, a, 0, 0)),
            pl.BlockSpec((1, 2, half, width), lambda a: (a, 0, 0, 0)),
            pl.BlockSpec((1, 2, GROUP, half), lambda a: (a, 0, 0, 0)),
            pl.BlockSpec((GROUP, width), lambda a: (0, 0)),
            pl.BlockSpec(memory_space=pl.ANY),
        ],
        out_specs=pl.BlockSpec((1, 2, half, width), lambda a: (a, 0, 0, 0)),
        out_shape=jax.ShapeDtypeStruct(air.shape, jnp.bfloat16),
        input_output_aliases={5: 0},
        compiler_params=compiler_params(),
        cost_estimate=cost(4 * lines * half * half * width, table, coeffs, coeffs, coeffs),
        name="synthesise_wide",
    )(table, coeffs, air, sea, warmth, begun)


def gather_flux(air, projector):
    flux_local = jnp.einsum(
        "anc,cf->fan",
        air,
        projector,
        preferred_element_type=jnp.float32,
    ).astype(jnp.bfloat16)
    return lax.all_gather(flux_local, "band", axis=1, tiled=True)


def shards(
    air_field_lattice,
    associated_polynomial_matrix,
    harmonic_damping_factor,
    boundary_exchange_projector,
    warmth_response_factor,
    water_patch_fields,
    kernel_coefficients,
    local_exchange_matrix,
    patch_average_matrix,
    water_kernel_offset,
    water_readout_matrix,
    patch_holder_index,
    water_point_indicator,
    water_point_totals,
):
    parallel_lines, meridian_number, channel_count = air_field_lattice.shape
    sec_count = lax.axis_size("sec")
    band_count = lax.axis_size("band")
    core_count = lax.axis_size("ch")
    device_count = sec_count * band_count * core_count
    total_cols = 2 * K
    per_device = total_cols // device_count
    slot_count = water_patch_fields.shape[0]
    mode_count = associated_polynomial_matrix.shape[0]
    lat_count = associated_polynomial_matrix.shape[1]
    wide = channel_count - SLIM
    in_kernels = (
        per_device == 2 * GROUP
        and wide > 0
        and wide % SLIM == 0
        and sec_count & (sec_count - 1) == 0
        and lat_count == device_count * parallel_lines
    )
    if in_kernels:
        plane = band_count * core_count
        sec_id = lax.axis_index("sec")
        sec = sec_id.reshape(1).astype(jnp.int32)
        forward, backward = map(jnp.asarray, transform_tables(meridian_number, device_count))
        hops = [[(i, i ^ o) for i in range(sec_count)] for o in range(sec_count)]

        twists = [[(i, i ^ p) for i in range(plane)] for p in range(plane)]
        place = (lax.axis_index("band") * core_count + lax.axis_index("ch")).astype(jnp.int32)

        def over_sections(blocks):
            return [lax.ppermute(x, "sec", hops[o]) if o else x for o, x in enumerate(blocks)]

        def over_plane(blocks):
            return [lax.ppermute(x, ("band", "ch"), twists[p]) if p else x for p, x in enumerate(blocks)]

        slim = analyse_slim(air_field_lattice, forward, wide, sec, sec_count, device_count)
        air_after, *slim = lax.optimization_barrier((air_field_lattice, *slim))
        slim = over_sections(slim)
        wide_coeffs = analyse_wide(air_after, forward, wide, device_count)
        wide_coeffs = lax.all_to_all(wide_coeffs, AXES, split_axis=0, concat_axis=0, tiled=True)
        slim = to_plane(slim, place.reshape(1))
        air_after, matrix_after, *slim = lax.optimization_barrier(
            (air_field_lattice, associated_polynomial_matrix, *slim)
        )
        slim = over_plane(slim)

        at_lat = jnp.arange(lat_count, dtype=jnp.int32)
        sections_at = at_lat // parallel_lines % sec_count ^ sec_id
        places_at = at_lat // (parallel_lines * sec_count) ^ place
        order = (sections_at * plane + places_at) * parallel_lines + at_lat % parallel_lines
        shuffle = (at_lat[:, None] == order[None, :]).astype(jnp.bfloat16)
        shuffled = jnp.einsum(
            "mlt,tu->mlu", matrix_after, shuffle, preferred_element_type=jnp.float32
        ).astype(jnp.bfloat16)

        gathered = gather_flux(air_after, boundary_exchange_projector)
        gathered, *slim = lax.optimization_barrier((gathered, *slim))
        slim = latitudinal_slim(slim, shuffled, harmonic_damping_factor, wide)
        slim = from_plane(over_plane(slim), place.reshape(1))
        wide_coeffs, *slim = lax.optimization_barrier((wide_coeffs, *slim))
        slim = over_sections(slim)
        wide_coeffs = latitudinal_wide(wide_coeffs, associated_polynomial_matrix, harmonic_damping_factor)
        wide_coeffs = lax.all_to_all(wide_coeffs, AXES, split_axis=0, concat_axis=0, tiled=True)
        water_patch_fields, gathered, warmth_response_factor, patch_holder_index, *slim = lax.optimization_barrier(
            (water_patch_fields, gathered, warmth_response_factor, patch_holder_index, *slim)
        )
    else:
        gathered = gather_flux(air_field_lattice, boundary_exchange_projector)
        table = dft_table(meridian_number)
        forward = jnp.asarray(np.ascontiguousarray(table.T))
        backward = jnp.asarray((table.astype(np.float32) * (2.0 / meridian_number)).astype(jnp.bfloat16))
        fourier = jnp.einsum(
            "qn,anc->aqc", forward, air_field_lattice, preferred_element_type=jnp.float32
        ).astype(jnp.bfloat16)
        collected = lax.all_to_all(fourier, AXES, split_axis=1, concat_axis=0, tiled=True)
        pairs = collected.reshape(lat_count, mode_count, 2, channel_count)
        spectrum = jnp.einsum(
            "mlt,tmpc->mlpc", associated_polynomial_matrix, pairs, preferred_element_type=jnp.float32
        )
        scaled = (spectrum * harmonic_damping_factor[None, :, None]).astype(jnp.bfloat16)
        damped = jnp.einsum(
            "mlt,mlpc->tmpc", associated_polynomial_matrix, scaled, preferred_element_type=jnp.float32
        ).astype(jnp.bfloat16).reshape(lat_count, per_device, channel_count)
        returned = lax.all_to_all(damped, AXES, split_axis=0, concat_axis=1, tiled=True)

    sec_id = lax.axis_index("sec")
    band_id = lax.axis_index("band")
    core_id = lax.axis_index("ch")
    owner_grid = patch_holder_index.reshape(sec_count, band_count, core_count, -1)
    tiles_per_row = owner_grid.shape[3]
    owner_group = lax.dynamic_index_in_dim(owner_grid, sec_id, 0, keepdims=False)
    owner_group = lax.dynamic_index_in_dim(owner_group, core_id, 1, keepdims=False)
    owner_flat = owner_group.reshape(-1)
    holders = jnp.arange(band_count, dtype=jnp.int32)
    mine_all = owner_flat[None, :] == holders[:, None]
    rank_all = jnp.cumsum(mine_all.astype(jnp.int32), axis=1) - 1
    slot_index = jnp.arange(slot_count, dtype=jnp.int32)
    pick_all = mine_all[:, None, :] & (rank_all[:, None, :] == slot_index[None, :, None])
    my_pick = lax.dynamic_index_in_dim(pick_all, band_id, 0, keepdims=False)
    flux_count = gathered.shape[0]
    tile_width = meridian_number // tiles_per_row
    pieces = gathered.reshape(flux_count, band_count, parallel_lines, tiles_per_row, tile_width)
    chooser = my_pick.reshape(slot_count, band_count, tiles_per_row).astype(jnp.bfloat16)
    tile_flux = jnp.einsum(
        "sbj,fbrjw->sfrw", chooser, pieces, preferred_element_type=jnp.float32
    ).astype(jnp.bfloat16)
    ocean_next = ocean_update(
        water_patch_fields,
        tile_flux,
        water_point_indicator,
        water_point_totals,
        kernel_coefficients,
        local_exchange_matrix,
        patch_average_matrix,
        water_kernel_offset,
        water_readout_matrix,
    )
    sea_slots = ocean_next[:, 0]
    sea_all = lax.all_gather(sea_slots, "band", axis=0, tiled=True)
    rank_tile = jnp.sum(jnp.where(mine_all, rank_all, 0), axis=0)
    my_owners = lax.dynamic_index_in_dim(owner_group, band_id, 0, keepdims=False)
    my_ranks = lax.dynamic_slice_in_dim(rank_tile, band_id * tiles_per_row, tiles_per_row)
    target = my_owners * slot_count + my_ranks
    selector = (
        target[:, None] == jnp.arange(band_count * slot_count, dtype=jnp.int32)[None, :]
    ).astype(jnp.bfloat16)
    water_patches = jnp.einsum(
        "jk,krw->rjw", selector, sea_all, preferred_element_type=jnp.float32
    ).astype(jnp.bfloat16)
    water_skin_warmth = water_patches.reshape(parallel_lines, meridian_number)
    if in_kernels:
        halves = (parallel_lines, 2, meridian_number // 2, -1)
        air = air_field_lattice.reshape(halves)
        sea = water_skin_warmth.reshape(parallel_lines, 2, 1, meridian_number // 2)
        sea = jnp.broadcast_to(sea, (parallel_lines, 2, GROUP, meridian_number // 2))
        warmth = three_parts(warmth_response_factor)
        begun = synthesise_slim(slim, backward, air, sea, warmth, wide, sec)
        advanced = synthesise_wide(wide_coeffs, backward, air, sea, warmth, begun)
        advanced = advanced.reshape(air_field_lattice.shape)
    else:
        rebuilt = jnp.einsum("nq,aqc->anc", backward, returned, preferred_element_type=jnp.float32)
        advanced = (
            air_field_lattice.astype(jnp.float32)
            + rebuilt
            + water_skin_warmth.astype(jnp.float32)[:, :, None] * warmth_response_factor[None, None]
        ).astype(jnp.bfloat16)
    return (advanced, ocean_next)


def solution(mesh):
    placed = (
        P(("sec", "band", "ch"), None, None),
        P(("sec", "band", "ch"), None, None),
        P(),
        P(),
        P(),
        P(("sec", "band", "ch"), None, None, None),
        P(),
        P(),
        P(),
        P(),
        P(),
        P(),
        P(("sec", "band", "ch"), None, None),
        P(("sec", "band", "ch")),
    )
    return jax.shard_map(
        shards,
        mesh=mesh,
        in_specs=placed,
        out_specs=(
            P(("sec", "band", "ch"), None, None),
            P(("sec", "band", "ch"), None, None, None),
        ),
        check_vma=False,
    )
```

```python
import functools
import math

import jax
import jax.numpy as jnp
import numpy as np
from jax import lax
from jax.experimental import pallas as pl
from jax.experimental.pallas import tpu as pltpu
from jax.sharding import PartitionSpec as P

K = 512
AXES = ("sec", "band", "ch")
GROUP = 16
SLIM = 128
MIB = 1024 * 1024


@functools.lru_cache(maxsize=None)
def dft_table(meridian_number):
    cell_index = np.arange(meridian_number, dtype=np.int64)[:, None]
    column = np.arange(2 * K, dtype=np.int64)[None, :]
    phase_angle = (cell_index * (column // 2) % meridian_number) * (2.0 * math.pi / meridian_number)
    table = np.where(column % 2 == 0, np.cos(phase_angle), -np.sin(phase_angle))
    return table.astype(np.float32).astype(jnp.bfloat16)


@functools.lru_cache(maxsize=None)
def transform_tables(meridian_number, groups):
    half = meridian_number // 2
    table = dft_table(meridian_number).astype(np.float32)
    by_parity = table.reshape(meridian_number, groups, -1, 2, 2).transpose(1, 3, 2, 4, 0)
    forward = by_parity.reshape(-1, meridian_number)
    backward = by_parity.transpose(1, 4, 0, 2, 3)[:, :half].reshape(2, half, -1) * (2.0 / meridian_number)
    return tuple(np.ascontiguousarray(x).astype(jnp.bfloat16) for x in (forward, backward))


def ocean_update(
    state,
    tile_flux,
    mask_tile,
    count_tile,
    kernel_coefficients,
    local_exchange_matrix,
    patch_average_matrix,
    water_kernel_offset,
    water_readout_matrix,
):
    parallel_lines = mask_tile.shape[1]
    tile_width = mask_tile.shape[2]
    mask_f = mask_tile.astype(jnp.float32)
    masked = tile_flux * mask_tile[:, None].astype(jnp.bfloat16)
    fmean = (
        jnp.sum(masked.astype(jnp.float32), axis=(2, 3))
        / jnp.maximum(count_tile.astype(jnp.float32), 1.0)[:, None]
    )
    total = jnp.einsum(
        "fo,sfrw->sorw", local_exchange_matrix, masked, preferred_element_type=jnp.float32
    )
    for shift_row in range(3):
        for shift_col in range(3):
            window = state[
                :, :, shift_row : shift_row + parallel_lines, shift_col : shift_col + tile_width
            ]
            total = total + jnp.einsum(
                "io,sirw->sorw",
                kernel_coefficients[shift_row, shift_col],
                window,
                preferred_element_type=jnp.float32,
            )
    mean_term = jnp.sum(fmean[:, :, None] * patch_average_matrix[None], axis=1)
    total = total + mean_term[:, :, None, None] + water_kernel_offset[None, :, None, None]
    hidden = jax.nn.gelu(total, approximate=True).astype(jnp.bfloat16)
    update = jnp.einsum(
        "io,sirw->sorw", water_readout_matrix, hidden, preferred_element_type=jnp.float32
    )
    fresh = (
        state[:, :, 1 : 1 + parallel_lines, 1 : 1 + tile_width].astype(jnp.float32) + update
    ) * mask_f[:, None]
    return fresh.astype(jnp.bfloat16)


def compiler_params(mib=60):
    return pltpu.CompilerParams(vmem_limit_bytes=mib * MIB)


def cost(flops, *arrays):
    return pl.CostEstimate(
        flops=flops, bytes_accessed=sum(x.size * x.dtype.itemsize for x in arrays), transcendentals=0
    )


def lane_spans(width, size=256):
    return [slice(at, min(at + size, width)) for at in range(0, width, size)]


def analyse_wide(air, table, width, groups):
    lines, cells, _ = air.shape
    rows = table.shape[0] // groups
    out = jax.ShapeDtypeStruct((groups, lines, rows, width), jnp.bfloat16)

    def body(table_ref, air_ref, out_ref):
        for span in lane_spans(width):
            coeffs = jnp.dot(table_ref[...], air_ref[0, :, span], preferred_element_type=jnp.float32)
            out_ref[:, :, :, span] = coeffs.astype(jnp.bfloat16).reshape(groups, 1, rows, -1)

    return pl.pallas_call(
        body,
        grid=(lines,),
        in_specs=[
            pl.BlockSpec(table.shape, lambda a: (0, 0)),
            pl.BlockSpec((1, cells, width), lambda a: (a, 0, 0)),
        ],
        out_specs=pl.BlockSpec((groups, 1, rows, width), lambda a: (0, a, 0, 0)),
        out_shape=out,
        compiler_params=compiler_params(),
        cost_estimate=cost(2 * lines * table.size * width, table, air, out),
        name="analyse_wide",
    )(table, air)


def analyse_slim(air, table, start, sec, sections, groups):
    lines, cells, channels = air.shape
    width = channels - start
    plane = groups // sections
    rows = table.shape[0] // groups
    size = plane * rows
    out = jax.ShapeDtypeStruct((lines, plane, rows, width), jnp.bfloat16)

    def body(sec_ref, table_ref, air_ref, *outs):
        both = jnp.concatenate([air_ref[a] for a in range(lines)], axis=1)
        for o, out_ref in enumerate(outs):
            part = pl.ds(pl.multiple_of((sec_ref[0] ^ o) * size, size), size)
            coeffs = jnp.dot(table_ref[part, :], both, preferred_element_type=jnp.float32).astype(jnp.bfloat16)
            for a in range(lines):
                out_ref[a] = coeffs[:, a * width : (a + 1) * width].reshape(plane, rows, width)

    return pl.pallas_call(
        body,
        grid=(1,),
        in_specs=[
            pl.BlockSpec(memory_space=pltpu.SMEM),
            pl.BlockSpec(table.shape, lambda i: (0, 0)),
            pl.BlockSpec((lines, cells, width), lambda i: (0, 0, start // width)),
        ],
        out_specs=[pl.BlockSpec(out.shape, lambda i: (0, 0, 0, 0))] * sections,
        out_shape=[out] * sections,
        compiler_params=compiler_params(),
        cost_estimate=cost(2 * lines * table.size * width, table, *[out] * 2 * sections),
        name="analyse_slim",
    )(sec, table, air)


def wavenumber_at(row):
    return row % GROUP // 2 * 2 + row // GROUP


def damp(transform, coeffs, damping):
    spectrum = jnp.dot(transform, coeffs, preferred_element_type=jnp.float32)
    scaled = (spectrum * damping).astype(jnp.bfloat16)
    back = lax.dot_general(transform, scaled, (((0,), (0,)), ((), ())), preferred_element_type=jnp.float32)
    return back.astype(jnp.bfloat16)


def latitudinal_wide(coeffs, matrix, damping):
    devices, lines, rows, width = coeffs.shape
    modes, degrees, lats = matrix.shape

    def body(x_ref, matrix_ref, damping_ref, out_ref):
        parity = pl.program_id(0)
        for span in lane_spans(width):
            by_coeff = jnp.swapaxes(x_ref[:, :, :, span].reshape(lats, GROUP, -1), 0, 1)
            results = [
                damp(matrix_ref[wavenumber_at(row) + parity], by_coeff[row], damping_ref[:, span])
                for row in range(GROUP)
            ]
            out_ref[:, :, :, span] = jnp.swapaxes(jnp.stack(results), 0, 1).reshape(devices, lines, GROUP, -1)

    half_rows = pl.BlockSpec((devices, lines, GROUP, width), lambda p: (0, 0, p, 0))
    return pl.pallas_call(
        body,
        grid=(rows // GROUP,),
        in_specs=[half_rows, whole(matrix), pl.BlockSpec((degrees, width), lambda p: (0, 0))],
        out_specs=half_rows,
        out_shape=jax.ShapeDtypeStruct(coeffs.shape, jnp.bfloat16),
        compiler_params=compiler_params(),
        cost_estimate=cost(4 * rows * degrees * lats * width, coeffs, coeffs, matrix),
        name="latitudinal_wide",
    )(coeffs, matrix, damping)


def whole(x):
    return pl.BlockSpec(x.shape, lambda *_: (0,) * len(x.shape))


def to_plane(parts, place):
    lines, plane, rows, width = parts[0].shape
    sections = len(parts)
    out = jax.ShapeDtypeStruct((sections, lines, rows, width), jnp.bfloat16)

    def body(place_ref, *refs):
        for p, out_ref in enumerate(refs[sections:]):
            for o in range(sections):
                for a in range(lines):
                    out_ref[o, a] = refs[o][a, place_ref[0] ^ p]

    return pl.pallas_call(
        body,
        grid=(1,),
        in_specs=[pl.BlockSpec(memory_space=pltpu.SMEM)] + [whole(parts[0])] * sections,
        out_specs=[whole(out)] * plane,
        out_shape=[out] * plane,
        compiler_params=compiler_params(),
        cost_estimate=cost(0, *parts, *parts),
        name="to_plane",
    )(place, *parts)


def from_plane(parts, place):
    sections, lines, rows, width = parts[0].shape
    plane = len(parts)
    out = jax.ShapeDtypeStruct((lines, plane, rows, width), jnp.bfloat16)

    def body(place_ref, *refs):
        for o, out_ref in enumerate(refs[plane:]):
            for p in range(plane):
                for a in range(lines):
                    out_ref[a, place_ref[0] ^ p] = refs[p][o, a]

    return pl.pallas_call(
        body,
        grid=(1,),
        in_specs=[pl.BlockSpec(memory_space=pltpu.SMEM)] + [whole(parts[0])] * plane,
        out_specs=[whole(out)] * sections,
        out_shape=[out] * sections,
        compiler_params=compiler_params(),
        cost_estimate=cost(0, *parts, *parts),
        name="from_plane",
    )(place, *parts)


def latitudinal_slim(parts, matrix, damping, start):
    sections, lines, rows, width = parts[0].shape
    plane = len(parts)
    degrees = damping.shape[0]
    own = sections * lines
    out = jax.ShapeDtypeStruct(parts[0].shape, jnp.bfloat16)

    def body(matrix_ref, damping_ref, *refs):
        latitudes = jnp.concatenate([ref[...].reshape(own, rows, width) for ref in refs[:plane]], axis=0)
        by_coeff = jnp.swapaxes(latitudes, 0, 1)
        results = [
            damp(matrix_ref[wavenumber_at(row)], by_coeff[row], damping_ref[...]) for row in range(rows)
        ]
        by_lat = jnp.swapaxes(jnp.stack(results), 0, 1)
        for p, out_ref in enumerate(refs[plane:]):
            out_ref[...] = by_lat[p * own : (p + 1) * own].reshape(out_ref.shape)

    return pl.pallas_call(
        body,
        grid=(1,),
        in_specs=[
            whole(matrix),
            pl.BlockSpec((degrees, width), lambda i: (0, start // width)),
        ]
        + [whole(out)] * plane,
        out_specs=[whole(out)] * plane,
        out_shape=[out] * plane,
        compiler_params=compiler_params(),
        cost_estimate=pl.CostEstimate(flops=10**11, bytes_accessed=3 * 10**8, transcendentals=0),
        name="latitudinal_slim",
    )(matrix, damping, *parts)


def advance(air, rebuilt, sea, warmth):
    warmed = lax.dot_general(sea, warmth, (((0,), (0,)), ((), ())), preferred_element_type=jnp.float32)
    return (air.astype(jnp.float32) + rebuilt + warmed).astype(jnp.bfloat16)


def three_parts(values):
    parts, rest = [], values
    for _ in range(3):
        parts.append(lax.reduce_precision(rest, 8, 7))
        rest = rest - parts[-1]
    parts += [jnp.zeros_like(values)] * (GROUP - 3)
    return jnp.stack(parts).astype(jnp.bfloat16)


def synthesise_slim(parts, table, air, sea, warmth, start, sec):
    lines, plane, rows, width = parts[0].shape
    sections = len(parts)
    half = air.shape[2]

    def body(sec_ref, table_ref, air_ref, sea_ref, warmth_ref, *refs):
        part_refs, out_ref, gathered = refs[:sections], refs[-2], refs[-1]
        for o, part_ref in enumerate(part_refs):
            for a in range(lines):
                for odd in range(2):
                    gathered[odd, sec_ref[0] ^ o, :, :, a * width : (a + 1) * width] = part_ref[
                        a, :, odd * GROUP : (odd + 1) * GROUP, :
                    ]
        even, odd = (
            jnp.dot(
                table_ref[odd],
                gathered[odd].reshape(sections * plane * GROUP, lines * width),
                preferred_element_type=jnp.float32,
            )
            for odd in range(2)
        )
        for at, rebuilt in enumerate((even + odd, even - odd)):
            for a in range(lines):
                out_ref[a, at] = advance(
                    air_ref[a, at], rebuilt[:, a * width : (a + 1) * width], sea_ref[a, at], warmth_ref[...]
                )

    return pl.pallas_call(
        body,
        grid=(1,),
        in_specs=[
            pl.BlockSpec(memory_space=pltpu.SMEM),
            pl.BlockSpec(table.shape, lambda i: (0, 0, 0)),
            pl.BlockSpec((lines, 2, half, width), lambda i: (0, 0, 0, start // width)),
            whole(sea),
            pl.BlockSpec((GROUP, width), lambda i: (0, start // width)),
        ]
        + [pl.BlockSpec(parts[0].shape, lambda i: (0, 0, 0, 0))] * sections,
        out_specs=pl.BlockSpec((lines, 2, half, width), lambda i: (0, 0, 0, start // width)),
        out_shape=jax.ShapeDtypeStruct(air.shape, jnp.bfloat16),
        scratch_shapes=[pltpu.VMEM((2, sections, plane, GROUP, lines * width), jnp.bfloat16)],
        compiler_params=compiler_params(),
        cost_estimate=pl.CostEstimate(flops=10**11, bytes_accessed=3 * 10**8, transcendentals=0),
        name="synthesise_slim",
    )(sec, table, air, sea, warmth, *parts)


def synthesise_wide(coeffs, table, air, sea, warmth, begun):
    groups, lines, rows, width = coeffs.shape
    half = air.shape[2]

    def body(table_ref, coeff_ref, air_ref, sea_ref, warmth_ref, begun_ref, out_ref):
        for span in lane_spans(width):
            even, odd = (
                jnp.dot(
                    table_ref[odd],
                    coeff_ref[:, 0, odd * GROUP : (odd + 1) * GROUP, span].reshape(groups * GROUP, -1),
                    preferred_element_type=jnp.float32,
                )
                for odd in range(2)
            )
            for at, rebuilt in enumerate((even + odd, even - odd)):
                out_ref[0, at, :, span] = advance(
                    air_ref[0, at, :, span], rebuilt, sea_ref[0, at], warmth_ref[:, span]
                )

    return pl.pallas_call(
        body,
        grid=(lines,),
        in_specs=[
            pl.BlockSpec(table.shape, lambda a: (0, 0, 0)),
            pl.BlockSpec((groups, 1, rows, width), lambda a: (0, a, 0, 0)),
            pl.BlockSpec((1, 2, half, width), lambda a: (a, 0, 0, 0)),
            pl.BlockSpec((1, 2, GROUP, half), lambda a: (a, 0, 0, 0)),
            pl.BlockSpec((GROUP, width), lambda a: (0, 0)),
            pl.BlockSpec(memory_space=pl.ANY),
        ],
        out_specs=pl.BlockSpec((1, 2, half, width), lambda a: (a, 0, 0, 0)),
        out_shape=jax.ShapeDtypeStruct(air.shape, jnp.bfloat16),
        input_output_aliases={5: 0},
        compiler_params=compiler_params(),
        cost_estimate=cost(4 * lines * half * half * width, table, coeffs, coeffs, coeffs),
        name="synthesise_wide",
    )(table, coeffs, air, sea, warmth, begun)


def gather_flux(air, projector):
    flux_local = jnp.einsum(
        "anc,cf->fan",
        air,
        projector,
        preferred_element_type=jnp.float32,
    ).astype(jnp.bfloat16)
    return lax.all_gather(flux_local, "band", axis=1, tiled=True)


def shards(
    air_field_lattice,
    associated_polynomial_matrix,
    harmonic_damping_factor,
    boundary_exchange_projector,
    warmth_response_factor,
    water_patch_fields,
    kernel_coefficients,
    local_exchange_matrix,
    patch_average_matrix,
    water_kernel_offset,
    water_readout_matrix,
    patch_holder_index,
    water_point_indicator,
    water_point_totals,
):
    parallel_lines, meridian_number, channel_count = air_field_lattice.shape
    sec_count = lax.axis_size("sec")
    band_count = lax.axis_size("band")
    core_count = lax.axis_size("ch")
    device_count = sec_count * band_count * core_count
    total_cols = 2 * K
    per_device = total_cols // device_count
    slot_count = water_patch_fields.shape[0]
    mode_count = associated_polynomial_matrix.shape[0]
    lat_count = associated_polynomial_matrix.shape[1]
    wide = channel_count - SLIM
    in_kernels = (
        per_device == 2 * GROUP
        and wide > 0
        and wide % SLIM == 0
        and sec_count & (sec_count - 1) == 0
        and lat_count == device_count * parallel_lines
    )
    if in_kernels:
        plane = band_count * core_count
        sec_id = lax.axis_index("sec")
        sec = sec_id.reshape(1).astype(jnp.int32)
        forward, backward = map(jnp.asarray, transform_tables(meridian_number, device_count))
        hops = [[(i, i ^ o) for i in range(sec_count)] for o in range(sec_count)]

        twists = [[(i, i ^ p) for i in range(plane)] for p in range(plane)]
        place = (lax.axis_index("band") * core_count + lax.axis_index("ch")).astype(jnp.int32)

        def over_sections(blocks):
            return [lax.ppermute(x, "sec", hops[o]) if o else x for o, x in enumerate(blocks)]

        def over_plane(blocks):
            return [lax.ppermute(x, ("band", "ch"), twists[p]) if p else x for p, x in enumerate(blocks)]

        slim = analyse_slim(air_field_lattice, forward, wide, sec, sec_count, device_count)
        air_after, *slim = lax.optimization_barrier((air_field_lattice, *slim))
        slim = over_sections(slim)
        wide_coeffs = analyse_wide(air_after, forward, wide, device_count)
        wide_coeffs = lax.all_to_all(wide_coeffs, AXES, split_axis=0, concat_axis=0, tiled=True)
        slim = to_plane(slim, place.reshape(1))
        air_after, matrix_after, *slim = lax.optimization_barrier(
            (air_field_lattice, associated_polynomial_matrix, *slim)
        )
        slim = over_plane(slim)

        at_lat = jnp.arange(lat_count, dtype=jnp.int32)
        sections_at = at_lat // parallel_lines % sec_count ^ sec_id
        places_at = at_lat // (parallel_lines * sec_count) ^ place
        order = (sections_at * plane + places_at) * parallel_lines + at_lat % parallel_lines
        shuffle = (at_lat[:, None] == order[None, :]).astype(jnp.bfloat16)
        shuffled = jnp.einsum(
            "mlt,tu->mlu", matrix_after, shuffle, preferred_element_type=jnp.float32
        ).astype(jnp.bfloat16)

        gathered = gather_flux(air_after, boundary_exchange_projector)
        gathered, *slim = lax.optimization_barrier((gathered, *slim))
        slim = latitudinal_slim(slim, shuffled, harmonic_damping_factor, wide)
        slim = from_plane(over_plane(slim), place.reshape(1))
        wide_coeffs, *slim = lax.optimization_barrier((wide_coeffs, *slim))
        slim = over_sections(slim)
        wide_coeffs = latitudinal_wide(wide_coeffs, associated_polynomial_matrix, harmonic_damping_factor)
        wide_coeffs = lax.all_to_all(wide_coeffs, AXES, split_axis=0, concat_axis=0, tiled=True)
        water_patch_fields, gathered, warmth_response_factor, patch_holder_index, *slim = lax.optimization_barrier(
            (water_patch_fields, gathered, warmth_response_factor, patch_holder_index, *slim)
        )
    else:
        gathered = gather_flux(air_field_lattice, boundary_exchange_projector)
        table = dft_table(meridian_number)
        forward = jnp.asarray(np.ascontiguousarray(table.T))
        backward = jnp.asarray((table.astype(np.float32) * (2.0 / meridian_number)).astype(jnp.bfloat16))
        fourier = jnp.einsum(
            "qn,anc->aqc", forward, air_field_lattice, preferred_element_type=jnp.float32
        ).astype(jnp.bfloat16)
        collected = lax.all_to_all(fourier, AXES, split_axis=1, concat_axis=0, tiled=True)
        pairs = collected.reshape(lat_count, mode_count, 2, channel_count)
        spectrum = jnp.einsum(
            "mlt,tmpc->mlpc", associated_polynomial_matrix, pairs, preferred_element_type=jnp.float32
        )
        scaled = (spectrum * harmonic_damping_factor[None, :, None]).astype(jnp.bfloat16)
        damped = jnp.einsum(
            "mlt,mlpc->tmpc", associated_polynomial_matrix, scaled, preferred_element_type=jnp.float32
        ).astype(jnp.bfloat16).reshape(lat_count, per_device, channel_count)
        returned = lax.all_to_all(damped, AXES, split_axis=0, concat_axis=1, tiled=True)

    sec_id = lax.axis_index("sec")
    band_id = lax.axis_index("band")
    core_id = lax.axis_index("ch")
    owner_grid = patch_holder_index.reshape(sec_count, band_count, core_count, -1)
    tiles_per_row = owner_grid.shape[3]
    owner_group = lax.dynamic_index_in_dim(owner_grid, sec_id, 0, keepdims=False)
    owner_group = lax.dynamic_index_in_dim(owner_group, core_id, 1, keepdims=False)
    owner_flat = owner_group.reshape(-1)
    holders = jnp.arange(band_count, dtype=jnp.int32)
    mine_all = owner_flat[None, :] == holders[:, None]
    rank_all = jnp.cumsum(mine_all.astype(jnp.int32), axis=1) - 1
    slot_index = jnp.arange(slot_count, dtype=jnp.int32)
    pick_all = mine_all[:, None, :] & (rank_all[:, None, :] == slot_index[None, :, None])
    my_pick = lax.dynamic_index_in_dim(pick_all, band_id, 0, keepdims=False)
    flux_count = gathered.shape[0]
    tile_width = meridian_number // tiles_per_row
    pieces = gathered.reshape(flux_count, band_count, parallel_lines, tiles_per_row, tile_width)
    chooser = my_pick.reshape(slot_count, band_count, tiles_per_row).astype(jnp.bfloat16)
    tile_flux = jnp.einsum(
        "sbj,fbrjw->sfrw", chooser, pieces, preferred_element_type=jnp.float32
    ).astype(jnp.bfloat16)
    ocean_next = ocean_update(
        water_patch_fields,
        tile_flux,
        water_point_indicator,
        water_point_totals,
        kernel_coefficients,
        local_exchange_matrix,
        patch_average_matrix,
        water_kernel_offset,
        water_readout_matrix,
    )
    sea_slots = ocean_next[:, 0]
    sea_all = lax.all_gather(sea_slots, "band", axis=0, tiled=True)
    rank_tile = jnp.sum(jnp.where(mine_all, rank_all, 0), axis=0)
    my_owners = lax.dynamic_index_in_dim(owner_group, band_id, 0, keepdims=False)
    my_ranks = lax.dynamic_slice_in_dim(rank_tile, band_id * tiles_per_row, tiles_per_row)
    target = my_owners * slot_count + my_ranks
    selector = (
        target[:, None] == jnp.arange(band_count * slot_count, dtype=jnp.int32)[None, :]
    ).astype(jnp.bfloat16)
    water_patches = jnp.einsum(
        "jk,krw->rjw", selector, sea_all, preferred_element_type=jnp.float32
    ).astype(jnp.bfloat16)
    water_skin_warmth = water_patches.reshape(parallel_lines, meridian_number)
    if in_kernels:
        halves = (parallel_lines, 2, meridian_number // 2, -1)
        air = air_field_lattice.reshape(halves)
        sea = water_skin_warmth.reshape(parallel_lines, 2, 1, meridian_number // 2)
        sea = jnp.broadcast_to(sea, (parallel_lines, 2, GROUP, meridian_number // 2))
        warmth = three_parts(warmth_response_factor)
        begun = synthesise_slim(slim, backward, air, sea, warmth, wide, sec)
        advanced = synthesise_wide(wide_coeffs, backward, air, sea, warmth, begun)
        advanced = advanced.reshape(air_field_lattice.shape)
    else:
        rebuilt = jnp.einsum("nq,aqc->anc", backward, returned, preferred_element_type=jnp.float32)
        advanced = (
            air_field_lattice.astype(jnp.float32)
            + rebuilt
            + water_skin_warmth.astype(jnp.float32)[:, :, None] * warmth_response_factor[None, None]
        ).astype(jnp.bfloat16)
    return (advanced, ocean_next)


def solution(mesh):
    placed = (
        P(("sec", "band", "ch"), None, None),
        P(("sec", "band", "ch"), None, None),
        P(),
        P(),
        P(),
        P(("sec", "band", "ch"), None, None, None),
        P(),
        P(),
        P(),
        P(),
        P(),
        P(),
        P(("sec", "band", "ch"), None, None),
        P(("sec", "band", "ch")),
    )
    return jax.shard_map(
        shards,
        mesh=mesh,
        in_specs=placed,
        out_specs=(
            P(("sec", "band", "ch"), None, None),
            P(("sec", "band", "ch"), None, None, None),
        ),
        check_vma=False,
    )
```

```python
import functools
import math

import jax
import jax.numpy as jnp
import numpy as np
from jax import lax
from jax.experimental import pallas as pl
from jax.experimental.pallas import tpu as pltpu
from jax.sharding import PartitionSpec as P

K = 512
AXES = ("sec", "band", "ch")
GROUP = 16
SLIM = 128
MIB = 1024 * 1024


@functools.lru_cache(maxsize=None)
def dft_table(meridian_number):
    cell_index = np.arange(meridian_number, dtype=np.int64)[:, None]
    column = np.arange(2 * K, dtype=np.int64)[None, :]
    phase_angle = (cell_index * (column // 2) % meridian_number) * (2.0 * math.pi / meridian_number)
    table = np.where(column % 2 == 0, np.cos(phase_angle), -np.sin(phase_angle))
    return table.astype(np.float32).astype(jnp.bfloat16)


@functools.lru_cache(maxsize=None)
def transform_tables(meridian_number, groups):
    half = meridian_number // 2
    table = dft_table(meridian_number).astype(np.float32)
    by_parity = table.reshape(meridian_number, groups, -1, 2, 2).transpose(1, 3, 2, 4, 0)
    forward = by_parity.reshape(-1, meridian_number)
    backward = by_parity.transpose(1, 4, 0, 2, 3)[:, :half].reshape(2, half, -1) * (2.0 / meridian_number)
    return tuple(np.ascontiguousarray(x).astype(jnp.bfloat16) for x in (forward, backward))


def ocean_update(
    state,
    tile_flux,
    mask_tile,
    count_tile,
    kernel_coefficients,
    local_exchange_matrix,
    patch_average_matrix,
    water_kernel_offset,
    water_readout_matrix,
):
    parallel_lines = mask_tile.shape[1]
    tile_width = mask_tile.shape[2]
    mask_f = mask_tile.astype(jnp.float32)
    masked = tile_flux * mask_tile[:, None].astype(jnp.bfloat16)
    fmean = (
        jnp.sum(masked.astype(jnp.float32), axis=(2, 3))
        / jnp.maximum(count_tile.astype(jnp.float32), 1.0)[:, None]
    )
    total = jnp.einsum(
        "fo,sfrw->sorw", local_exchange_matrix, masked, preferred_element_type=jnp.float32
    )
    for shift_row in range(3):
        for shift_col in range(3):
            window = state[
                :, :, shift_row : shift_row + parallel_lines, shift_col : shift_col + tile_width
            ]
            total = total + jnp.einsum(
                "io,sirw->sorw",
                kernel_coefficients[shift_row, shift_col],
                window,
                preferred_element_type=jnp.float32,
            )
    mean_term = jnp.sum(fmean[:, :, None] * patch_average_matrix[None], axis=1)
    total = total + mean_term[:, :, None, None] + water_kernel_offset[None, :, None, None]
    hidden = jax.nn.gelu(total, approximate=True).astype(jnp.bfloat16)
    update = jnp.einsum(
        "io,sirw->sorw", water_readout_matrix, hidden, preferred_element_type=jnp.float32
    )
    fresh = (
        state[:, :, 1 : 1 + parallel_lines, 1 : 1 + tile_width].astype(jnp.float32) + update
    ) * mask_f[:, None]
    return fresh.astype(jnp.bfloat16)


def compiler_params(mib=60):
    return pltpu.CompilerParams(vmem_limit_bytes=mib * MIB)


def cost(flops, *arrays):
    return pl.CostEstimate(
        flops=flops, bytes_accessed=sum(x.size * x.dtype.itemsize for x in arrays), transcendentals=0
    )


def lane_spans(width, size=256):
    return [slice(at, min(at + size, width)) for at in range(0, width, size)]


def analyse_wide(air, table, width, groups):
    lines, cells, _ = air.shape
    rows = table.shape[0] // groups
    places = [(0, 0, width - SLIM), (1, width - SLIM, width)]
    out = jax.ShapeDtypeStruct((groups, rows, 2 * width - SLIM), jnp.bfloat16)

    def body(table_ref, air_ref, out_ref):
        for line, at, size in places:
            for span in lane_spans(size):
                coeffs = jnp.dot(table_ref[...], air_ref[line, :, span], preferred_element_type=jnp.float32)
                out_ref[:, :, at + span.start : at + span.stop] = coeffs.astype(jnp.bfloat16).reshape(
                    groups, rows, -1
                )

    return pl.pallas_call(
        body,
        grid=(1,),
        in_specs=[
            pl.BlockSpec(table.shape, lambda i: (0, 0)),
            pl.BlockSpec((lines, cells, width), lambda i: (0, 0, 0)),
        ],
        out_specs=pl.BlockSpec(out.shape, lambda i: (0, 0, 0)),
        out_shape=out,
        compiler_params=compiler_params(),
        cost_estimate=cost(2 * lines * table.size * width, table, air, out),
        name="analyse_wide",
    )(table, air)


def analyse_slim(air, table, start, sec, sections, groups):
    lines, cells, channels = air.shape
    width = channels - start
    plane = groups // sections
    rows = table.shape[0] // groups
    size = plane * rows
    pieces = lines + 1
    out = jax.ShapeDtypeStruct((pieces, plane, rows, width), jnp.bfloat16)

    def body(sec_ref, table_ref, air_ref, before_ref, *outs):
        joined = jnp.concatenate([air_ref[a] for a in range(lines)] + [before_ref[0]], axis=1)
        for o, out_ref in enumerate(outs):
            part = pl.ds(pl.multiple_of((sec_ref[0] ^ o) * size, size), size)
            coeffs = jnp.dot(table_ref[part, :], joined, preferred_element_type=jnp.float32).astype(jnp.bfloat16)
            for a in range(pieces):
                out_ref[a] = coeffs[:, a * width : (a + 1) * width].reshape(plane, rows, width)

    return pl.pallas_call(
        body,
        grid=(1,),
        in_specs=[
            pl.BlockSpec(memory_space=pltpu.SMEM),
            pl.BlockSpec(table.shape, lambda i: (0, 0)),
            pl.BlockSpec((lines, cells, width), lambda i: (0, 0, start // width)),
            pl.BlockSpec((1, cells, width), lambda i: (0, 0, start // width - 1)),
        ],
        out_specs=[pl.BlockSpec(out.shape, lambda i: (0, 0, 0, 0))] * sections,
        out_shape=[out] * sections,
        compiler_params=compiler_params(),
        cost_estimate=cost(2 * pieces * table.size * width, table, *[out] * 2 * sections),
        name="analyse_slim",
    )(sec, table, air, air)


def wavenumber_at(row):
    return row % GROUP // 2 * 2 + row // GROUP


def damp(transform, coeffs, damping):
    spectrum = jnp.dot(transform, coeffs, preferred_element_type=jnp.float32)
    scaled = (spectrum * damping).astype(jnp.bfloat16)
    back = lax.dot_general(transform, scaled, (((0,), (0,)), ((), ())), preferred_element_type=jnp.float32)
    return back.astype(jnp.bfloat16)


def latitudinal_wide(coeffs, joined, matrix, damping):
    devices, rows, _ = coeffs.shape
    modes, degrees, lats = matrix.shape
    lines = lats // devices
    width = (coeffs.shape[-1] + SLIM) // 2
    both = width - SLIM

    def body(x_ref, joined_ref, matrix_ref, damping_ref, out_ref):
        parity = pl.program_id(0)
        for span in lane_spans(both) + [slice(both, width)]:
            first = x_ref[:, :, span] if span.start < both else joined_ref[...]
            second = x_ref[:, :, both + span.start : both + span.stop]
            by_coeff = jnp.swapaxes(jnp.stack([first, second], axis=1).reshape(lats, GROUP, -1), 0, 1)
            results = [
                damp(matrix_ref[wavenumber_at(row) + parity], by_coeff[row], damping_ref[:, span])
                for row in range(GROUP)
            ]
            out_ref[:, :, :, span] = jnp.swapaxes(jnp.stack(results), 0, 1).reshape(devices, lines, GROUP, -1)

    return pl.pallas_call(
        body,
        grid=(rows // GROUP,),
        in_specs=[
            pl.BlockSpec((devices, GROUP, coeffs.shape[-1]), lambda p: (0, p, 0)),
            pl.BlockSpec((devices, GROUP, SLIM), lambda p: (0, p, 0)),
            whole(matrix),
            pl.BlockSpec((degrees, width), lambda p: (0, 0)),
        ],
        out_specs=pl.BlockSpec((devices, lines, GROUP, width), lambda p: (0, 0, p, 0)),
        out_shape=jax.ShapeDtypeStruct((devices, lines, rows, width), jnp.bfloat16),
        compiler_params=compiler_params(),
        cost_estimate=cost(4 * rows * degrees * lats * width, coeffs, coeffs, matrix),
        name="latitudinal_wide",
    )(coeffs, joined, matrix, damping)


def whole(x):
    return pl.BlockSpec(x.shape, lambda *_: (0,) * len(x.shape))


def to_plane(parts, place):
    lines, plane, rows, width = parts[0].shape
    sections = len(parts)
    out = jax.ShapeDtypeStruct((sections, lines, rows, width), jnp.bfloat16)

    def body(place_ref, *refs):
        for p, out_ref in enumerate(refs[sections:]):
            for o in range(sections):
                for a in range(lines):
                    out_ref[o, a] = refs[o][a, place_ref[0] ^ p]

    return pl.pallas_call(
        body,
        grid=(1,),
        in_specs=[pl.BlockSpec(memory_space=pltpu.SMEM)] + [whole(parts[0])] * sections,
        out_specs=[whole(out)] * plane,
        out_shape=[out] * plane,
        compiler_params=compiler_params(),
        cost_estimate=cost(0, *parts, *parts),
        name="to_plane",
    )(place, *parts)


def from_plane(parts, place):
    sections, lines, rows, width = parts[0].shape
    plane = len(parts)
    out = jax.ShapeDtypeStruct((lines, plane, rows, width), jnp.bfloat16)

    def body(place_ref, *refs):
        for o, out_ref in enumerate(refs[plane:]):
            for p in range(plane):
                for a in range(lines):
                    out_ref[a, place_ref[0] ^ p] = refs[p][o, a]

    return pl.pallas_call(
        body,
        grid=(1,),
        in_specs=[pl.BlockSpec(memory_space=pltpu.SMEM)] + [whole(parts[0])] * plane,
        out_specs=[whole(out)] * sections,
        out_shape=[out] * sections,
        compiler_params=compiler_params(),
        cost_estimate=cost(0, *parts, *parts),
        name="from_plane",
    )(place, *parts)


def latitudinal_slim(parts, matrix, damping, start, position):
    sections, pieces, rows, width = parts[0].shape
    lines = pieces - 1
    plane = len(parts)
    degrees = damping.shape[0]
    own = sections * lines
    out = jax.ShapeDtypeStruct((sections, lines, rows, width), jnp.bfloat16)
    joined = jax.ShapeDtypeStruct((sections * plane, rows, width), jnp.bfloat16)

    def body(position_ref, matrix_ref, damping_ref, *refs):
        part_refs, joined_ref, out_refs = refs[:plane], refs[plane], refs[plane + 1 :]
        latitudes = jnp.concatenate([ref[:, :lines].reshape(own, rows, width) for ref in part_refs], axis=0)
        by_coeff = jnp.swapaxes(latitudes, 0, 1)
        results = [
            damp(matrix_ref[wavenumber_at(row)], by_coeff[row], damping_ref[...]) for row in range(rows)
        ]
        by_lat = jnp.swapaxes(jnp.stack(results), 0, 1)
        for p, out_ref in enumerate(out_refs):
            out_ref[...] = by_lat[p * own : (p + 1) * own].reshape(out_ref.shape)
            for o in range(sections):
                device = (position_ref[0] ^ o) * plane + (position_ref[1] ^ p)
                joined_ref[device] = part_refs[p][o, lines]

    return pl.pallas_call(
        body,
        grid=(1,),
        in_specs=[
            pl.BlockSpec(memory_space=pltpu.SMEM),
            whole(matrix),
            pl.BlockSpec((degrees, width), lambda i: (0, start // width)),
        ]
        + [whole(parts[0])] * plane,
        out_specs=[whole(joined)] + [whole(out)] * plane,
        out_shape=[joined] + [out] * plane,
        compiler_params=compiler_params(),
        cost_estimate=pl.CostEstimate(flops=10**11, bytes_accessed=3 * 10**8, transcendentals=0),
        name="latitudinal_slim",
    )(position, matrix, damping, *parts)


def advance(air, rebuilt, sea, warmth):
    warmed = lax.dot_general(sea, warmth, (((0,), (0,)), ((), ())), preferred_element_type=jnp.float32)
    return (air.astype(jnp.float32) + rebuilt + warmed).astype(jnp.bfloat16)


def three_parts(values):
    parts, rest = [], values
    for _ in range(3):
        parts.append(lax.reduce_precision(rest, 8, 7))
        rest = rest - parts[-1]
    parts += [jnp.zeros_like(values)] * (GROUP - 3)
    return jnp.stack(parts).astype(jnp.bfloat16)


def synthesise_slim(parts, table, air, sea, warmth, start, sec):
    lines, plane, rows, width = parts[0].shape
    sections = len(parts)
    half = air.shape[2]

    def body(sec_ref, table_ref, air_ref, sea_ref, warmth_ref, *refs):
        part_refs, out_ref, gathered = refs[:sections], refs[-2], refs[-1]
        for o, part_ref in enumerate(part_refs):
            for a in range(lines):
                for odd in range(2):
                    gathered[odd, sec_ref[0] ^ o, :, :, a * width : (a + 1) * width] = part_ref[
                        a, :, odd * GROUP : (odd + 1) * GROUP, :
                    ]
        even, odd = (
            jnp.dot(
                table_ref[odd],
                gathered[odd].reshape(sections * plane * GROUP, lines * width),
                preferred_element_type=jnp.float32,
            )
            for odd in range(2)
        )
        for at, rebuilt in enumerate((even + odd, even - odd)):
            for a in range(lines):
                out_ref[a, at] = advance(
                    air_ref[a, at], rebuilt[:, a * width : (a + 1) * width], sea_ref[a, at], warmth_ref[...]
                )

    return pl.pallas_call(
        body,
        grid=(1,),
        in_specs=[
            pl.BlockSpec(memory_space=pltpu.SMEM),
            pl.BlockSpec(table.shape, lambda i: (0, 0, 0)),
            pl.BlockSpec((lines, 2, half, width), lambda i: (0, 0, 0, start // width)),
            whole(sea),
            pl.BlockSpec((GROUP, width), lambda i: (0, start // width)),
        ]
        + [pl.BlockSpec(parts[0].shape, lambda i: (0, 0, 0, 0))] * sections,
        out_specs=pl.BlockSpec((lines, 2, half, width), lambda i: (0, 0, 0, start // width)),
        out_shape=jax.ShapeDtypeStruct(air.shape, jnp.bfloat16),
        scratch_shapes=[pltpu.VMEM((2, sections, plane, GROUP, lines * width), jnp.bfloat16)],
        compiler_params=compiler_params(),
        cost_estimate=pl.CostEstimate(flops=10**11, bytes_accessed=3 * 10**8, transcendentals=0),
        name="synthesise_slim",
    )(sec, table, air, sea, warmth, *parts)


def synthesise_wide(coeffs, table, air, sea, warmth, begun):
    groups, lines, rows, width = coeffs.shape
    half = air.shape[2]

    def body(table_ref, coeff_ref, air_ref, sea_ref, warmth_ref, begun_ref, out_ref):
        for span in lane_spans(width):
            even, odd = (
                jnp.dot(
                    table_ref[odd],
                    coeff_ref[:, 0, odd * GROUP : (odd + 1) * GROUP, span].reshape(groups * GROUP, -1),
                    preferred_element_type=jnp.float32,
                )
                for odd in range(2)
            )
            for at, rebuilt in enumerate((even + odd, even - odd)):
                out_ref[0, at, :, span] = advance(
                    air_ref[0, at, :, span], rebuilt, sea_ref[0, at], warmth_ref[:, span]
                )

    return pl.pallas_call(
        body,
        grid=(lines,),
        in_specs=[
            pl.BlockSpec(table.shape, lambda a: (0, 0, 0)),
            pl.BlockSpec((groups, 1, rows, width), lambda a: (0, a, 0, 0)),
            pl.BlockSpec((1, 2, half, width), lambda a: (a, 0, 0, 0)),
            pl.BlockSpec((1, 2, GROUP, half), lambda a: (a, 0, 0, 0)),
            pl.BlockSpec((GROUP, width), lambda a: (0, 0)),
            pl.BlockSpec(memory_space=pl.ANY),
        ],
        out_specs=pl.BlockSpec((1, 2, half, width), lambda a: (a, 0, 0, 0)),
        out_shape=jax.ShapeDtypeStruct(air.shape, jnp.bfloat16),
        input_output_aliases={5: 0},
        compiler_params=compiler_params(),
        cost_estimate=cost(4 * lines * half * half * width, table, coeffs, coeffs, coeffs),
        name="synthesise_wide",
    )(table, coeffs, air, sea, warmth, begun)


def gather_flux(air, projector):
    flux_local = jnp.einsum(
        "anc,cf->fan",
        air,
        projector,
        preferred_element_type=jnp.float32,
    ).astype(jnp.bfloat16)
    return lax.all_gather(flux_local, "band", axis=1, tiled=True)


def shards(
    air_field_lattice,
    associated_polynomial_matrix,
    harmonic_damping_factor,
    boundary_exchange_projector,
    warmth_response_factor,
    water_patch_fields,
    kernel_coefficients,
    local_exchange_matrix,
    patch_average_matrix,
    water_kernel_offset,
    water_readout_matrix,
    patch_holder_index,
    water_point_indicator,
    water_point_totals,
):
    parallel_lines, meridian_number, channel_count = air_field_lattice.shape
    sec_count = lax.axis_size("sec")
    band_count = lax.axis_size("band")
    core_count = lax.axis_size("ch")
    device_count = sec_count * band_count * core_count
    total_cols = 2 * K
    per_device = total_cols // device_count
    slot_count = water_patch_fields.shape[0]
    mode_count = associated_polynomial_matrix.shape[0]
    lat_count = associated_polynomial_matrix.shape[1]
    wide = channel_count - SLIM
    in_kernels = (
        per_device == 2 * GROUP
        and wide > SLIM
        and wide % SLIM == 0
        and parallel_lines == 2
        and sec_count & (sec_count - 1) == 0
        and lat_count == device_count * parallel_lines
    )
    if in_kernels:
        plane = band_count * core_count
        sec_id = lax.axis_index("sec")
        sec = sec_id.reshape(1).astype(jnp.int32)
        forward, backward = map(jnp.asarray, transform_tables(meridian_number, device_count))
        hops = [[(i, i ^ o) for i in range(sec_count)] for o in range(sec_count)]

        twists = [[(i, i ^ p) for i in range(plane)] for p in range(plane)]
        place = (lax.axis_index("band") * core_count + lax.axis_index("ch")).astype(jnp.int32)

        def over_sections(blocks):
            return [lax.ppermute(x, "sec", hops[o]) if o else x for o, x in enumerate(blocks)]

        def over_plane(blocks):
            return [lax.ppermute(x, ("band", "ch"), twists[p]) if p else x for p, x in enumerate(blocks)]

        slim = analyse_slim(air_field_lattice, forward, wide, sec, sec_count, device_count)
        air_after, *slim = lax.optimization_barrier((air_field_lattice, *slim))
        slim = over_sections(slim)
        wide_coeffs = analyse_wide(air_after, forward, wide, device_count)
        wide_coeffs = lax.all_to_all(wide_coeffs, AXES, split_axis=0, concat_axis=0, tiled=True)
        slim = to_plane(slim, place.reshape(1))
        matrix_after, *slim = lax.optimization_barrier((associated_polynomial_matrix, *slim))
        slim = over_plane(slim)

        at_lat = jnp.arange(lat_count, dtype=jnp.int32)
        sections_at = at_lat // parallel_lines % sec_count ^ sec_id
        places_at = at_lat // (parallel_lines * sec_count) ^ place
        order = (sections_at * plane + places_at) * parallel_lines + at_lat % parallel_lines
        shuffle = (at_lat[:, None] == order[None, :]).astype(jnp.bfloat16)
        shuffled = jnp.einsum(
            "mlt,tu->mlu", matrix_after, shuffle, preferred_element_type=jnp.float32
        ).astype(jnp.bfloat16)

        position = jnp.stack([sec_id, place]).astype(jnp.int32)
        joined, *slim = latitudinal_slim(slim, shuffled, harmonic_damping_factor, wide, position)
        slim = from_plane(over_plane(slim), place.reshape(1))
        wide_coeffs, *slim = lax.optimization_barrier((wide_coeffs, *slim))
        slim = over_sections(slim)
        wide_coeffs = latitudinal_wide(
            wide_coeffs, joined, associated_polynomial_matrix, harmonic_damping_factor
        )
        wide_coeffs = lax.all_to_all(wide_coeffs, AXES, split_axis=0, concat_axis=0, tiled=True)
        (air_after, water_patch_fields, warmth_response_factor, patch_holder_index, *slim) = lax.optimization_barrier(
            (air_field_lattice, water_patch_fields, warmth_response_factor, patch_holder_index, *slim)
        )
        gathered = gather_flux(air_after, boundary_exchange_projector)
    else:
        gathered = gather_flux(air_field_lattice, boundary_exchange_projector)
        table = dft_table(meridian_number)
        forward = jnp.asarray(np.ascontiguousarray(table.T))
        backward = jnp.asarray((table.astype(np.float32) * (2.0 / meridian_number)).astype(jnp.bfloat16))
        fourier = jnp.einsum(
            "qn,anc->aqc", forward, air_field_lattice, preferred_element_type=jnp.float32
        ).astype(jnp.bfloat16)
        collected = lax.all_to_all(fourier, AXES, split_axis=1, concat_axis=0, tiled=True)
        pairs = collected.reshape(lat_count, mode_count, 2, channel_count)
        spectrum = jnp.einsum(
            "mlt,tmpc->mlpc", associated_polynomial_matrix, pairs, preferred_element_type=jnp.float32
        )
        scaled = (spectrum * harmonic_damping_factor[None, :, None]).astype(jnp.bfloat16)
        damped = jnp.einsum(
            "mlt,mlpc->tmpc", associated_polynomial_matrix, scaled, preferred_element_type=jnp.float32
        ).astype(jnp.bfloat16).reshape(lat_count, per_device, channel_count)
        returned = lax.all_to_all(damped, AXES, split_axis=0, concat_axis=1, tiled=True)

    sec_id = lax.axis_index("sec")
    band_id = lax.axis_index("band")
    core_id = lax.axis_index("ch")
    owner_grid = patch_holder_index.reshape(sec_count, band_count, core_count, -1)
    tiles_per_row = owner_grid.shape[3]
    owner_group = lax.dynamic_index_in_dim(owner_grid, sec_id, 0, keepdims=False)
    owner_group = lax.dynamic_index_in_dim(owner_group, core_id, 1, keepdims=False)
    owner_flat = owner_group.reshape(-1)
    holders = jnp.arange(band_count, dtype=jnp.int32)
    mine_all = owner_flat[None, :] == holders[:, None]
    rank_all = jnp.cumsum(mine_all.astype(jnp.int32), axis=1) - 1
    slot_index = jnp.arange(slot_count, dtype=jnp.int32)
    pick_all = mine_all[:, None, :] & (rank_all[:, None, :] == slot_index[None, :, None])
    my_pick = lax.dynamic_index_in_dim(pick_all, band_id, 0, keepdims=False)
    flux_count = gathered.shape[0]
    tile_width = meridian_number // tiles_per_row
    pieces = gathered.reshape(flux_count, band_count, parallel_lines, tiles_per_row, tile_width)
    chooser = my_pick.reshape(slot_count, band_count, tiles_per_row).astype(jnp.bfloat16)
    tile_flux = jnp.einsum(
        "sbj,fbrjw->sfrw", chooser, pieces, preferred_element_type=jnp.float32
    ).astype(jnp.bfloat16)
    ocean_next = ocean_update(
        water_patch_fields,
        tile_flux,
        water_point_indicator,
        water_point_totals,
        kernel_coefficients,
        local_exchange_matrix,
        patch_average_matrix,
        water_kernel_offset,
        water_readout_matrix,
    )
    sea_slots = ocean_next[:, 0]
    sea_all = lax.all_gather(sea_slots, "band", axis=0, tiled=True)
    rank_tile = jnp.sum(jnp.where(mine_all, rank_all, 0), axis=0)
    my_owners = lax.dynamic_index_in_dim(owner_group, band_id, 0, keepdims=False)
    my_ranks = lax.dynamic_slice_in_dim(rank_tile, band_id * tiles_per_row, tiles_per_row)
    target = my_owners * slot_count + my_ranks
    selector = (
        target[:, None] == jnp.arange(band_count * slot_count, dtype=jnp.int32)[None, :]
    ).astype(jnp.bfloat16)
    water_patches = jnp.einsum(
        "jk,krw->rjw", selector, sea_all, preferred_element_type=jnp.float32
    ).astype(jnp.bfloat16)
    water_skin_warmth = water_patches.reshape(parallel_lines, meridian_number)
    if in_kernels:
        halves = (parallel_lines, 2, meridian_number // 2, -1)
        air = air_field_lattice.reshape(halves)
        sea = water_skin_warmth.reshape(parallel_lines, 2, 1, meridian_number // 2)
        sea = jnp.broadcast_to(sea, (parallel_lines, 2, GROUP, meridian_number // 2))
        warmth = three_parts(warmth_response_factor)
        begun = synthesise_slim(slim, backward, air, sea, warmth, wide, sec)
        advanced = synthesise_wide(wide_coeffs, backward, air, sea, warmth, begun)
        advanced = advanced.reshape(air_field_lattice.shape)
    else:
        rebuilt = jnp.einsum("nq,aqc->anc", backward, returned, preferred_element_type=jnp.float32)
        advanced = (
            air_field_lattice.astype(jnp.float32)
            + rebuilt
            + water_skin_warmth.astype(jnp.float32)[:, :, None] * warmth_response_factor[None, None]
        ).astype(jnp.bfloat16)
    return (advanced, ocean_next)


def solution(mesh):
    placed = (
        P(("sec", "band", "ch"), None, None),
        P(("sec", "band", "ch"), None, None),
        P(),
        P(),
        P(),
        P(("sec", "band", "ch"), None, None, None),
        P(),
        P(),
        P(),
        P(),
        P(),
        P(),
        P(("sec", "band", "ch"), None, None),
        P(("sec", "band", "ch")),
    )
    return jax.shard_map(
        shards,
        mesh=mesh,
        in_specs=placed,
        out_specs=(
            P(("sec", "band", "ch"), None, None),
            P(("sec", "band", "ch"), None, None, None),
        ),
        check_vma=False,
    )
```

```python
import functools
import math

import jax
import jax.numpy as jnp
import numpy as np
from jax import lax
from jax.experimental import pallas as pl
from jax.experimental.pallas import tpu as pltpu
from jax.sharding import PartitionSpec as P

K = 512
AXES = ("sec", "band", "ch")
GROUP = 16
SLIM = 128
MIB = 1024 * 1024


@functools.lru_cache(maxsize=None)
def dft_table(meridian_number):
    cell_index = np.arange(meridian_number, dtype=np.int64)[:, None]
    column = np.arange(2 * K, dtype=np.int64)[None, :]
    phase_angle = (cell_index * (column // 2) % meridian_number) * (2.0 * math.pi / meridian_number)
    table = np.where(column % 2 == 0, np.cos(phase_angle), -np.sin(phase_angle))
    return table.astype(np.float32).astype(jnp.bfloat16)


@functools.lru_cache(maxsize=None)
def transform_tables(meridian_number, groups):
    half = meridian_number // 2
    table = dft_table(meridian_number).astype(np.float32)
    by_parity = table.reshape(meridian_number, groups, -1, 2, 2).transpose(1, 3, 2, 4, 0)
    forward = by_parity.reshape(-1, meridian_number)
    backward = by_parity.transpose(1, 4, 0, 2, 3)[:, :half].reshape(2, half, -1) * (2.0 / meridian_number)
    return tuple(np.ascontiguousarray(x).astype(jnp.bfloat16) for x in (forward, backward))


def ocean_update(
    state,
    tile_flux,
    mask_tile,
    count_tile,
    kernel_coefficients,
    local_exchange_matrix,
    patch_average_matrix,
    water_kernel_offset,
    water_readout_matrix,
):
    parallel_lines = mask_tile.shape[1]
    tile_width = mask_tile.shape[2]
    mask_f = mask_tile.astype(jnp.float32)
    masked = tile_flux * mask_tile[:, None].astype(jnp.bfloat16)
    fmean = (
        jnp.sum(masked.astype(jnp.float32), axis=(2, 3))
        / jnp.maximum(count_tile.astype(jnp.float32), 1.0)[:, None]
    )
    total = jnp.einsum(
        "fo,sfrw->sorw", local_exchange_matrix, masked, preferred_element_type=jnp.float32
    )
    for shift_row in range(3):
        for shift_col in range(3):
            window = state[
                :, :, shift_row : shift_row + parallel_lines, shift_col : shift_col + tile_width
            ]
            total = total + jnp.einsum(
                "io,sirw->sorw",
                kernel_coefficients[shift_row, shift_col],
                window,
                preferred_element_type=jnp.float32,
            )
    mean_term = jnp.sum(fmean[:, :, None] * patch_average_matrix[None], axis=1)
    total = total + mean_term[:, :, None, None] + water_kernel_offset[None, :, None, None]
    hidden = jax.nn.gelu(total, approximate=True).astype(jnp.bfloat16)
    update = jnp.einsum(
        "io,sirw->sorw", water_readout_matrix, hidden, preferred_element_type=jnp.float32
    )
    fresh = (
        state[:, :, 1 : 1 + parallel_lines, 1 : 1 + tile_width].astype(jnp.float32) + update
    ) * mask_f[:, None]
    return fresh.astype(jnp.bfloat16)


def compiler_params(mib=60):
    return pltpu.CompilerParams(vmem_limit_bytes=mib * MIB)


def cost(flops, *arrays):
    return pl.CostEstimate(
        flops=flops, bytes_accessed=sum(x.size * x.dtype.itemsize for x in arrays), transcendentals=0
    )


def lane_spans(width, size=256):
    return [slice(at, min(at + size, width)) for at in range(0, width, size)]


def analyse_wide(air, table, width, groups):
    lines, cells, _ = air.shape
    rows = table.shape[0] // groups
    places = [(0, 0, width - SLIM), (1, width - SLIM, width)]
    out = jax.ShapeDtypeStruct((groups, rows, 2 * width - SLIM), jnp.bfloat16)

    def body(table_ref, air_ref, out_ref):
        for line, at, size in places:
            for span in lane_spans(size):
                coeffs = jnp.dot(table_ref[...], air_ref[line, :, span], preferred_element_type=jnp.float32)
                out_ref[:, :, at + span.start : at + span.stop] = coeffs.astype(jnp.bfloat16).reshape(
                    groups, rows, -1
                )

    return pl.pallas_call(
        body,
        grid=(1,),
        in_specs=[
            pl.BlockSpec(table.shape, lambda i: (0, 0)),
            pl.BlockSpec((lines, cells, width), lambda i: (0, 0, 0)),
        ],
        out_specs=pl.BlockSpec(out.shape, lambda i: (0, 0, 0)),
        out_shape=out,
        compiler_params=compiler_params(),
        cost_estimate=cost(2 * lines * table.size * width, table, air, out),
        name="analyse_wide",
    )(table, air)


def analyse_slim(air, table, start, sec, sections, groups):
    lines, cells, channels = air.shape
    width = channels - start
    plane = groups // sections
    rows = table.shape[0] // groups
    size = plane * rows
    pieces = lines + 1
    out = jax.ShapeDtypeStruct((pieces, plane, rows, width), jnp.bfloat16)

    def body(sec_ref, table_ref, air_ref, before_ref, *outs):
        joined = jnp.concatenate([air_ref[a] for a in range(lines)] + [before_ref[0]], axis=1)
        for o, out_ref in enumerate(outs):
            part = pl.ds(pl.multiple_of((sec_ref[0] ^ o) * size, size), size)
            coeffs = jnp.dot(table_ref[part, :], joined, preferred_element_type=jnp.float32).astype(jnp.bfloat16)
            for a in range(pieces):
                out_ref[a] = coeffs[:, a * width : (a + 1) * width].reshape(plane, rows, width)

    return pl.pallas_call(
        body,
        grid=(1,),
        in_specs=[
            pl.BlockSpec(memory_space=pltpu.SMEM),
            pl.BlockSpec(table.shape, lambda i: (0, 0)),
            pl.BlockSpec((lines, cells, width), lambda i: (0, 0, start // width)),
            pl.BlockSpec((1, cells, width), lambda i: (0, 0, start // width - 1)),
        ],
        out_specs=[pl.BlockSpec(out.shape, lambda i: (0, 0, 0, 0))] * sections,
        out_shape=[out] * sections,
        compiler_params=compiler_params(),
        cost_estimate=cost(2 * pieces * table.size * width, table, *[out] * 2 * sections),
        name="analyse_slim",
    )(sec, table, air, air)


def wavenumber_at(row):
    return row % GROUP // 2 * 2 + row // GROUP


def damp(transform, coeffs, damping):
    spectrum = jnp.dot(transform, coeffs, preferred_element_type=jnp.float32)
    scaled = (spectrum * damping).astype(jnp.bfloat16)
    back = lax.dot_general(transform, scaled, (((0,), (0,)), ((), ())), preferred_element_type=jnp.float32)
    return back.astype(jnp.bfloat16)


def latitudinal_wide(coeffs, joined, matrix, damping):
    devices, rows, _ = coeffs.shape
    modes, degrees, lats = matrix.shape
    lines = lats // devices
    width = (coeffs.shape[-1] + SLIM) // 2
    both = width - SLIM

    def body(x_ref, joined_ref, matrix_ref, damping_ref, out_ref):
        parity = pl.program_id(0)
        for span in lane_spans(both) + [slice(both, width)]:
            first = x_ref[:, :, span] if span.start < both else joined_ref[...]
            second = x_ref[:, :, both + span.start : both + span.stop]
            by_coeff = jnp.swapaxes(jnp.stack([first, second], axis=1).reshape(lats, GROUP, -1), 0, 1)
            results = [
                damp(matrix_ref[wavenumber_at(row) + parity], by_coeff[row], damping_ref[:, span])
                for row in range(GROUP)
            ]
            out_ref[:, :, :, span] = jnp.swapaxes(jnp.stack(results), 0, 1).reshape(devices, lines, GROUP, -1)

    return pl.pallas_call(
        body,
        grid=(rows // GROUP,),
        in_specs=[
            pl.BlockSpec((devices, GROUP, coeffs.shape[-1]), lambda p: (0, p, 0)),
            pl.BlockSpec((devices, GROUP, SLIM), lambda p: (0, p, 0)),
            whole(matrix),
            pl.BlockSpec((degrees, width), lambda p: (0, 0)),
        ],
        out_specs=pl.BlockSpec((devices, lines, GROUP, width), lambda p: (0, 0, p, 0)),
        out_shape=jax.ShapeDtypeStruct((devices, lines, rows, width), jnp.bfloat16),
        compiler_params=compiler_params(),
        cost_estimate=cost(4 * rows * degrees * lats * width, coeffs, coeffs, matrix),
        name="latitudinal_wide",
    )(coeffs, joined, matrix, damping)


def whole(x):
    return pl.BlockSpec(x.shape, lambda *_: (0,) * len(x.shape))


def to_plane(parts, place):
    lines, plane, rows, width = parts[0].shape
    sections = len(parts)
    out = jax.ShapeDtypeStruct((sections, lines, rows, width), jnp.bfloat16)

    def body(place_ref, *refs):
        for p, out_ref in enumerate(refs[sections:]):
            for o in range(sections):
                for a in range(lines):
                    out_ref[o, a] = refs[o][a, place_ref[0] ^ p]

    return pl.pallas_call(
        body,
        grid=(1,),
        in_specs=[pl.BlockSpec(memory_space=pltpu.SMEM)] + [whole(parts[0])] * sections,
        out_specs=[whole(out)] * plane,
        out_shape=[out] * plane,
        compiler_params=compiler_params(63),
        cost_estimate=cost(0, *parts, *parts),
        name="to_plane",
    )(place, *parts)


def from_plane(parts, place):
    sections, lines, rows, width = parts[0].shape
    plane = len(parts)
    out = jax.ShapeDtypeStruct((lines, plane, rows, width), jnp.bfloat16)

    def body(place_ref, *refs):
        for o, out_ref in enumerate(refs[plane:]):
            for p in range(plane):
                for a in range(lines):
                    out_ref[a, place_ref[0] ^ p] = refs[p][o, a]

    return pl.pallas_call(
        body,
        grid=(1,),
        in_specs=[pl.BlockSpec(memory_space=pltpu.SMEM)] + [whole(parts[0])] * plane,
        out_specs=[whole(out)] * sections,
        out_shape=[out] * sections,
        compiler_params=compiler_params(63),
        cost_estimate=cost(0, *parts, *parts),
        name="from_plane",
    )(place, *parts)


def latitudinal_slim(parts, matrix, damping, start, position):
    sections, pieces, rows, width = parts[0].shape
    lines = pieces - 1
    plane = len(parts)
    degrees = damping.shape[0]
    own = sections * lines
    out = jax.ShapeDtypeStruct((sections, lines, rows, width), jnp.bfloat16)
    joined = jax.ShapeDtypeStruct((sections * plane, rows, width), jnp.bfloat16)

    def body(position_ref, matrix_ref, damping_ref, *refs):
        part_refs, joined_ref, out_refs = refs[:plane], refs[plane], refs[plane + 1 :]
        latitudes = jnp.concatenate([ref[:, :lines].reshape(own, rows, width) for ref in part_refs], axis=0)
        by_coeff = jnp.swapaxes(latitudes, 0, 1)
        results = [
            damp(matrix_ref[wavenumber_at(row)], by_coeff[row], damping_ref[...]) for row in range(rows)
        ]
        by_lat = jnp.swapaxes(jnp.stack(results), 0, 1)
        for p, out_ref in enumerate(out_refs):
            out_ref[...] = by_lat[p * own : (p + 1) * own].reshape(out_ref.shape)
            for o in range(sections):
                device = (position_ref[0] ^ o) * plane + (position_ref[1] ^ p)
                joined_ref[device] = part_refs[p][o, lines]

    return pl.pallas_call(
        body,
        grid=(1,),
        in_specs=[
            pl.BlockSpec(memory_space=pltpu.SMEM),
            whole(matrix),
            pl.BlockSpec((degrees, width), lambda i: (0, start // width)),
        ]
        + [whole(parts[0])] * plane,
        out_specs=[whole(joined)] + [whole(out)] * plane,
        out_shape=[joined] + [out] * plane,
        compiler_params=compiler_params(63),
        cost_estimate=pl.CostEstimate(flops=10**11, bytes_accessed=3 * 10**8, transcendentals=0),
        name="latitudinal_slim",
    )(position, matrix, damping, *parts)


def advance(air, rebuilt, sea, warmth):
    warmed = lax.dot_general(sea, warmth, (((0,), (0,)), ((), ())), preferred_element_type=jnp.float32)
    return (air.astype(jnp.float32) + rebuilt + warmed).astype(jnp.bfloat16)


def three_parts(values):
    parts, rest = [], values
    for _ in range(3):
        parts.append(lax.reduce_precision(rest, 8, 7))
        rest = rest - parts[-1]
    parts += [jnp.zeros_like(values)] * (GROUP - 3)
    return jnp.stack(parts).astype(jnp.bfloat16)


def synthesise_slim(parts, table, air, sea, warmth, start, sec):
    lines, plane, rows, width = parts[0].shape
    sections = len(parts)
    half = air.shape[2]

    def body(sec_ref, table_ref, air_ref, sea_ref, warmth_ref, *refs):
        part_refs, out_ref, gathered = refs[:sections], refs[-2], refs[-1]
        for o, part_ref in enumerate(part_refs):
            for a in range(lines):
                for odd in range(2):
                    gathered[odd, sec_ref[0] ^ o, :, :, a * width : (a + 1) * width] = part_ref[
                        a, :, odd * GROUP : (odd + 1) * GROUP, :
                    ]
        even, odd = (
            jnp.dot(
                table_ref[odd],
                gathered[odd].reshape(sections * plane * GROUP, lines * width),
                preferred_element_type=jnp.float32,
            )
            for odd in range(2)
        )
        for at, rebuilt in enumerate((even + odd, even - odd)):
            for a in range(lines):
                out_ref[a, at] = advance(
                    air_ref[a, at], rebuilt[:, a * width : (a + 1) * width], sea_ref[a, at], warmth_ref[...]
                )

    return pl.pallas_call(
        body,
        grid=(1,),
        in_specs=[
            pl.BlockSpec(memory_space=pltpu.SMEM),
            pl.BlockSpec(table.shape, lambda i: (0, 0, 0)),
            pl.BlockSpec((lines, 2, half, width), lambda i: (0, 0, 0, start // width)),
            whole(sea),
            pl.BlockSpec((GROUP, width), lambda i: (0, start // width)),
        ]
        + [pl.BlockSpec(parts[0].shape, lambda i: (0, 0, 0, 0))] * sections,
        out_specs=pl.BlockSpec((lines, 2, half, width), lambda i: (0, 0, 0, start // width)),
        out_shape=jax.ShapeDtypeStruct(air.shape, jnp.bfloat16),
        scratch_shapes=[pltpu.VMEM((2, sections, plane, GROUP, lines * width), jnp.bfloat16)],
        compiler_params=compiler_params(),
        cost_estimate=pl.CostEstimate(flops=10**11, bytes_accessed=3 * 10**8, transcendentals=0),
        name="synthesise_slim",
    )(sec, table, air, sea, warmth, *parts)


def synthesise_wide(coeffs, table, air, sea, warmth, begun):
    groups, lines, rows, width = coeffs.shape
    half = air.shape[2]

    def body(table_ref, coeff_ref, air_ref, sea_ref, warmth_ref, begun_ref, out_ref):
        for span in lane_spans(width):
            even, odd = (
                jnp.dot(
                    table_ref[odd],
                    coeff_ref[:, 0, odd * GROUP : (odd + 1) * GROUP, span].reshape(groups * GROUP, -1),
                    preferred_element_type=jnp.float32,
                )
                for odd in range(2)
            )
            for at, rebuilt in enumerate((even + odd, even - odd)):
                out_ref[0, at, :, span] = advance(
                    air_ref[0, at, :, span], rebuilt, sea_ref[0, at], warmth_ref[:, span]
                )

    return pl.pallas_call(
        body,
        grid=(lines,),
        in_specs=[
            pl.BlockSpec(table.shape, lambda a: (0, 0, 0)),
            pl.BlockSpec((groups, 1, rows, width), lambda a: (0, a, 0, 0)),
            pl.BlockSpec((1, 2, half, width), lambda a: (a, 0, 0, 0)),
            pl.BlockSpec((1, 2, GROUP, half), lambda a: (a, 0, 0, 0)),
            pl.BlockSpec((GROUP, width), lambda a: (0, 0)),
            pl.BlockSpec(memory_space=pl.ANY),
        ],
        out_specs=pl.BlockSpec((1, 2, half, width), lambda a: (a, 0, 0, 0)),
        out_shape=jax.ShapeDtypeStruct(air.shape, jnp.bfloat16),
        input_output_aliases={5: 0},
        compiler_params=compiler_params(),
        cost_estimate=cost(4 * lines * half * half * width, table, coeffs, coeffs, coeffs),
        name="synthesise_wide",
    )(table, coeffs, air, sea, warmth, begun)


def gather_flux(air, projector):
    flux_local = jnp.einsum(
        "anc,cf->fan",
        air,
        projector,
        preferred_element_type=jnp.float32,
    ).astype(jnp.bfloat16)
    return lax.all_gather(flux_local, "band", axis=1, tiled=True)


def shards(
    air_field_lattice,
    associated_polynomial_matrix,
    harmonic_damping_factor,
    boundary_exchange_projector,
    warmth_response_factor,
    water_patch_fields,
    kernel_coefficients,
    local_exchange_matrix,
    patch_average_matrix,
    water_kernel_offset,
    water_readout_matrix,
    patch_holder_index,
    water_point_indicator,
    water_point_totals,
):
    parallel_lines, meridian_number, channel_count = air_field_lattice.shape
    sec_count = lax.axis_size("sec")
    band_count = lax.axis_size("band")
    core_count = lax.axis_size("ch")
    device_count = sec_count * band_count * core_count
    total_cols = 2 * K
    per_device = total_cols // device_count
    slot_count = water_patch_fields.shape[0]
    mode_count = associated_polynomial_matrix.shape[0]
    lat_count = associated_polynomial_matrix.shape[1]
    wide = channel_count - SLIM
    in_kernels = (
        per_device == 2 * GROUP
        and wide > SLIM
        and wide % SLIM == 0
        and parallel_lines == 2
        and sec_count & (sec_count - 1) == 0
        and lat_count == device_count * parallel_lines
    )
    if in_kernels:
        plane = band_count * core_count
        sec_id = lax.axis_index("sec")
        sec = sec_id.reshape(1).astype(jnp.int32)
        forward, backward = map(jnp.asarray, transform_tables(meridian_number, device_count))
        hops = [[(i, i ^ o) for i in range(sec_count)] for o in range(sec_count)]

        twists = [[(i, i ^ p) for i in range(plane)] for p in range(plane)]
        place = (lax.axis_index("band") * core_count + lax.axis_index("ch")).astype(jnp.int32)

        def over_sections(blocks):
            return [lax.ppermute(x, "sec", hops[o]) if o else x for o, x in enumerate(blocks)]

        def over_plane(blocks):
            moved = {p: lax.ppermute(blocks[p], ("band", "ch"), twists[p]) for p in range(plane - 1, 0, -1)}
            return [moved.get(p, x) for p, x in enumerate(blocks)]

        slim = analyse_slim(air_field_lattice, forward, wide, sec, sec_count, device_count)
        air_after, *slim = lax.optimization_barrier((air_field_lattice, *slim))
        slim = over_sections(slim)
        wide_coeffs = analyse_wide(air_after, forward, wide, device_count)
        wide_coeffs = lax.all_to_all(wide_coeffs, AXES, split_axis=0, concat_axis=0, tiled=True)
        slim = to_plane(slim, place.reshape(1))
        matrix_after, *slim = lax.optimization_barrier((associated_polynomial_matrix, *slim))
        slim = over_plane(slim)

        at_lat = jnp.arange(lat_count, dtype=jnp.int32)
        sections_at = at_lat // parallel_lines % sec_count ^ sec_id
        places_at = at_lat // (parallel_lines * sec_count) ^ place
        order = (sections_at * plane + places_at) * parallel_lines + at_lat % parallel_lines
        shuffle = (at_lat[:, None] == order[None, :]).astype(jnp.bfloat16)
        shuffled = jnp.einsum(
            "mlt,tu->mlu", matrix_after, shuffle, preferred_element_type=jnp.float32
        ).astype(jnp.bfloat16)

        position = jnp.stack([sec_id, place]).astype(jnp.int32)
        joined, *slim = latitudinal_slim(slim, shuffled, harmonic_damping_factor, wide, position)
        slim = from_plane(over_plane(slim), place.reshape(1))
        wide_coeffs, *slim = lax.optimization_barrier((wide_coeffs, *slim))
        slim = over_sections(slim)
        wide_coeffs = latitudinal_wide(
            wide_coeffs, joined, associated_polynomial_matrix, harmonic_damping_factor
        )
        wide_coeffs = lax.all_to_all(wide_coeffs, AXES, split_axis=0, concat_axis=0, tiled=True)
        (air_after, water_patch_fields, warmth_response_factor, patch_holder_index, *slim) = lax.optimization_barrier(
            (air_field_lattice, water_patch_fields, warmth_response_factor, patch_holder_index, *slim)
        )
        gathered = gather_flux(air_after, boundary_exchange_projector)
    else:
        gathered = gather_flux(air_field_lattice, boundary_exchange_projector)
        table = dft_table(meridian_number)
        forward = jnp.asarray(np.ascontiguousarray(table.T))
        backward = jnp.asarray((table.astype(np.float32) * (2.0 / meridian_number)).astype(jnp.bfloat16))
        fourier = jnp.einsum(
            "qn,anc->aqc", forward, air_field_lattice, preferred_element_type=jnp.float32
        ).astype(jnp.bfloat16)
        collected = lax.all_to_all(fourier, AXES, split_axis=1, concat_axis=0, tiled=True)
        pairs = collected.reshape(lat_count, mode_count, 2, channel_count)
        spectrum = jnp.einsum(
            "mlt,tmpc->mlpc", associated_polynomial_matrix, pairs, preferred_element_type=jnp.float32
        )
        scaled = (spectrum * harmonic_damping_factor[None, :, None]).astype(jnp.bfloat16)
        damped = jnp.einsum(
            "mlt,mlpc->tmpc", associated_polynomial_matrix, scaled, preferred_element_type=jnp.float32
        ).astype(jnp.bfloat16).reshape(lat_count, per_device, channel_count)
        returned = lax.all_to_all(damped, AXES, split_axis=0, concat_axis=1, tiled=True)

    sec_id = lax.axis_index("sec")
    band_id = lax.axis_index("band")
    core_id = lax.axis_index("ch")
    owner_grid = patch_holder_index.reshape(sec_count, band_count, core_count, -1)
    tiles_per_row = owner_grid.shape[3]
    owner_group = lax.dynamic_index_in_dim(owner_grid, sec_id, 0, keepdims=False)
    owner_group = lax.dynamic_index_in_dim(owner_group, core_id, 1, keepdims=False)
    owner_flat = owner_group.reshape(-1)
    holders = jnp.arange(band_count, dtype=jnp.int32)
    mine_all = owner_flat[None, :] == holders[:, None]
    rank_all = jnp.cumsum(mine_all.astype(jnp.int32), axis=1) - 1
    slot_index = jnp.arange(slot_count, dtype=jnp.int32)
    pick_all = mine_all[:, None, :] & (rank_all[:, None, :] == slot_index[None, :, None])
    my_pick = lax.dynamic_index_in_dim(pick_all, band_id, 0, keepdims=False)
    flux_count = gathered.shape[0]
    tile_width = meridian_number // tiles_per_row
    pieces = gathered.reshape(flux_count, band_count, parallel_lines, tiles_per_row, tile_width)
    chooser = my_pick.reshape(slot_count, band_count, tiles_per_row).astype(jnp.bfloat16)
    tile_flux = jnp.einsum(
        "sbj,fbrjw->sfrw", chooser, pieces, preferred_element_type=jnp.float32
    ).astype(jnp.bfloat16)
    ocean_next = ocean_update(
        water_patch_fields,
        tile_flux,
        water_point_indicator,
        water_point_totals,
        kernel_coefficients,
        local_exchange_matrix,
        patch_average_matrix,
        water_kernel_offset,
        water_readout_matrix,
    )
    sea_slots = ocean_next[:, 0]
    sea_all = lax.all_gather(sea_slots, "band", axis=0, tiled=True)
    rank_tile = jnp.sum(jnp.where(mine_all, rank_all, 0), axis=0)
    my_owners = lax.dynamic_index_in_dim(owner_group, band_id, 0, keepdims=False)
    my_ranks = lax.dynamic_slice_in_dim(rank_tile, band_id * tiles_per_row, tiles_per_row)
    target = my_owners * slot_count + my_ranks
    selector = (
        target[:, None] == jnp.arange(band_count * slot_count, dtype=jnp.int32)[None, :]
    ).astype(jnp.bfloat16)
    water_patches = jnp.einsum(
        "jk,krw->rjw", selector, sea_all, preferred_element_type=jnp.float32
    ).astype(jnp.bfloat16)
    water_skin_warmth = water_patches.reshape(parallel_lines, meridian_number)
    if in_kernels:
        halves = (parallel_lines, 2, meridian_number // 2, -1)
        air = air_field_lattice.reshape(halves)
        sea = water_skin_warmth.reshape(parallel_lines, 2, 1, meridian_number // 2)
        sea = jnp.broadcast_to(sea, (parallel_lines, 2, GROUP, meridian_number // 2))
        warmth = three_parts(warmth_response_factor)
        begun = synthesise_slim(slim, backward, air, sea, warmth, wide, sec)
        advanced = synthesise_wide(wide_coeffs, backward, air, sea, warmth, begun)
        advanced = advanced.reshape(air_field_lattice.shape)
    else:
        rebuilt = jnp.einsum("nq,aqc->anc", backward, returned, preferred_element_type=jnp.float32)
        advanced = (
            air_field_lattice.astype(jnp.float32)
            + rebuilt
            + water_skin_warmth.astype(jnp.float32)[:, :, None] * warmth_response_factor[None, None]
        ).astype(jnp.bfloat16)
    return (advanced, ocean_next)


def solution(mesh):
    placed = (
        P(("sec", "band", "ch"), None, None),
        P(("sec", "band", "ch"), None, None),
        P(),
        P(),
        P(),
        P(("sec", "band", "ch"), None, None, None),
        P(),
        P(),
        P(),
        P(),
        P(),
        P(),
        P(("sec", "band", "ch"), None, None),
        P(("sec", "band", "ch")),
    )
    return jax.shard_map(
        shards,
        mesh=mesh,
        in_specs=placed,
        out_specs=(
            P(("sec", "band", "ch"), None, None),
            P(("sec", "band", "ch"), None, None, None),
        ),
        check_vma=False,
    )
```

```python
import functools
import math

import jax
import jax.numpy as jnp
import numpy as np
from jax import lax
from jax.experimental import pallas as pl
from jax.experimental.pallas import tpu as pltpu
from jax.sharding import PartitionSpec as P

K = 512
AXES = ("sec", "band", "ch")
GROUP = 16
SLIM = 128
MIB = 1024 * 1024


@functools.lru_cache(maxsize=None)
def dft_table(meridian_number):
    cell_index = np.arange(meridian_number, dtype=np.int64)[:, None]
    column = np.arange(2 * K, dtype=np.int64)[None, :]
    phase_angle = (cell_index * (column // 2) % meridian_number) * (2.0 * math.pi / meridian_number)
    table = np.where(column % 2 == 0, np.cos(phase_angle), -np.sin(phase_angle))
    return table.astype(np.float32).astype(jnp.bfloat16)


@functools.lru_cache(maxsize=None)
def transform_tables(meridian_number, groups):
    half = meridian_number // 2
    table = dft_table(meridian_number).astype(np.float32)
    by_parity = table.reshape(meridian_number, groups, -1, 2, 2).transpose(1, 3, 2, 4, 0)
    forward = by_parity.reshape(-1, meridian_number)
    backward = by_parity.transpose(1, 4, 0, 2, 3)[:, :half].reshape(2, half, -1) * (2.0 / meridian_number)
    return tuple(np.ascontiguousarray(x).astype(jnp.bfloat16) for x in (forward, backward))


def ocean_update(
    state,
    tile_flux,
    mask_tile,
    count_tile,
    kernel_coefficients,
    local_exchange_matrix,
    patch_average_matrix,
    water_kernel_offset,
    water_readout_matrix,
):
    parallel_lines = mask_tile.shape[1]
    tile_width = mask_tile.shape[2]
    mask_f = mask_tile.astype(jnp.float32)
    masked = tile_flux * mask_tile[:, None].astype(jnp.bfloat16)
    fmean = (
        jnp.sum(masked.astype(jnp.float32), axis=(2, 3))
        / jnp.maximum(count_tile.astype(jnp.float32), 1.0)[:, None]
    )
    total = jnp.einsum(
        "fo,sfrw->sorw", local_exchange_matrix, masked, preferred_element_type=jnp.float32
    )
    for shift_row in range(3):
        for shift_col in range(3):
            window = state[
                :, :, shift_row : shift_row + parallel_lines, shift_col : shift_col + tile_width
            ]
            total = total + jnp.einsum(
                "io,sirw->sorw",
                kernel_coefficients[shift_row, shift_col],
                window,
                preferred_element_type=jnp.float32,
            )
    mean_term = jnp.sum(fmean[:, :, None] * patch_average_matrix[None], axis=1)
    total = total + mean_term[:, :, None, None] + water_kernel_offset[None, :, None, None]
    hidden = jax.nn.gelu(total, approximate=True).astype(jnp.bfloat16)
    update = jnp.einsum(
        "io,sirw->sorw", water_readout_matrix, hidden, preferred_element_type=jnp.float32
    )
    fresh = (
        state[:, :, 1 : 1 + parallel_lines, 1 : 1 + tile_width].astype(jnp.float32) + update
    ) * mask_f[:, None]
    return fresh.astype(jnp.bfloat16)


def compiler_params(mib=60):
    return pltpu.CompilerParams(vmem_limit_bytes=mib * MIB)


def cost(flops, *arrays):
    return pl.CostEstimate(
        flops=flops, bytes_accessed=sum(x.size * x.dtype.itemsize for x in arrays), transcendentals=0
    )


def lane_spans(width, size=256):
    return [slice(at, min(at + size, width)) for at in range(0, width, size)]


def analyse_wide(air, table, width, groups):
    lines, cells, _ = air.shape
    rows = table.shape[0] // groups
    places = [(0, 0, width - SLIM), (1, width - SLIM, width)]
    out = jax.ShapeDtypeStruct((groups, rows, 2 * width - SLIM), jnp.bfloat16)

    def body(table_ref, air_ref, out_ref):
        for line, at, size in places:
            for span in lane_spans(size):
                coeffs = jnp.dot(table_ref[...], air_ref[line, :, span], preferred_element_type=jnp.float32)
                out_ref[:, :, at + span.start : at + span.stop] = coeffs.astype(jnp.bfloat16).reshape(
                    groups, rows, -1
                )

    return pl.pallas_call(
        body,
        grid=(1,),
        in_specs=[
            pl.BlockSpec(table.shape, lambda i: (0, 0)),
            pl.BlockSpec((lines, cells, width), lambda i: (0, 0, 0)),
        ],
        out_specs=pl.BlockSpec(out.shape, lambda i: (0, 0, 0)),
        out_shape=out,
        compiler_params=compiler_params(),
        cost_estimate=cost(2 * lines * table.size * width, table, air, out),
        name="analyse_wide",
    )(table, air)


def analyse_slim(air, table, start, sec, sections, groups):
    lines, cells, channels = air.shape
    width = channels - start
    plane = groups // sections
    rows = table.shape[0] // groups
    size = plane * rows
    pieces = lines + 1
    out = jax.ShapeDtypeStruct((pieces, plane, rows, width), jnp.bfloat16)

    def body(sec_ref, table_ref, air_ref, before_ref, *outs):
        joined = jnp.concatenate([air_ref[a] for a in range(lines)] + [before_ref[0]], axis=1)
        for o, out_ref in enumerate(outs):
            part = pl.ds(pl.multiple_of((sec_ref[0] ^ o) * size, size), size)
            coeffs = jnp.dot(table_ref[part, :], joined, preferred_element_type=jnp.float32).astype(jnp.bfloat16)
            for a in range(pieces):
                out_ref[a] = coeffs[:, a * width : (a + 1) * width].reshape(plane, rows, width)

    return pl.pallas_call(
        body,
        grid=(1,),
        in_specs=[
            pl.BlockSpec(memory_space=pltpu.SMEM),
            pl.BlockSpec(table.shape, lambda i: (0, 0)),
            pl.BlockSpec((lines, cells, width), lambda i: (0, 0, start // width)),
            pl.BlockSpec((1, cells, width), lambda i: (0, 0, start // width - 1)),
        ],
        out_specs=[pl.BlockSpec(out.shape, lambda i: (0, 0, 0, 0))] * sections,
        out_shape=[out] * sections,
        compiler_params=compiler_params(),
        cost_estimate=cost(2 * pieces * table.size * width, table, *[out] * 2 * sections),
        name="analyse_slim",
    )(sec, table, air, air)


def wavenumber_at(row):
    return row % GROUP // 2 * 2 + row // GROUP


def damp(transform, coeffs, damping):
    spectrum = jnp.dot(transform, coeffs, preferred_element_type=jnp.float32)
    scaled = (spectrum * damping).astype(jnp.bfloat16)
    back = lax.dot_general(transform, scaled, (((0,), (0,)), ((), ())), preferred_element_type=jnp.float32)
    return back.astype(jnp.bfloat16)


def latitudinal_wide(coeffs, joined, matrix, damping):
    devices, rows, _ = coeffs.shape
    modes, degrees, lats = matrix.shape
    lines = lats // devices
    width = (coeffs.shape[-1] + SLIM) // 2
    both = width - SLIM

    def body(x_ref, joined_ref, matrix_ref, damping_ref, out_ref):
        parity = pl.program_id(0)
        for span in lane_spans(both) + [slice(both, width)]:
            first = x_ref[:, :, span] if span.start < both else joined_ref[...]
            second = x_ref[:, :, both + span.start : both + span.stop]
            by_coeff = jnp.swapaxes(jnp.stack([first, second], axis=1).reshape(lats, GROUP, -1), 0, 1)
            results = [
                damp(matrix_ref[wavenumber_at(row) + parity], by_coeff[row], damping_ref[:, span])
                for row in range(GROUP)
            ]
            out_ref[:, :, :, span] = jnp.swapaxes(jnp.stack(results), 0, 1).reshape(devices, lines, GROUP, -1)

    return pl.pallas_call(
        body,
        grid=(rows // GROUP,),
        in_specs=[
            pl.BlockSpec((devices, GROUP, coeffs.shape[-1]), lambda p: (0, p, 0)),
            pl.BlockSpec((devices, GROUP, SLIM), lambda p: (0, p, 0)),
            whole(matrix),
            pl.BlockSpec((degrees, width), lambda p: (0, 0)),
        ],
        out_specs=pl.BlockSpec((devices, lines, GROUP, width), lambda p: (0, 0, p, 0)),
        out_shape=jax.ShapeDtypeStruct((devices, lines, rows, width), jnp.bfloat16),
        compiler_params=compiler_params(),
        cost_estimate=cost(4 * rows * degrees * lats * width, coeffs, coeffs, matrix),
        name="latitudinal_wide",
    )(coeffs, joined, matrix, damping)


def whole(x):
    return pl.BlockSpec(x.shape, lambda *_: (0,) * len(x.shape))


def to_plane(parts, place):
    lines, plane, rows, width = parts[0].shape
    sections = len(parts)
    out = jax.ShapeDtypeStruct((sections, lines, rows, width), jnp.bfloat16)

    def body(place_ref, *refs):
        for p, out_ref in enumerate(refs[sections:]):
            for o in range(sections):
                for a in range(lines):
                    out_ref[o, a] = refs[sections - 1 - o][a, place_ref[0] ^ p]

    return pl.pallas_call(
        body,
        grid=(1,),
        in_specs=[pl.BlockSpec(memory_space=pltpu.SMEM)] + [whole(parts[0])] * sections,
        out_specs=[whole(out)] * plane,
        out_shape=[out] * plane,
        compiler_params=compiler_params(63),
        cost_estimate=cost(0, *parts, *parts),
        name="to_plane",
    )(place, *parts[::-1])


def from_plane(parts, place):
    sections, lines, rows, width = parts[0].shape
    plane = len(parts)
    out = jax.ShapeDtypeStruct((lines, plane, rows, width), jnp.bfloat16)

    def body(place_ref, *refs):
        for o, out_ref in enumerate(refs[plane:]):
            for p in range(plane):
                for a in range(lines):
                    out_ref[a, place_ref[0] ^ p] = refs[p][o, a]

    return pl.pallas_call(
        body,
        grid=(1,),
        in_specs=[pl.BlockSpec(memory_space=pltpu.SMEM)] + [whole(parts[0])] * plane,
        out_specs=[whole(out)] * sections,
        out_shape=[out] * sections,
        compiler_params=compiler_params(63),
        cost_estimate=cost(0, *parts, *parts),
        name="from_plane",
    )(place, *parts)


def latitudinal_slim(parts, matrix, damping, start, position):
    sections, pieces, rows, width = parts[0].shape
    lines = pieces - 1
    plane = len(parts)
    degrees = damping.shape[0]
    own = sections * lines
    out = jax.ShapeDtypeStruct((sections, lines, rows, width), jnp.bfloat16)
    joined = jax.ShapeDtypeStruct((sections * plane, rows, width), jnp.bfloat16)

    def body(position_ref, matrix_ref, damping_ref, *refs):
        part_refs, joined_ref, out_refs = refs[:plane], refs[plane], refs[plane + 1 :]
        latitudes = jnp.concatenate([ref[:, :lines].reshape(own, rows, width) for ref in part_refs], axis=0)
        by_coeff = jnp.swapaxes(latitudes, 0, 1)
        results = [
            damp(matrix_ref[wavenumber_at(row)], by_coeff[row], damping_ref[...]) for row in range(rows)
        ]
        by_lat = jnp.swapaxes(jnp.stack(results), 0, 1)
        for p, out_ref in enumerate(out_refs):
            out_ref[...] = by_lat[p * own : (p + 1) * own].reshape(out_ref.shape)
            for o in range(sections):
                device = (position_ref[0] ^ o) * plane + (position_ref[1] ^ p)
                joined_ref[device] = part_refs[p][o, lines]

    return pl.pallas_call(
        body,
        grid=(1,),
        in_specs=[
            pl.BlockSpec(memory_space=pltpu.SMEM),
            whole(matrix),
            pl.BlockSpec((degrees, width), lambda i: (0, start // width)),
        ]
        + [whole(parts[0])] * plane,
        out_specs=[whole(joined)] + [whole(out)] * plane,
        out_shape=[joined] + [out] * plane,
        compiler_params=compiler_params(63),
        cost_estimate=pl.CostEstimate(flops=10**11, bytes_accessed=3 * 10**8, transcendentals=0),
        name="latitudinal_slim",
    )(position, matrix, damping, *parts)


def advance(air, rebuilt, sea, warmth):
    warmed = lax.dot_general(sea, warmth, (((0,), (0,)), ((), ())), preferred_element_type=jnp.float32)
    return (air.astype(jnp.float32) + rebuilt + warmed).astype(jnp.bfloat16)


def three_parts(values):
    parts, rest = [], values
    for _ in range(3):
        parts.append(lax.reduce_precision(rest, 8, 7))
        rest = rest - parts[-1]
    parts += [jnp.zeros_like(values)] * (GROUP - 3)
    return jnp.stack(parts).astype(jnp.bfloat16)


def synthesise_slim(parts, table, air, sea, warmth, start, sec):
    lines, plane, rows, width = parts[0].shape
    sections = len(parts)
    half = air.shape[2]

    def body(sec_ref, table_ref, air_ref, sea_ref, warmth_ref, *refs):
        part_refs, out_ref, gathered = refs[:sections], refs[-2], refs[-1]
        for o, part_ref in enumerate(part_refs):
            for a in range(lines):
                for odd in range(2):
                    gathered[odd, sec_ref[0] ^ o, :, :, a * width : (a + 1) * width] = part_ref[
                        a, :, odd * GROUP : (odd + 1) * GROUP, :
                    ]
        even, odd = (
            jnp.dot(
                table_ref[odd],
                gathered[odd].reshape(sections * plane * GROUP, lines * width),
                preferred_element_type=jnp.float32,
            )
            for odd in range(2)
        )
        for at, rebuilt in enumerate((even + odd, even - odd)):
            for a in range(lines):
                out_ref[a, at] = advance(
                    air_ref[a, at], rebuilt[:, a * width : (a + 1) * width], sea_ref[a, at], warmth_ref[...]
                )

    return pl.pallas_call(
        body,
        grid=(1,),
        in_specs=[
            pl.BlockSpec(memory_space=pltpu.SMEM),
            pl.BlockSpec(table.shape, lambda i: (0, 0, 0)),
            pl.BlockSpec((lines, 2, half, width), lambda i: (0, 0, 0, start // width)),
            whole(sea),
            pl.BlockSpec((GROUP, width), lambda i: (0, start // width)),
        ]
        + [pl.BlockSpec(parts[0].shape, lambda i: (0, 0, 0, 0))] * sections,
        out_specs=pl.BlockSpec((lines, 2, half, width), lambda i: (0, 0, 0, start // width)),
        out_shape=jax.ShapeDtypeStruct(air.shape, jnp.bfloat16),
        scratch_shapes=[pltpu.VMEM((2, sections, plane, GROUP, lines * width), jnp.bfloat16)],
        compiler_params=compiler_params(),
        cost_estimate=pl.CostEstimate(flops=10**11, bytes_accessed=3 * 10**8, transcendentals=0),
        name="synthesise_slim",
    )(sec, table, air, sea, warmth, *parts)


def synthesise_wide(coeffs, table, air, sea, warmth, begun):
    groups, lines, rows, width = coeffs.shape
    half = air.shape[2]

    def body(table_ref, coeff_ref, air_ref, sea_ref, warmth_ref, begun_ref, out_ref):
        for span in lane_spans(width):
            even, odd = (
                jnp.dot(
                    table_ref[odd],
                    coeff_ref[:, 0, odd * GROUP : (odd + 1) * GROUP, span].reshape(groups * GROUP, -1),
                    preferred_element_type=jnp.float32,
                )
                for odd in range(2)
            )
            for at, rebuilt in enumerate((even + odd, even - odd)):
                out_ref[0, at, :, span] = advance(
                    air_ref[0, at, :, span], rebuilt, sea_ref[0, at], warmth_ref[:, span]
                )

    return pl.pallas_call(
        body,
        grid=(lines,),
        in_specs=[
            pl.BlockSpec(table.shape, lambda a: (0, 0, 0)),
            pl.BlockSpec((groups, 1, rows, width), lambda a: (0, a, 0, 0)),
            pl.BlockSpec((1, 2, half, width), lambda a: (a, 0, 0, 0)),
            pl.BlockSpec((1, 2, GROUP, half), lambda a: (a, 0, 0, 0)),
            pl.BlockSpec((GROUP, width), lambda a: (0, 0)),
            pl.BlockSpec(memory_space=pl.ANY),
        ],
        out_specs=pl.BlockSpec((1, 2, half, width), lambda a: (a, 0, 0, 0)),
        out_shape=jax.ShapeDtypeStruct(air.shape, jnp.bfloat16),
        input_output_aliases={5: 0},
        compiler_params=compiler_params(),
        cost_estimate=cost(4 * lines * half * half * width, table, coeffs, coeffs, coeffs),
        name="synthesise_wide",
    )(table, coeffs, air, sea, warmth, begun)


def gather_flux(air, projector):
    flux_local = jnp.einsum(
        "anc,cf->fan",
        air,
        projector,
        preferred_element_type=jnp.float32,
    ).astype(jnp.bfloat16)
    return lax.all_gather(flux_local, "band", axis=1, tiled=True)


def shards(
    air_field_lattice,
    associated_polynomial_matrix,
    harmonic_damping_factor,
    boundary_exchange_projector,
    warmth_response_factor,
    water_patch_fields,
    kernel_coefficients,
    local_exchange_matrix,
    patch_average_matrix,
    water_kernel_offset,
    water_readout_matrix,
    patch_holder_index,
    water_point_indicator,
    water_point_totals,
):
    parallel_lines, meridian_number, channel_count = air_field_lattice.shape
    sec_count = lax.axis_size("sec")
    band_count = lax.axis_size("band")
    core_count = lax.axis_size("ch")
    device_count = sec_count * band_count * core_count
    total_cols = 2 * K
    per_device = total_cols // device_count
    slot_count = water_patch_fields.shape[0]
    mode_count = associated_polynomial_matrix.shape[0]
    lat_count = associated_polynomial_matrix.shape[1]
    wide = channel_count - SLIM
    in_kernels = (
        per_device == 2 * GROUP
        and wide > SLIM
        and wide % SLIM == 0
        and parallel_lines == 2
        and sec_count & (sec_count - 1) == 0
        and lat_count == device_count * parallel_lines
    )
    if in_kernels:
        plane = band_count * core_count
        sec_id = lax.axis_index("sec")
        sec = sec_id.reshape(1).astype(jnp.int32)
        forward, backward = map(jnp.asarray, transform_tables(meridian_number, device_count))
        hops = [[(i, i ^ o) for i in range(sec_count)] for o in range(sec_count)]

        twists = [[(i, i ^ p) for i in range(plane)] for p in range(plane)]
        place = (lax.axis_index("band") * core_count + lax.axis_index("ch")).astype(jnp.int32)

        def over_sections(blocks):
            return [lax.ppermute(x, "sec", hops[o]) if o else x for o, x in enumerate(blocks)]

        def over_plane(blocks):
            moved = {p: lax.ppermute(blocks[p], ("band", "ch"), twists[p]) for p in range(plane - 1, 0, -1)}
            return [moved.get(p, x) for p, x in enumerate(blocks)]

        slim = analyse_slim(air_field_lattice, forward, wide, sec, sec_count, device_count)
        air_after, *slim = lax.optimization_barrier((air_field_lattice, *slim))
        slim = over_sections(slim)
        wide_coeffs = analyse_wide(air_after, forward, wide, device_count)
        wide_coeffs = lax.all_to_all(wide_coeffs, AXES, split_axis=0, concat_axis=0, tiled=True)
        slim = to_plane(slim, place.reshape(1))
        matrix_after, *slim = lax.optimization_barrier((associated_polynomial_matrix, *slim))
        slim = over_plane(slim)

        at_lat = jnp.arange(lat_count, dtype=jnp.int32)
        sections_at = at_lat // parallel_lines % sec_count ^ sec_id
        places_at = at_lat // (parallel_lines * sec_count) ^ place
        order = (sections_at * plane + places_at) * parallel_lines + at_lat % parallel_lines
        shuffle = (at_lat[:, None] == order[None, :]).astype(jnp.bfloat16)
        shuffled = jnp.einsum(
            "mlt,tu->mlu", matrix_after, shuffle, preferred_element_type=jnp.float32
        ).astype(jnp.bfloat16)

        position = jnp.stack([sec_id, place]).astype(jnp.int32)
        joined, *slim = latitudinal_slim(slim, shuffled, harmonic_damping_factor, wide, position)
        slim = from_plane(over_plane(slim), place.reshape(1))
        wide_coeffs, *slim = lax.optimization_barrier((wide_coeffs, *slim))
        slim = over_sections(slim)
        wide_coeffs = latitudinal_wide(
            wide_coeffs, joined, associated_polynomial_matrix, harmonic_damping_factor
        )
        wide_coeffs = lax.all_to_all(wide_coeffs, AXES, split_axis=0, concat_axis=0, tiled=True)
        (air_after, water_patch_fields, warmth_response_factor, patch_holder_index, *slim) = lax.optimization_barrier(
            (air_field_lattice, water_patch_fields, warmth_response_factor, patch_holder_index, *slim)
        )
        gathered = gather_flux(air_after, boundary_exchange_projector)
    else:
        gathered = gather_flux(air_field_lattice, boundary_exchange_projector)
        table = dft_table(meridian_number)
        forward = jnp.asarray(np.ascontiguousarray(table.T))
        backward = jnp.asarray((table.astype(np.float32) * (2.0 / meridian_number)).astype(jnp.bfloat16))
        fourier = jnp.einsum(
            "qn,anc->aqc", forward, air_field_lattice, preferred_element_type=jnp.float32
        ).astype(jnp.bfloat16)
        collected = lax.all_to_all(fourier, AXES, split_axis=1, concat_axis=0, tiled=True)
        pairs = collected.reshape(lat_count, mode_count, 2, channel_count)
        spectrum = jnp.einsum(
            "mlt,tmpc->mlpc", associated_polynomial_matrix, pairs, preferred_element_type=jnp.float32
        )
        scaled = (spectrum * harmonic_damping_factor[None, :, None]).astype(jnp.bfloat16)
        damped = jnp.einsum(
            "mlt,mlpc->tmpc", associated_polynomial_matrix, scaled, preferred_element_type=jnp.float32
        ).astype(jnp.bfloat16).reshape(lat_count, per_device, channel_count)
        returned = lax.all_to_all(damped, AXES, split_axis=0, concat_axis=1, tiled=True)

    sec_id = lax.axis_index("sec")
    band_id = lax.axis_index("band")
    core_id = lax.axis_index("ch")
    owner_grid = patch_holder_index.reshape(sec_count, band_count, core_count, -1)
    tiles_per_row = owner_grid.shape[3]
    owner_group = lax.dynamic_index_in_dim(owner_grid, sec_id, 0, keepdims=False)
    owner_group = lax.dynamic_index_in_dim(owner_group, core_id, 1, keepdims=False)
    owner_flat = owner_group.reshape(-1)
    holders = jnp.arange(band_count, dtype=jnp.int32)
    mine_all = owner_flat[None, :] == holders[:, None]
    rank_all = jnp.cumsum(mine_all.astype(jnp.int32), axis=1) - 1
    slot_index = jnp.arange(slot_count, dtype=jnp.int32)
    pick_all = mine_all[:, None, :] & (rank_all[:, None, :] == slot_index[None, :, None])
    my_pick = lax.dynamic_index_in_dim(pick_all, band_id, 0, keepdims=False)
    flux_count = gathered.shape[0]
    tile_width = meridian_number // tiles_per_row
    pieces = gathered.reshape(flux_count, band_count, parallel_lines, tiles_per_row, tile_width)
    chooser = my_pick.reshape(slot_count, band_count, tiles_per_row).astype(jnp.bfloat16)
    tile_flux = jnp.einsum(
        "sbj,fbrjw->sfrw", chooser, pieces, preferred_element_type=jnp.float32
    ).astype(jnp.bfloat16)
    ocean_next = ocean_update(
        water_patch_fields,
        tile_flux,
        water_point_indicator,
        water_point_totals,
        kernel_coefficients,
        local_exchange_matrix,
        patch_average_matrix,
        water_kernel_offset,
        water_readout_matrix,
    )
    sea_slots = ocean_next[:, 0]
    sea_all = lax.all_gather(sea_slots, "band", axis=0, tiled=True)
    rank_tile = jnp.sum(jnp.where(mine_all, rank_all, 0), axis=0)
    my_owners = lax.dynamic_index_in_dim(owner_group, band_id, 0, keepdims=False)
    my_ranks = lax.dynamic_slice_in_dim(rank_tile, band_id * tiles_per_row, tiles_per_row)
    target = my_owners * slot_count + my_ranks
    selector = (
        target[:, None] == jnp.arange(band_count * slot_count, dtype=jnp.int32)[None, :]
    ).astype(jnp.bfloat16)
    water_patches = jnp.einsum(
        "jk,krw->rjw", selector, sea_all, preferred_element_type=jnp.float32
    ).astype(jnp.bfloat16)
    water_skin_warmth = water_patches.reshape(parallel_lines, meridian_number)
    if in_kernels:
        halves = (parallel_lines, 2, meridian_number // 2, -1)
        air = air_field_lattice.reshape(halves)
        sea = water_skin_warmth.reshape(parallel_lines, 2, 1, meridian_number // 2)
        sea = jnp.broadcast_to(sea, (parallel_lines, 2, GROUP, meridian_number // 2))
        warmth = three_parts(warmth_response_factor)
        begun = synthesise_slim(slim, backward, air, sea, warmth, wide, sec)
        advanced = synthesise_wide(wide_coeffs, backward, air, sea, warmth, begun)
        advanced = advanced.reshape(air_field_lattice.shape)
    else:
        rebuilt = jnp.einsum("nq,aqc->anc", backward, returned, preferred_element_type=jnp.float32)
        advanced = (
            air_field_lattice.astype(jnp.float32)
            + rebuilt
            + water_skin_warmth.astype(jnp.float32)[:, :, None] * warmth_response_factor[None, None]
        ).astype(jnp.bfloat16)
    return (advanced, ocean_next)


def solution(mesh):
    placed = (
        P(("sec", "band", "ch"), None, None),
        P(("sec", "band", "ch"), None, None),
        P(),
        P(),
        P(),
        P(("sec", "band", "ch"), None, None, None),
        P(),
        P(),
        P(),
        P(),
        P(),
        P(),
        P(("sec", "band", "ch"), None, None),
        P(("sec", "band", "ch")),
    )
    return jax.shard_map(
        shards,
        mesh=mesh,
        in_specs=placed,
        out_specs=(
            P(("sec", "band", "ch"), None, None),
            P(("sec", "band", "ch"), None, None, None),
        ),
        check_vma=False,
    )
```

```python
import functools
import math

import jax
import jax.numpy as jnp
import numpy as np
from jax import lax
from jax.experimental import pallas as pl
from jax.experimental.pallas import tpu as pltpu
from jax.sharding import PartitionSpec as P

K = 512
AXES = ("sec", "band", "ch")
GROUP = 16
SLIM = 128
MIB = 1024 * 1024


@functools.lru_cache(maxsize=None)
def dft_table(meridian_number):
    cell_index = np.arange(meridian_number, dtype=np.int64)[:, None]
    column = np.arange(2 * K, dtype=np.int64)[None, :]
    phase_angle = (cell_index * (column // 2) % meridian_number) * (2.0 * math.pi / meridian_number)
    table = np.where(column % 2 == 0, np.cos(phase_angle), -np.sin(phase_angle))
    return table.astype(np.float32).astype(jnp.bfloat16)


@functools.lru_cache(maxsize=None)
def transform_tables(meridian_number, groups):
    half = meridian_number // 2
    table = dft_table(meridian_number).astype(np.float32)
    by_parity = table.reshape(meridian_number, groups, -1, 2, 2).transpose(1, 3, 2, 4, 0)
    forward = by_parity.reshape(-1, meridian_number)
    backward = by_parity.transpose(1, 4, 0, 2, 3)[:, :half].reshape(2, half, -1) * (2.0 / meridian_number)
    return tuple(np.ascontiguousarray(x).astype(jnp.bfloat16) for x in (forward, backward))


def ocean_update(
    state,
    tile_flux,
    mask_tile,
    count_tile,
    kernel_coefficients,
    local_exchange_matrix,
    patch_average_matrix,
    water_kernel_offset,
    water_readout_matrix,
):
    parallel_lines = mask_tile.shape[1]
    tile_width = mask_tile.shape[2]
    mask_f = mask_tile.astype(jnp.float32)
    masked = tile_flux * mask_tile[:, None].astype(jnp.bfloat16)
    fmean = (
        jnp.sum(masked.astype(jnp.float32), axis=(2, 3))
        / jnp.maximum(count_tile.astype(jnp.float32), 1.0)[:, None]
    )
    total = jnp.einsum(
        "fo,sfrw->sorw", local_exchange_matrix, masked, preferred_element_type=jnp.float32
    )
    for shift_row in range(3):
        for shift_col in range(3):
            window = state[
                :, :, shift_row : shift_row + parallel_lines, shift_col : shift_col + tile_width
            ]
            total = total + jnp.einsum(
                "io,sirw->sorw",
                kernel_coefficients[shift_row, shift_col],
                window,
                preferred_element_type=jnp.float32,
            )
    mean_term = jnp.sum(fmean[:, :, None] * patch_average_matrix[None], axis=1)
    total = total + mean_term[:, :, None, None] + water_kernel_offset[None, :, None, None]
    hidden = jax.nn.gelu(total, approximate=True).astype(jnp.bfloat16)
    update = jnp.einsum(
        "io,sirw->sorw", water_readout_matrix, hidden, preferred_element_type=jnp.float32
    )
    fresh = (
        state[:, :, 1 : 1 + parallel_lines, 1 : 1 + tile_width].astype(jnp.float32) + update
    ) * mask_f[:, None]
    return fresh.astype(jnp.bfloat16)


def compiler_params(mib=60):
    return pltpu.CompilerParams(vmem_limit_bytes=mib * MIB)


def cost(flops, *arrays):
    return pl.CostEstimate(
        flops=flops, bytes_accessed=sum(x.size * x.dtype.itemsize for x in arrays), transcendentals=0
    )


def lane_spans(width, size=256):
    return [slice(at, min(at + size, width)) for at in range(0, width, size)]


def analyse_wide(air, table, width, groups):
    lines, cells, _ = air.shape
    rows = table.shape[0] // groups
    places = [(0, 0, width - SLIM), (1, width - SLIM, width)]
    out = jax.ShapeDtypeStruct((groups, rows, 2 * width - SLIM), jnp.bfloat16)

    def body(table_ref, air_ref, out_ref):
        for line, at, size in places:
            for span in lane_spans(size):
                coeffs = jnp.dot(table_ref[...], air_ref[line, :, span], preferred_element_type=jnp.float32)
                out_ref[:, :, at + span.start : at + span.stop] = coeffs.astype(jnp.bfloat16).reshape(
                    groups, rows, -1
                )

    return pl.pallas_call(
        body,
        grid=(1,),
        in_specs=[
            pl.BlockSpec(table.shape, lambda i: (0, 0)),
            pl.BlockSpec((lines, cells, width), lambda i: (0, 0, 0)),
        ],
        out_specs=pl.BlockSpec(out.shape, lambda i: (0, 0, 0)),
        out_shape=out,
        compiler_params=compiler_params(),
        cost_estimate=cost(2 * lines * table.size * width, table, air, out),
        name="analyse_wide",
    )(table, air)


def analyse_slim(air, table, start, sec, sections, groups):
    lines, cells, channels = air.shape
    width = channels - start
    plane = groups // sections
    rows = table.shape[0] // groups
    size = plane * rows
    pieces = lines + 1
    out = jax.ShapeDtypeStruct((pieces, plane, rows, width), jnp.bfloat16)

    def body(sec_ref, table_ref, air_ref, before_ref, *outs):
        joined = jnp.concatenate([air_ref[a] for a in range(lines)] + [before_ref[0]], axis=1)
        for o, out_ref in enumerate(outs):
            part = pl.ds(pl.multiple_of((sec_ref[0] ^ o) * size, size), size)
            coeffs = jnp.dot(table_ref[part, :], joined, preferred_element_type=jnp.float32).astype(jnp.bfloat16)
            for a in range(pieces):
                out_ref[a] = coeffs[:, a * width : (a + 1) * width].reshape(plane, rows, width)

    return pl.pallas_call(
        body,
        grid=(1,),
        in_specs=[
            pl.BlockSpec(memory_space=pltpu.SMEM),
            pl.BlockSpec(table.shape, lambda i: (0, 0)),
            pl.BlockSpec((lines, cells, width), lambda i: (0, 0, start // width)),
            pl.BlockSpec((1, cells, width), lambda i: (0, 0, start // width - 1)),
        ],
        out_specs=[pl.BlockSpec(out.shape, lambda i: (0, 0, 0, 0))] * sections,
        out_shape=[out] * sections,
        compiler_params=compiler_params(),
        cost_estimate=cost(2 * pieces * table.size * width, table, *[out] * 2 * sections),
        name="analyse_slim",
    )(sec, table, air, air)


def wavenumber_at(row):
    return row % GROUP // 2 * 2 + row // GROUP


def damp(transform, coeffs, damping):
    spectrum = jnp.dot(transform, coeffs, preferred_element_type=jnp.float32)
    scaled = (spectrum * damping).astype(jnp.bfloat16)
    back = lax.dot_general(transform, scaled, (((0,), (0,)), ((), ())), preferred_element_type=jnp.float32)
    return back.astype(jnp.bfloat16)


def latitudinal_wide(coeffs, joined, matrix, damping):
    devices, rows, _ = coeffs.shape
    modes, degrees, lats = matrix.shape
    lines = lats // devices
    width = (coeffs.shape[-1] + SLIM) // 2
    both = width - SLIM

    def body(x_ref, joined_ref, matrix_ref, damping_ref, out_ref):
        parity = pl.program_id(0)
        for span in lane_spans(both) + [slice(both, width)]:
            first = x_ref[:, :, span] if span.start < both else joined_ref[...]
            second = x_ref[:, :, both + span.start : both + span.stop]
            by_coeff = jnp.swapaxes(jnp.stack([first, second], axis=1).reshape(lats, GROUP, -1), 0, 1)
            results = [
                damp(matrix_ref[wavenumber_at(row) + parity], by_coeff[row], damping_ref[:, span])
                for row in range(GROUP)
            ]
            out_ref[:, :, :, span] = jnp.swapaxes(jnp.stack(results), 0, 1).reshape(devices, lines, GROUP, -1)

    return pl.pallas_call(
        body,
        grid=(rows // GROUP,),
        in_specs=[
            pl.BlockSpec((devices, GROUP, coeffs.shape[-1]), lambda p: (0, p, 0)),
            pl.BlockSpec((devices, GROUP, SLIM), lambda p: (0, p, 0)),
            whole(matrix),
            pl.BlockSpec((degrees, width), lambda p: (0, 0)),
        ],
        out_specs=pl.BlockSpec((devices, lines, GROUP, width), lambda p: (0, 0, p, 0)),
        out_shape=jax.ShapeDtypeStruct((devices, lines, rows, width), jnp.bfloat16),
        compiler_params=compiler_params(),
        cost_estimate=cost(4 * rows * degrees * lats * width, coeffs, coeffs, matrix),
        name="latitudinal_wide",
    )(coeffs, joined, matrix, damping)


def whole(x):
    return pl.BlockSpec(x.shape, lambda *_: (0,) * len(x.shape))


def to_plane(parts, place):
    lines, plane, rows, width = parts[0].shape
    sections = len(parts)
    out = jax.ShapeDtypeStruct((sections, lines, rows, width), jnp.bfloat16)

    def body(place_ref, *refs):
        for p, out_ref in enumerate(refs[sections:]):
            for o in range(sections):
                for a in range(lines):
                    out_ref[o, a] = refs[sections - 1 - o][a, place_ref[0] ^ p]

    return pl.pallas_call(
        body,
        grid=(1,),
        in_specs=[pl.BlockSpec(memory_space=pltpu.SMEM)] + [whole(parts[0])] * sections,
        out_specs=[whole(out)] * plane,
        out_shape=[out] * plane,
        compiler_params=compiler_params(63),
        cost_estimate=cost(0, *parts, *parts),
        name="to_plane",
    )(place, *parts[::-1])


def from_plane(parts, place):
    sections, lines, rows, width = parts[0].shape
    plane = len(parts)
    out = jax.ShapeDtypeStruct((lines, plane, rows, width), jnp.bfloat16)

    def body(place_ref, *refs):
        for o, out_ref in enumerate(refs[plane:]):
            for p in range(plane):
                for a in range(lines):
                    out_ref[a, place_ref[0] ^ p] = refs[p][o, a]

    return pl.pallas_call(
        body,
        grid=(1,),
        in_specs=[pl.BlockSpec(memory_space=pltpu.SMEM)] + [whole(parts[0])] * plane,
        out_specs=[whole(out)] * sections,
        out_shape=[out] * sections,
        compiler_params=compiler_params(63),
        cost_estimate=cost(0, *parts, *parts),
        name="from_plane",
    )(place, *parts)


def latitudinal_slim(parts, matrix, damping, start, position):
    sections, pieces, rows, width = parts[0].shape
    lines = pieces - 1
    plane = len(parts)
    degrees = damping.shape[0]
    own = sections * lines
    out = jax.ShapeDtypeStruct((sections, lines, rows, width), jnp.bfloat16)
    joined = jax.ShapeDtypeStruct((sections * plane, rows, width), jnp.bfloat16)

    def body(position_ref, matrix_ref, damping_ref, *refs):
        part_refs, joined_ref, out_refs = refs[:plane], refs[plane], refs[plane + 1 :]
        latitudes = jnp.concatenate([ref[:, :lines].reshape(own, rows, width) for ref in part_refs], axis=0)
        by_coeff = jnp.swapaxes(latitudes, 0, 1)
        results = [
            damp(matrix_ref[wavenumber_at(row)], by_coeff[row], damping_ref[...]) for row in range(rows)
        ]
        by_lat = jnp.swapaxes(jnp.stack(results), 0, 1)
        for p, out_ref in enumerate(out_refs):
            out_ref[...] = by_lat[p * own : (p + 1) * own].reshape(out_ref.shape)
            for o in range(sections):
                device = (position_ref[0] ^ o) * plane + (position_ref[1] ^ p)
                joined_ref[device] = part_refs[p][o, lines]

    return pl.pallas_call(
        body,
        grid=(1,),
        in_specs=[
            pl.BlockSpec(memory_space=pltpu.SMEM),
            whole(matrix),
            pl.BlockSpec((degrees, width), lambda i: (0, start // width)),
        ]
        + [whole(parts[0])] * plane,
        out_specs=[whole(joined)] + [whole(out)] * plane,
        out_shape=[joined] + [out] * plane,
        compiler_params=compiler_params(63),
        cost_estimate=pl.CostEstimate(flops=10**11, bytes_accessed=3 * 10**8, transcendentals=0),
        name="latitudinal_slim",
    )(position, matrix, damping, *parts)


def advance(air, rebuilt, sea, warmth):
    warmed = lax.dot_general(sea, warmth, (((0,), (0,)), ((), ())), preferred_element_type=jnp.float32)
    return (air.astype(jnp.float32) + rebuilt + warmed).astype(jnp.bfloat16)


def three_parts(values):
    parts, rest = [], values
    for _ in range(3):
        parts.append(lax.reduce_precision(rest, 8, 7))
        rest = rest - parts[-1]
    parts += [jnp.zeros_like(values)] * (GROUP - 3)
    return jnp.stack(parts).astype(jnp.bfloat16)


def synthesise_slim(parts, table, air, sea, warmth, start, sec):
    lines, plane, rows, width = parts[0].shape
    sections = len(parts)
    half = air.shape[2]

    def body(sec_ref, table_ref, air_ref, sea_ref, warmth_ref, *refs):
        part_refs, out_ref, gathered = refs[:sections], refs[-2], refs[-1]
        for o, part_ref in enumerate(part_refs[::-1]):
            for a in range(lines):
                for odd in range(2):
                    gathered[odd, sec_ref[0] ^ o, :, :, a * width : (a + 1) * width] = part_ref[
                        a, :, odd * GROUP : (odd + 1) * GROUP, :
                    ]
        even, odd = (
            jnp.dot(
                table_ref[odd],
                gathered[odd].reshape(sections * plane * GROUP, lines * width),
                preferred_element_type=jnp.float32,
            )
            for odd in range(2)
        )
        for at, rebuilt in enumerate((even + odd, even - odd)):
            for a in range(lines):
                out_ref[a, at] = advance(
                    air_ref[a, at], rebuilt[:, a * width : (a + 1) * width], sea_ref[a, at], warmth_ref[...]
                )

    return pl.pallas_call(
        body,
        grid=(1,),
        in_specs=[
            pl.BlockSpec(memory_space=pltpu.SMEM),
            pl.BlockSpec(table.shape, lambda i: (0, 0, 0)),
            pl.BlockSpec((lines, 2, half, width), lambda i: (0, 0, 0, start // width)),
            whole(sea),
            pl.BlockSpec((GROUP, width), lambda i: (0, start // width)),
        ]
        + [pl.BlockSpec(parts[0].shape, lambda i: (0, 0, 0, 0))] * sections,
        out_specs=pl.BlockSpec((lines, 2, half, width), lambda i: (0, 0, 0, start // width)),
        out_shape=jax.ShapeDtypeStruct(air.shape, jnp.bfloat16),
        scratch_shapes=[pltpu.VMEM((2, sections, plane, GROUP, lines * width), jnp.bfloat16)],
        compiler_params=compiler_params(),
        cost_estimate=pl.CostEstimate(flops=10**11, bytes_accessed=3 * 10**8, transcendentals=0),
        name="synthesise_slim",
    )(sec, table, air, sea, warmth, *parts[::-1])


def synthesise_wide(coeffs, table, air, sea, warmth, begun):
    groups, lines, rows, width = coeffs.shape
    half = air.shape[2]

    def body(table_ref, coeff_ref, air_ref, sea_ref, warmth_ref, begun_ref, out_ref):
        for span in lane_spans(width):
            even, odd = (
                jnp.dot(
                    table_ref[odd],
                    coeff_ref[:, 0, odd * GROUP : (odd + 1) * GROUP, span].reshape(groups * GROUP, -1),
                    preferred_element_type=jnp.float32,
                )
                for odd in range(2)
            )
            for at, rebuilt in enumerate((even + odd, even - odd)):
                out_ref[0, at, :, span] = advance(
                    air_ref[0, at, :, span], rebuilt, sea_ref[0, at], warmth_ref[:, span]
                )

    return pl.pallas_call(
        body,
        grid=(lines,),
        in_specs=[
            pl.BlockSpec(table.shape, lambda a: (0, 0, 0)),
            pl.BlockSpec((groups, 1, rows, width), lambda a: (0, a, 0, 0)),
            pl.BlockSpec((1, 2, half, width), lambda a: (a, 0, 0, 0)),
            pl.BlockSpec((1, 2, GROUP, half), lambda a: (a, 0, 0, 0)),
            pl.BlockSpec((GROUP, width), lambda a: (0, 0)),
            pl.BlockSpec(memory_space=pl.ANY),
        ],
        out_specs=pl.BlockSpec((1, 2, half, width), lambda a: (a, 0, 0, 0)),
        out_shape=jax.ShapeDtypeStruct(air.shape, jnp.bfloat16),
        input_output_aliases={5: 0},
        compiler_params=compiler_params(),
        cost_estimate=cost(4 * lines * half * half * width, table, coeffs, coeffs, coeffs),
        name="synthesise_wide",
    )(table, coeffs, air, sea, warmth, begun)


def gather_flux(air, projector):
    flux_local = jnp.einsum(
        "anc,cf->fan",
        air,
        projector,
        preferred_element_type=jnp.float32,
    ).astype(jnp.bfloat16)
    return lax.all_gather(flux_local, "band", axis=1, tiled=True)


def shards(
    air_field_lattice,
    associated_polynomial_matrix,
    harmonic_damping_factor,
    boundary_exchange_projector,
    warmth_response_factor,
    water_patch_fields,
    kernel_coefficients,
    local_exchange_matrix,
    patch_average_matrix,
    water_kernel_offset,
    water_readout_matrix,
    patch_holder_index,
    water_point_indicator,
    water_point_totals,
):
    parallel_lines, meridian_number, channel_count = air_field_lattice.shape
    sec_count = lax.axis_size("sec")
    band_count = lax.axis_size("band")
    core_count = lax.axis_size("ch")
    device_count = sec_count * band_count * core_count
    total_cols = 2 * K
    per_device = total_cols // device_count
    slot_count = water_patch_fields.shape[0]
    mode_count = associated_polynomial_matrix.shape[0]
    lat_count = associated_polynomial_matrix.shape[1]
    wide = channel_count - SLIM
    in_kernels = (
        per_device == 2 * GROUP
        and wide > SLIM
        and wide % SLIM == 0
        and parallel_lines == 2
        and sec_count & (sec_count - 1) == 0
        and lat_count == device_count * parallel_lines
    )
    if in_kernels:
        plane = band_count * core_count
        sec_id = lax.axis_index("sec")
        sec = sec_id.reshape(1).astype(jnp.int32)
        forward, backward = map(jnp.asarray, transform_tables(meridian_number, device_count))
        hops = [[(i, i ^ o) for i in range(sec_count)] for o in range(sec_count)]

        twists = [[(i, i ^ p) for i in range(plane)] for p in range(plane)]
        place = (lax.axis_index("band") * core_count + lax.axis_index("ch")).astype(jnp.int32)

        def over_sections(blocks):
            return [lax.ppermute(x, "sec", hops[o]) if o else x for o, x in enumerate(blocks)]

        def over_plane(blocks):
            moved = {p: lax.ppermute(blocks[p], ("band", "ch"), twists[p]) for p in range(plane - 1, 0, -1)}
            return [moved.get(p, x) for p, x in enumerate(blocks)]

        slim = analyse_slim(air_field_lattice, forward, wide, sec, sec_count, device_count)
        air_after, *slim = lax.optimization_barrier((air_field_lattice, *slim))
        slim = over_sections(slim)
        wide_coeffs = analyse_wide(air_after, forward, wide, device_count)
        wide_coeffs = lax.all_to_all(wide_coeffs, AXES, split_axis=0, concat_axis=0, tiled=True)
        slim = to_plane(slim, place.reshape(1))
        matrix_after, *slim = lax.optimization_barrier((associated_polynomial_matrix, *slim))
        slim = over_plane(slim)

        at_lat = jnp.arange(lat_count, dtype=jnp.int32)
        sections_at = at_lat // parallel_lines % sec_count ^ sec_id
        places_at = at_lat // (parallel_lines * sec_count) ^ place
        order = (sections_at * plane + places_at) * parallel_lines + at_lat % parallel_lines
        shuffle = (at_lat[:, None] == order[None, :]).astype(jnp.bfloat16)
        shuffled = jnp.einsum(
            "mlt,tu->mlu", matrix_after, shuffle, preferred_element_type=jnp.float32
        ).astype(jnp.bfloat16)

        position = jnp.stack([sec_id, place]).astype(jnp.int32)
        joined, *slim = latitudinal_slim(slim, shuffled, harmonic_damping_factor, wide, position)
        slim = from_plane(over_plane(slim), place.reshape(1))
        wide_coeffs, *slim = lax.optimization_barrier((wide_coeffs, *slim))
        slim = over_sections(slim)
        wide_coeffs = latitudinal_wide(
            wide_coeffs, joined, associated_polynomial_matrix, harmonic_damping_factor
        )
        wide_coeffs = lax.all_to_all(wide_coeffs, AXES, split_axis=0, concat_axis=0, tiled=True)
        (air_after, water_patch_fields, warmth_response_factor, patch_holder_index, *slim) = lax.optimization_barrier(
            (air_field_lattice, water_patch_fields, warmth_response_factor, patch_holder_index, *slim)
        )
        gathered = gather_flux(air_after, boundary_exchange_projector)
    else:
        gathered = gather_flux(air_field_lattice, boundary_exchange_projector)
        table = dft_table(meridian_number)
        forward = jnp.asarray(np.ascontiguousarray(table.T))
        backward = jnp.asarray((table.astype(np.float32) * (2.0 / meridian_number)).astype(jnp.bfloat16))
        fourier = jnp.einsum(
            "qn,anc->aqc", forward, air_field_lattice, preferred_element_type=jnp.float32
        ).astype(jnp.bfloat16)
        collected = lax.all_to_all(fourier, AXES, split_axis=1, concat_axis=0, tiled=True)
        pairs = collected.reshape(lat_count, mode_count, 2, channel_count)
        spectrum = jnp.einsum(
            "mlt,tmpc->mlpc", associated_polynomial_matrix, pairs, preferred_element_type=jnp.float32
        )
        scaled = (spectrum * harmonic_damping_factor[None, :, None]).astype(jnp.bfloat16)
        damped = jnp.einsum(
            "mlt,mlpc->tmpc", associated_polynomial_matrix, scaled, preferred_element_type=jnp.float32
        ).astype(jnp.bfloat16).reshape(lat_count, per_device, channel_count)
        returned = lax.all_to_all(damped, AXES, split_axis=0, concat_axis=1, tiled=True)

    sec_id = lax.axis_index("sec")
    band_id = lax.axis_index("band")
    core_id = lax.axis_index("ch")
    owner_grid = patch_holder_index.reshape(sec_count, band_count, core_count, -1)
    tiles_per_row = owner_grid.shape[3]
    owner_group = lax.dynamic_index_in_dim(owner_grid, sec_id, 0, keepdims=False)
    owner_group = lax.dynamic_index_in_dim(owner_group, core_id, 1, keepdims=False)
    owner_flat = owner_group.reshape(-1)
    holders = jnp.arange(band_count, dtype=jnp.int32)
    mine_all = owner_flat[None, :] == holders[:, None]
    rank_all = jnp.cumsum(mine_all.astype(jnp.int32), axis=1) - 1
    slot_index = jnp.arange(slot_count, dtype=jnp.int32)
    pick_all = mine_all[:, None, :] & (rank_all[:, None, :] == slot_index[None, :, None])
    my_pick = lax.dynamic_index_in_dim(pick_all, band_id, 0, keepdims=False)
    flux_count = gathered.shape[0]
    tile_width = meridian_number // tiles_per_row
    pieces = gathered.reshape(flux_count, band_count, parallel_lines, tiles_per_row, tile_width)
    chooser = my_pick.reshape(slot_count, band_count, tiles_per_row).astype(jnp.bfloat16)
    tile_flux = jnp.einsum(
        "sbj,fbrjw->sfrw", chooser, pieces, preferred_element_type=jnp.float32
    ).astype(jnp.bfloat16)
    ocean_next = ocean_update(
        water_patch_fields,
        tile_flux,
        water_point_indicator,
        water_point_totals,
        kernel_coefficients,
        local_exchange_matrix,
        patch_average_matrix,
        water_kernel_offset,
        water_readout_matrix,
    )
    sea_slots = ocean_next[:, 0]
    sea_all = lax.all_gather(sea_slots, "band", axis=0, tiled=True)
    rank_tile = jnp.sum(jnp.where(mine_all, rank_all, 0), axis=0)
    my_owners = lax.dynamic_index_in_dim(owner_group, band_id, 0, keepdims=False)
    my_ranks = lax.dynamic_slice_in_dim(rank_tile, band_id * tiles_per_row, tiles_per_row)
    target = my_owners * slot_count + my_ranks
    selector = (
        target[:, None] == jnp.arange(band_count * slot_count, dtype=jnp.int32)[None, :]
    ).astype(jnp.bfloat16)
    water_patches = jnp.einsum(
        "jk,krw->rjw", selector, sea_all, preferred_element_type=jnp.float32
    ).astype(jnp.bfloat16)
    water_skin_warmth = water_patches.reshape(parallel_lines, meridian_number)
    if in_kernels:
        halves = (parallel_lines, 2, meridian_number // 2, -1)
        air = air_field_lattice.reshape(halves)
        sea = water_skin_warmth.reshape(parallel_lines, 2, 1, meridian_number // 2)
        sea = jnp.broadcast_to(sea, (parallel_lines, 2, GROUP, meridian_number // 2))
        warmth = three_parts(warmth_response_factor)
        begun = synthesise_slim(slim, backward, air, sea, warmth, wide, sec)
        advanced = synthesise_wide(wide_coeffs, backward, air, sea, warmth, begun)
        advanced = advanced.reshape(air_field_lattice.shape)
    else:
        rebuilt = jnp.einsum("nq,aqc->anc", backward, returned, preferred_element_type=jnp.float32)
        advanced = (
            air_field_lattice.astype(jnp.float32)
            + rebuilt
            + water_skin_warmth.astype(jnp.float32)[:, :, None] * warmth_response_factor[None, None]
        ).astype(jnp.bfloat16)
    return (advanced, ocean_next)


def solution(mesh):
    placed = (
        P(("sec", "band", "ch"), None, None),
        P(("sec", "band", "ch"), None, None),
        P(),
        P(),
        P(),
        P(("sec", "band", "ch"), None, None, None),
        P(),
        P(),
        P(),
        P(),
        P(),
        P(),
        P(("sec", "band", "ch"), None, None),
        P(("sec", "band", "ch")),
    )
    return jax.shard_map(
        shards,
        mesh=mesh,
        in_specs=placed,
        out_specs=(
            P(("sec", "band", "ch"), None, None),
            P(("sec", "band", "ch"), None, None, None),
        ),
        check_vma=False,
    )
```
